32 devices in a mesh: sec: 2 (over x), grp: 4 (over y, core), rank: 4 (over z).
Axes of the slice: x: 2, y: 2, z: 4, core: 2. Of those that a mesh axis runs over, the one named last changes fastest.
Arguments:
- queries: bfloat16 [8, 128, 8192], P(('sec', 'grp')), may hold values from -6 to 14
- kv_cache: bfloat16 [8, 4096, 2048], P(('sec', 'grp'), 'rank'), may hold values from -6 to 10
- key_scale: float32 [1024], replicated, may hold values from 0.5 to 2
- fresh_input: bfloat16 [8, 128, 8192], P(('sec', 'grp'), None, 'rank'), may hold values from -6 to 6
- kv_weight: bfloat16 [8192, 2048], P('rank'), may hold values from -0.0625 to 0.0625
- lengths: int32 [8, 1], P(('sec', 'grp')), may hold values from 1 to 4096
- page_list: int32 [512], P(('sec', 'grp', 'rank')), may hold values from 0 to 63, as said below
- owners: int32 [512, 1], P(('sec', 'grp', 'rank')), may hold values from 0 to 3; in each aligned block of 16 rows (0 to 15, 16 to 31, ...) at most 8 rows name the same one
Outputs:
- attended: bfloat16 [8, 128, 8192], P(('sec', 'grp'), None, 'rank')
- handed: bfloat16 [32, 32, 16, 2048], P(('sec', 'grp', 'rank'))
The draws below stay inside these ranges and needn't reach their ends.
Inputs may be any that keep to these rules, and one draw needn't show every extreme that they name: `page_list`: the 16 entries of one device are distinct page numbers of its own cache. `owners`: among the 16 entries of one device at most 8 name the same owner, and some device has exactly 8 for one owner.
All inputs are finite; a program needn't handle non-finite values.
Results may differ from the reference program's by a relative error of at most 0.0045.
The reference program's roundings to bfloat16 on the way (of `fresh_kv`, `query_rot`, `cache_keys`, `fresh_keys` and `rounded`) count: a program that leaves them out, or rounds other values in their place, can miss the bound.
Values may be sent and summed in bfloat16 or wider, within the bound.
No kernel may reach another device: no remote copies, remote signals or barrier semaphores. Data moves between devices by JAX's collectives and lax.ppermute only.
A program may use at most 192 MiB of HBM per device.

```python
import math
import jax
import jax.numpy as jnp
import numpy as np
from jax import lax

D = 8192
HEADS = 64
KVH = 8
HD = 128
ROWS = 128
CTX = 1024
PAGE = 16
GQ = 8
KVW = 1024
QW = 8192
PAGES = 64
FIN = 16
CAP = 8
SEQ = 4096
GROUPS = 8
N_GRP = 4
N_RANK = 4


def draw_queries(key, part):
    key = jax.random.fold_in(key, 11)
    key_first = jax.random.fold_in(key, 0)
    base_values = jnp.clip(jax.random.normal(key_first, (GROUPS, ROWS, QW), jnp.float32), -6.0, 6.0)
    return base_values.astype(jnp.bfloat16)


def draw_kv_cache(key, part):
    key = jax.random.fold_in(key, 5)
    key_first = jax.random.fold_in(key, 0)
    base_values = jnp.clip(jax.random.normal(key_first, (GROUPS, SEQ, 2 * KVW), jnp.float32), -6.0, 6.0)
    return base_values.astype(jnp.bfloat16)


def draw_page_list(key, part):
    key = jax.random.fold_in(key, 7)
    device_keys = jax.random.split(key, GROUPS * N_RANK)
    chosen = jax.vmap(lambda device_key: jax.random.permutation(device_key, PAGES)[:FIN])(device_keys)
    return chosen.reshape(GROUPS * N_RANK * FIN).astype(jnp.int32)


def with_ends(array, stream_key, low, high):
    longest = array.shape.index(max(array.shape))
    spots = []
    for shift in (0, 1):
        where = [jax.random.randint(jax.random.fold_in(stream_key, axis), (), 0, length) for axis, length in enumerate(array.shape)]
        where[longest] = (where[longest] + shift) % array.shape[longest]
        spots.append(tuple(where))
    return array.at[spots[0]].set(low).at[spots[1]].set(high)


def block_scale(stream_key, extent, cuts, least, largest):
    def one(dim, parts):
        draws = jax.random.uniform(jax.random.fold_in(jax.random.fold_in(stream_key, 6), dim), (parts,), jnp.float32, least / len(cuts), largest / len(cuts))
        return jnp.repeat(jnp.exp(draws), extent[dim] // parts).reshape((-1,) + (1,) * (len(extent) - dim - 1))

    loudness = one(*cuts[0])
    for cut in cuts[1:]:
        loudness = loudness * one(*cut)
    return loudness


def assign_block(own_key, own, number, rows, count, top, bound, slope):
    sequence = jax.random.permutation(own_key, count)
    heavy_load, ordinary = load_shares(count, rows * top, bound, slope, True), load_shares(count, rows * top, bound, slope, False)
    places = jnp.arange(count)

    def named(sizes, rotation):
        used = int((sizes > 0).sum())
        fixed = max(1, used // 4)
        passed = fixed + (places - fixed + rotation * (used - fixed)) % max(1, count - fixed)
        return jnp.zeros((count,), jnp.int32).at[sequence[jnp.where(places < fixed, places, passed)]].set(jnp.asarray(sizes, jnp.int32))

    sizes = jnp.where(number % 4 == 0, named(heavy_load, number // 4), named(ordinary, number - number // 4 - 1))
    mixed = jax.random.permutation(jax.random.fold_in(own, 3), count)
    giver, taker = mixed[0:count // 2 * 2:2], mixed[1:count // 2 * 2:2]
    slack = jnp.minimum(sizes[giver] - 1, bound - sizes[taker]) // 2
    slack = jnp.where((giver == sequence[0]) | (taker == sequence[0]) | (sizes[taker] == 0), 0, jnp.maximum(slack, 0))
    passed = jax.random.randint(jax.random.fold_in(own, 4), (count // 2,), 0, 1 << 20) % (slack + 1)
    sizes = sizes.at[giver].add(-passed).at[taker].add(passed)
    labels = jnp.searchsorted(jnp.cumsum(sizes), jnp.arange(rows * top), side="right").astype(jnp.int32)
    grid = labels.reshape(top, rows).T
    grid = grid[jax.random.permutation(jax.random.fold_in(own, 1), rows)]
    rotation = jax.random.randint(jax.random.fold_in(own, 2), (rows, 1), 0, top)
    return jnp.take_along_axis(grid, (jnp.arange(top)[None, :] + rotation) % top, axis=1)


def load_shares(number_of, total, bound, slope, full):
    weights = [(1 << 20) // math.isqrt(grade ** slope) + 1 for grade in range(1, number_of + 1)]
    largest = bound if full else min(bound, max(-(-total // number_of), total * weights[0] // sum(weights)))
    least = 1 if total - largest >= number_of - 1 else 0
    given, rest = [largest] + [least] * (number_of - 1), total - largest - least * (number_of - 1)
    while rest > 0:
        movable = [i for i in range(1, number_of) if given[i] < largest] or [i for i in range(1, number_of) if given[i] < bound]
        mass, remaining = sum([weights[i] for i in movable]), rest
        for i in movable:
            more = min(bound - given[i], max(1, remaining * weights[i] // mass), rest)
            given[i] = given[i] + more
            rest = rest - more
    return np.array(given)


def normal_values(own_key, extent, scale, reach, cuts=(), kind=jnp.bfloat16):
    result = jax.random.normal(own_key, extent, jnp.float32) * scale
    if len(cuts) > 0:
        result = block_scale(own_key, extent, cuts, -0.22, 0.18) * result
    return jnp.clip(result, min=-reach, max=reach).astype(kind)


def setup_inputs(seed: int = 0) -> dict:
    keys = jax.random.split(jax.random.key(seed), 9)
    queries = draw_queries(jax.random.fold_in(keys[8], 71), 0)
    kv_cache = draw_kv_cache(jax.random.fold_in(keys[8], 71), 0)
    key_scale = jnp.clip(jnp.exp(jax.random.uniform(keys[2], (KVW,), jnp.float32, math.log(0.5), math.log(2.0))), 0.5, 2.0)
    fresh_input = normal_values(keys[3], (GROUPS, ROWS, D), 1.0, 6.0, ((0, 8), (2, 4)))
    kv_weight = normal_values(keys[4], (D, 2 * KVW), D ** -0.5, 0.0625, ((0, 4),))
    lengths = with_ends(jax.random.randint(keys[5], (GROUPS, 1), 1, SEQ + 1), jax.random.fold_in(keys[5], 1), 1, SEQ).astype(jnp.int32)
    page_list = draw_page_list(jax.random.fold_in(keys[8], 71), 0)
    owners_keys = jax.random.split(jax.random.fold_in(keys[7], 1), (GROUPS * N_RANK * FIN) // FIN)
    owners_turns = jax.random.permutation(jax.random.fold_in(keys[7], 3), (GROUPS * N_RANK * FIN) // FIN)
    owners = jax.vmap(lambda own, number: assign_block(jax.random.fold_in(keys[7], 2), own, number, FIN, N_RANK, 1, CAP, 1))(owners_keys, owners_turns).reshape((GROUPS * N_RANK * FIN, 1))
    return dict(queries=queries, kv_cache=kv_cache, key_scale=key_scale, fresh_input=fresh_input, kv_weight=kv_weight, lengths=lengths, page_list=page_list, owners=owners)


ROPE_BASE = 500000.0
NEG_FILL = -1e+30

def rope_tables(positions):
    half_width = HD // 2
    steps_index = jnp.arange(half_width, dtype=jnp.float32)
    inverse = jnp.exp(steps_index * (-2.0 * math.log(ROPE_BASE) / HD))
    angles = positions.astype(jnp.float32)[:, None] * inverse[None, :]
    return (jnp.cos(angles)[:, None, :], jnp.sin(angles)[:, None, :])

def rotate_heads(values, cosine, sine_part):
    half_width = HD // 2
    first_half = values[..., :half_width]
    second_half = values[..., half_width:]
    return jnp.concatenate([first_half * cosine - second_half * sine_part, second_half * cosine + first_half * sine_part], axis=-1)

def to_half(values):
    return lax.optimization_barrier(values.astype(jnp.bfloat16))

def attend_group(group_item, key_scale, kv_weight):
    query_rows, cache_rows, rows_in, length = group_item
    row_share = ROWS // N_RANK
    row_ids = jnp.arange(ROWS, dtype=jnp.int32)
    positions = length + row_ids
    cosine, sine_part = rope_tables(positions)
    query_rot = to_half(rotate_heads(query_rows.astype(jnp.float32).reshape(ROWS, HEADS, HD), cosine, sine_part))
    fresh_kv = to_half(jnp.dot(rows_in, kv_weight, preferred_element_type=jnp.float32))
    fresh_keys = to_half(rotate_heads(fresh_kv[:, :KVW].astype(jnp.float32).reshape(ROWS, KVH, HD), cosine, sine_part))
    cache_pos = jnp.arange(SEQ, dtype=jnp.int32)
    cache_cos, cache_sin = rope_tables(cache_pos)
    scaled = (cache_rows[:, :KVW].astype(jnp.float32) * key_scale[None, :]).reshape(SEQ, KVH, HD)
    cache_keys = to_half(rotate_heads(scaled, cache_cos, cache_sin))
    keys_all = jnp.concatenate([cache_keys.reshape(N_RANK, CTX, KVH, HD), fresh_keys.reshape(N_RANK, row_share, KVH, HD)], axis=1)
    vals_all = jnp.concatenate([cache_rows[:, KVW:].reshape(N_RANK, CTX, KVH, HD), fresh_kv[:, KVW:].reshape(N_RANK, row_share, KVH, HD)], axis=1)
    cache_ok = jnp.broadcast_to((cache_pos < length).reshape(1, N_RANK, CTX), (ROWS, N_RANK, CTX))
    fresh_ok = (row_ids[None, :] <= row_ids[:, None]).reshape(ROWS, N_RANK, row_share)
    allowed = jnp.concatenate([cache_ok, fresh_ok], axis=2)[:, None]
    query_groups = query_rot.reshape(ROWS, KVH, GQ, HD).transpose(1, 0, 2, 3)

    def per_head(head_item):
        query_head, key_head, value_head = head_item
        scores = jnp.einsum('rgd,nkd->rgnk', query_head.astype(jnp.float32), key_head.astype(jnp.float32)) / math.sqrt(HD)
        masked = jnp.where(allowed, scores, NEG_FILL)
        row_peak = lax.optimization_barrier(jnp.max(masked, axis=-1))
        weights = jnp.where(allowed, jnp.exp(masked - row_peak[..., None]), 0.0)
        row_total = lax.optimization_barrier(jnp.sum(weights, axis=-1))
        rounded = to_half(weights).astype(jnp.float32)
        numerator = jnp.einsum('rgnk,nkd->rgnd', rounded, value_head.astype(jnp.float32))
        row_top = lax.optimization_barrier(jnp.max(row_peak, axis=-1))
        factor = jnp.exp(row_peak - row_top[..., None])
        return lax.optimization_barrier(jnp.sum(numerator * factor[..., None], axis=2)) / lax.optimization_barrier(jnp.sum(row_total * factor, axis=2))[..., None]
    outputs = lax.map(per_head, (query_groups, keys_all.transpose(2, 0, 1, 3), vals_all.transpose(2, 0, 1, 3)))
    return outputs.transpose(1, 0, 2, 3).reshape(ROWS, QW).astype(jnp.bfloat16)

def hand_pages(kv_cache, page_list, owners):
    page_blocks = kv_cache[:N_GRP].reshape(N_GRP, N_RANK, PAGES, PAGE, 2 * KVW)
    listed = page_list.reshape(GROUPS, N_RANK, FIN)[:N_GRP].astype(jnp.int32)
    owner_ids = owners.reshape(GROUPS, N_RANK, FIN)[:N_GRP].astype(jnp.int32)
    targets = jnp.arange(N_RANK, dtype=jnp.int32)
    onehot = (owner_ids[..., None] == targets).astype(jnp.int32)
    running = jnp.cumsum(onehot, axis=2).astype(jnp.int32)
    slot_index = lax.optimization_barrier(jnp.sum(onehot * running, axis=-1)).astype(jnp.int32) - 1
    places = jnp.arange(CAP, dtype=jnp.int32)
    matches = (owner_ids[:, :, None, None, :] == targets[None, None, :, None, None]) & (slot_index[:, :, None, None, :] == places[None, None, None, :, None])
    present = jnp.any(matches, axis=-1)
    chosen = lax.optimization_barrier(jnp.sum(jnp.where(matches, listed[:, :, None, None, :], 0), axis=-1)).astype(jnp.int32)
    group_ids = jnp.arange(N_GRP, dtype=jnp.int32)[:, None, None, None]
    source_ids = jnp.arange(N_RANK, dtype=jnp.int32)[None, :, None, None]
    moved_pages = page_blocks[group_ids, source_ids, chosen]
    moved_pages = jnp.where(present[..., None, None], moved_pages, jnp.zeros((), jnp.bfloat16))
    moved_pages = moved_pages.transpose(0, 2, 1, 3, 4, 5).reshape(N_GRP * N_RANK, N_RANK * CAP, PAGE, 2 * KVW)
    return jnp.concatenate([jnp.zeros_like(moved_pages), moved_pages], axis=0)

def reference(queries, kv_cache, key_scale, fresh_input, kv_weight, lengths, page_list, owners):
    attended = lax.map(lambda group_item: attend_group(group_item, key_scale, kv_weight), (queries, kv_cache, fresh_input, lengths[:, 0].astype(jnp.int32)))
    handed = hand_pages(kv_cache, page_list, owners)
    return (attended, handed)
```

```python
import functools
import math

import jax
import jax.numpy as jnp
import numpy as np
from jax import lax
from jax.experimental import pallas as pl
from jax.experimental.pallas import tpu as pltpu
from jax.sharding import PartitionSpec as P

HEADS = 64
KVH = 8
HD = 128
ROWS = 128
CTX = 1024
PAGE = 16
GQ = 8
KVW = 1024

ROPE_BASE = 500000.0
NEG_FILL = -1e30
LOW = -1e29
TINY = 1.2e-38
NO_LEVEL = -16000.0
LEVELS = 32767.0
SCALE = 1.0 / math.sqrt(HD)
EXP2_SCALE = SCALE * math.log2(math.e)
LANES = 256
KEYS = 256
DEPTH = 512
TAIL = 8
CONTRACT_FIRST = (((0,), (0,)), ((), ()))
CONTRACT_LAST = (((1,), (1,)), ((), ()))
PARAMS = pltpu.CompilerParams(vmem_limit_bytes=60 << 20)
SMALL_PARAMS = pltpu.CompilerParams(vmem_limit_bytes=40 << 20)


def small_cost(flops):
    return pl.CostEstimate(flops=flops, bytes_accessed=1 << 16, transcendentals=0)


def inverse_frequencies():
    steps = np.arange(HD // 2, dtype=np.float32) * np.float32(-2.0 * math.log(ROPE_BASE) / HD)
    return np.exp(steps.astype(np.float64)).astype(np.float32)


def rope_tables(positions):
    inverse = jnp.asarray(np.tile(inverse_frequencies(), 2))
    sign = np.repeat(np.array([-1.0, 1.0], np.float32), HD // 2)
    angles = positions.astype(jnp.float32)[:, None] * inverse[None, :]
    return jnp.cos(angles), jnp.sin(angles) * sign[None, :]


def rotated(values, cosine, signed_sine):
    return values * cosine + pltpu.roll(values, HD // 2, 1) * signed_sine


def project_kernel(ranks, rank_ref, x_ref, w_ref, page_ref, owner_ref, cache_ref, *refs):
    out_refs, page_refs, there_ref = refs[:ranks], refs[ranks:2 * ranks], refs[2 * ranks]
    weight, total, sems, counts, page_sems = refs[2 * ranks + 1:]
    entries = page_ref.shape[0]
    share = out_refs[0].shape[0]
    chunks = weight.shape[0]

    def weight_copy(j):
        rows = pl.ds(j * weight.shape[1], weight.shape[1])
        return pltpu.make_async_copy(w_ref.at[rows, :], weight.at[j], sems.at[j])

    def page_rows(e):
        return pl.ds(pl.multiple_of(page_ref[e] * PAGE, PAGE), PAGE)

    def kept(e, slot):
        return pltpu.make_async_copy(cache_ref.at[page_rows(e), :], page_refs[0].at[slot], page_sems.at[e])

    def near(e, k, slot):
        source = cache_ref.at[page_rows(e), pl.ds(0, KVW)]
        return pltpu.make_async_copy(source, page_refs[k].at[slot], page_sems.at[e])

    def far(e, k, slot):
        source = cache_ref.at[page_rows(e), pl.ds(KVW, KVW)]
        return pltpu.make_async_copy(source, there_ref.at[k - 1, slot], page_sems.at[e])

    for j in range(chunks):
        weight_copy(j).start()
    for ref in [*page_refs, there_ref]:
        ref[...] = jnp.zeros_like(ref)
    for r in range(ranks):
        counts[r] = 0

    def begin(e, carry):
        owner = owner_ref[e]
        slot = counts[owner]
        counts[owner] = slot + 1
        place = lax.rem(owner - rank_ref[0] + ranks, ranks)

        @pl.when(place == 0)
        def _():
            kept(e, slot).start()

        for k in range(1, ranks):
            @pl.when(place == k)
            def _():
                near(e, k, slot).start()
                far(e, k, slot).start()
        return carry

    lax.fori_loop(0, entries, begin, 0)
    for j in range(chunks):
        weight_copy(j).wait()
        depth = weight.shape[1]
        part = jnp.dot(
            x_ref[:, j * depth:(j + 1) * depth], weight[j], preferred_element_type=jnp.float32
        )
        if j:
            part = part + total[...]
        total[...] = part
    for k in range(ranks):
        dest = lax.rem(rank_ref[0] + k, ranks)
        out_refs[k][...] = total[pl.ds(pl.multiple_of(dest * share, share), share), :]

    def end(e, carry):
        kept(e, 0).wait()
        return carry

    lax.fori_loop(0, entries, end, 0)


def project(me, x, weight, page_list, owner_ids, cache, ranks):
    share = ROWS // ranks
    depth = weight.shape[0]
    block = min(depth, DEPTH)
    entries = page_list.shape[0]
    slots = 2 * entries // ranks
    smem = pl.BlockSpec(memory_space=pltpu.SMEM)
    vmem = pl.BlockSpec(memory_space=pltpu.VMEM)
    anywhere = pl.BlockSpec(memory_space=pl.ANY)
    out_shape = [jax.ShapeDtypeStruct((share, 2 * KVW), jnp.float32)] * ranks
    out_shape += [jax.ShapeDtypeStruct((slots, PAGE, 2 * KVW), jnp.bfloat16)]
    out_shape += [jax.ShapeDtypeStruct((slots, PAGE, KVW), jnp.bfloat16)] * (ranks - 1)
    out_shape += [jax.ShapeDtypeStruct((ranks - 1, slots, PAGE, KVW), jnp.bfloat16)]
    out = pl.pallas_call(
        functools.partial(project_kernel, ranks),
        in_specs=[smem, vmem, anywhere, smem, smem, anywhere],
        out_specs=[vmem] * len(out_shape),
        out_shape=out_shape,
        scratch_shapes=[
            pltpu.VMEM((depth // block, block, 2 * KVW), jnp.bfloat16),
            pltpu.VMEM((ROWS, 2 * KVW), jnp.float32),
            pltpu.SemaphoreType.DMA((depth // block,)),
            pltpu.SMEM((ranks,), jnp.int32),
            pltpu.SemaphoreType.DMA((entries,)),
        ],
        compiler_params=PARAMS,
        cost_estimate=small_cost(1 << 20),
        name="project",
    )(me.reshape(1), x, weight, page_list, owner_ids, cache)
    return out[:ranks], out[ranks:2 * ranks], out[2 * ranks]


def prepare_kernel(q_ref, k_ref, scale_ref, qc_ref, qs_ref, kc_ref, ks_ref, q_out, k_out):
    for g in range(GQ):
        q = rotated(q_ref[:, g * HD:(g + 1) * HD].astype(jnp.float32), qc_ref[...], qs_ref[...])
        q_out[g * ROWS:(g + 1) * ROWS, :] = q.astype(jnp.bfloat16)
    for h in range(KVH):
        columns = slice(h * HD, (h + 1) * HD)
        key = k_ref[:, columns].astype(jnp.float32) * scale_ref[:, columns]
        k_out[h] = rotated(key, kc_ref[...], ks_ref[...]).astype(jnp.bfloat16)


def prepare(queries, cache, key_scale, q_tables, k_tables):
    fixed = lambda j: (0, 0)
    rows = CTX // KVH
    return pl.pallas_call(
        prepare_kernel,
        grid=(KVH,),
        in_specs=[
            pl.BlockSpec((ROWS, GQ * HD), lambda j: (0, j)),
            pl.BlockSpec((rows, KVW), lambda j: (j, 0)),
            pl.BlockSpec((1, KVW), fixed),
            pl.BlockSpec((ROWS, HD), fixed),
            pl.BlockSpec((ROWS, HD), fixed),
            pl.BlockSpec((rows, HD), lambda j: (j, 0)),
            pl.BlockSpec((rows, HD), lambda j: (j, 0)),
        ],
        out_specs=[
            pl.BlockSpec((GQ * ROWS, HD), lambda j: (j, 0)),
            pl.BlockSpec((KVH, rows, HD), lambda j: (0, j, 0)),
        ],
        out_shape=[
            jax.ShapeDtypeStruct((HEADS * ROWS, HD), jnp.bfloat16),
            jax.ShapeDtypeStruct((KVH, CTX, HD), jnp.bfloat16),
        ],
        compiler_params=PARAMS,
        cost_estimate=small_cost(1 << 20),
        name="prepare",
    )(queries, cache, key_scale, *q_tables, *k_tables)


def split_level(level):
    doubled = jnp.maximum(level, NO_LEVEL) * 2.0
    high = jnp.floor(doubled)
    return [high, (doubled - high) * 65536.0 - 32768.0]


def joined_level(high, low):
    return (high + (low + 32768.0) * (1.0 / 65536.0)) * 0.5


def code_into(out_ref, lanes, top, total, numerator):
    largest = jnp.maximum(jnp.max(jnp.abs(numerator), axis=0, keepdims=True), TINY)
    coded = jnp.round(numerator * (1.0 / largest) * LEVELS)
    out_ref[:HD, lanes] = coded.astype(jnp.int32).astype(jnp.int16)
    tail = split_level(top + jnp.log2(largest)) + split_level(top + jnp.log2(total))
    tail = jnp.concatenate(tail + [jnp.zeros((TAIL - 4, top.shape[1]), jnp.float32)], axis=0)
    out_ref[HD:, lanes] = tail.astype(jnp.int32).astype(jnp.int16)


def decode(ref, lanes):
    tail = ref[HD:, lanes].astype(jnp.int32).astype(jnp.float32)
    values = ref[:HD, lanes].astype(jnp.int32).astype(jnp.float32)
    return joined_level(tail[0:1], tail[1:2]), joined_level(tail[2:3], tail[3:4]), values


def merged(top, total, numerator, parts):
    peak = functools.reduce(jnp.maximum, [p[1] for p in parts], top)
    if total is not None:
        factor = jnp.exp2(top - peak)
        total, numerator = total * factor, numerator * factor
    for level, weight, values in parts:
        more = jnp.exp2(weight - peak)
        part = values * (jnp.exp2(level - peak) * (1.0 / LEVELS))
        total = more if total is None else total + more
        numerator = part if numerator is None else numerator + part
    return peak, total, numerator


def fold_rows(values, combine):
    rows, cols = values.shape
    return combine(values.reshape(rows // 8, 8, cols), axis=0)


def attend_kernel(ranks, is_open, info, q_ref, k_ref, v_ref, qc_ref, qs_ref, *refs):
    fk_refs, refs = refs[:ranks], refs[ranks:]
    fv_refs, refs = refs[:ranks], refs[ranks:]
    if is_open:
        num_ref, stat_ref, scores = refs
    else:
        out_ref, scores = refs
    fresh_value = sum(ref[...] for ref in fv_refs).astype(jnp.bfloat16)
    rank = info[1]
    share = fk_refs[0].shape[0]
    valid = info[0] - rank * CTX
    first = pl.multiple_of(rank * share, share)
    fresh_key = sum(ref[...] for ref in fk_refs).astype(jnp.bfloat16).astype(jnp.float32)
    fresh_key = rotated(
        fresh_key, qc_ref[pl.ds(first, share), :], qs_ref[pl.ds(first, share), :]
    ).astype(jnp.bfloat16)
    cols = q_ref.shape[0]
    queries = q_ref[...]
    key_id = first + lax.broadcasted_iota(jnp.int32, (share, cols), 0)
    row_id = lax.broadcasted_iota(jnp.int32, (share, cols), 1) % ROWS
    fs = lax.dot_general(fresh_key, queries, CONTRACT_LAST, preferred_element_type=jnp.float32)
    fs = jnp.where(key_id <= row_id, fs, NEG_FILL)
    peak = fold_rows(fs, jnp.max)
    for t in range(CTX // KEYS):
        rows = slice(t * KEYS, (t + 1) * KEYS)
        s = lax.dot_general(
            k_ref[0, rows, :], queries, CONTRACT_LAST, preferred_element_type=jnp.float32
        )
        position = t * KEYS + lax.broadcasted_iota(jnp.int32, (KEYS, cols), 0)
        s = jnp.where(position < valid, s, NEG_FILL)
        scores[rows, :] = s
        peak = jnp.maximum(peak, fold_rows(s, jnp.max))
    peak = jnp.max(peak, axis=0, keepdims=True)
    base = jnp.maximum(peak, LOW)
    w = jnp.exp((fs - base) * SCALE)
    total = fold_rows(w, jnp.sum)
    numerator = lax.dot_general(
        fresh_value, w.astype(jnp.bfloat16), CONTRACT_FIRST, preferred_element_type=jnp.float32
    )
    for t in range(CTX // KEYS):
        rows = slice(t * KEYS, (t + 1) * KEYS)
        w = jnp.exp((scores[rows, :] - base) * SCALE)
        total = total + fold_rows(w, jnp.sum)
        numerator = numerator + lax.dot_general(
            v_ref[rows, :], w.astype(jnp.bfloat16), CONTRACT_FIRST, preferred_element_type=jnp.float32
        )
    total = jnp.sum(total, axis=0, keepdims=True)
    top = jnp.maximum(peak * EXP2_SCALE, NO_LEVEL)
    if is_open:
        num_ref[0] = numerator
        stat_ref[0] = jnp.concatenate([top, total, jnp.zeros((6, cols), jnp.float32)], axis=0)
    else:
        code_into(out_ref, slice(0, cols), top, total, numerator)


def layout(ranks):
    heads_here = HEADS // ranks
    pieces = max(1, heads_here // GQ)
    heads = heads_here // pieces
    return pieces, heads, heads * ROWS, ROWS // ranks


def whole(j, s):
    return (0, 0)


def opened_specs(cols):
    place = lambda j, s: (j, 0, 0)
    return [pl.BlockSpec((1, HD, cols), place), pl.BlockSpec((1, 8, cols), place)]


def attend(info, queries, keys, cache, q_tables, fresh, ranks, is_open):
    _, _, cols, share = layout(ranks)
    steps = (info.shape[0] - 2) // 2
    if is_open:
        out_specs = opened_specs(cols)
        out_shape = [
            jax.ShapeDtypeStruct((steps, HD, cols), jnp.float32),
            jax.ShapeDtypeStruct((steps, 8, cols), jnp.float32),
        ]
    else:
        out_specs = pl.BlockSpec((HD + TAIL, cols), lambda j, s: (0, j))
        out_shape = jax.ShapeDtypeStruct((HD + TAIL, steps * cols), jnp.int16)
    return pl.pallas_call(
        functools.partial(attend_kernel, ranks, is_open),
        grid_spec=pltpu.PrefetchScalarGridSpec(
            num_scalar_prefetch=1,
            grid=(steps,),
            in_specs=[
                pl.BlockSpec((cols, HD), lambda j, s: (s[2 + 2 * j], 0)),
                pl.BlockSpec((1, CTX, HD), lambda j, s: (s[3 + 2 * j], 0, 0)),
                pl.BlockSpec((CTX, HD), lambda j, s: (0, KVH + s[3 + 2 * j])),
                pl.BlockSpec((ROWS, HD), whole),
                pl.BlockSpec((ROWS, HD), whole),
            ]
            + [pl.BlockSpec((share, HD), lambda j, s: (0, s[3 + 2 * j]))] * ranks
            + [pl.BlockSpec((share, HD), lambda j, s: (0, KVH + s[3 + 2 * j]))] * ranks,
            out_specs=out_specs,
            scratch_shapes=[pltpu.VMEM((CTX, cols), jnp.float32)],
        ),
        out_shape=out_shape,
        compiler_params=PARAMS,
        cost_estimate=small_cost(1 << 31),
        name="attend_open" if is_open else "attend",
    )(info, queries, keys, cache, *q_tables, *fresh, *fresh)


def close_kernel(is_last, num_ref, stat_ref, *refs):
    in_refs, out_ref = refs[:-1], refs[-1]
    for b in range(out_ref.shape[1] // LANES):
        lanes = slice(b * LANES, (b + 1) * LANES)
        top, total, numerator = stat_ref[0, 0:1, lanes], stat_ref[0, 1:2, lanes], num_ref[0, :, lanes]
        parts = [decode(ref, lanes) for ref in in_refs]
        top, total, numerator = merged(top, total, numerator, parts)
        if not is_last:
            code_into(out_ref, lanes, top, total, numerator)
            continue
        numerator = numerator / total
        for h in range(LANES // ROWS):
            column = b * LANES + h * HD
            out_ref[:, column:column + HD] = (
                numerator[:, h * ROWS:(h + 1) * ROWS].T.astype(jnp.bfloat16)
            )


def close(opened, received, ranks, is_last=False):
    pieces, _, cols, _ = layout(ranks)
    rows, kind = (ROWS, jnp.bfloat16) if is_last else (HD + TAIL, jnp.int16)
    place = lambda j: (j, 0, 0)
    return pl.pallas_call(
        functools.partial(close_kernel, is_last),
        grid=(pieces,),
        in_specs=[pl.BlockSpec((1, HD, cols), place), pl.BlockSpec((1, 8, cols), place)]
        + [pl.BlockSpec((HD + TAIL, cols), lambda j: (0, j))] * len(received),
        out_specs=pl.BlockSpec((rows, cols), lambda j: (0, j)),
        out_shape=jax.ShapeDtypeStruct((rows, pieces * cols), kind),
        compiler_params=PARAMS,
        cost_estimate=small_cost(1 << 18),
        name="finish" if is_last else "close",
    )(*opened, *received)


def choose_kernel(sec_ref, *refs):
    count = (len(refs) - 2) // 2
    near, there_ref, out_refs, sems = refs[:count], refs[count], refs[count + 1:-1], refs[-1]
    first = sec_ref[0] == 0
    for k in range(count):
        @pl.when(first)
        def _():
            pltpu.make_async_copy(near[k], out_refs[k], sems.at[k]).start()

        @pl.when(jnp.logical_not(first))
        def _():
            pltpu.make_async_copy(there_ref.at[k], out_refs[k], sems.at[k]).start()

    for k in range(count):
        pltpu.make_async_copy(near[k], out_refs[k], sems.at[k]).wait()


def choose(sec, near, there):
    count = len(near)
    return pl.pallas_call(
        choose_kernel,
        in_specs=[pl.BlockSpec(memory_space=pltpu.SMEM)] + [pl.BlockSpec(memory_space=pl.ANY)] * (count + 1),
        out_specs=[pl.BlockSpec(memory_space=pltpu.VMEM)] * count,
        out_shape=[jax.ShapeDtypeStruct(there.shape[1:], there.dtype)] * count,
        scratch_shapes=[pltpu.SemaphoreType.DMA((count,))],
        compiler_params=SMALL_PARAMS,
        cost_estimate=small_cost(1 << 18),
        name="choose",
    )(sec.reshape(1), *near, there)


def stack_kernel(*refs):
    out_ref, sems = refs[-2:]
    copies = [
        pltpu.make_async_copy(ref, out_ref.at[k], sems.at[k]) for k, ref in enumerate(refs[:-2])
    ]
    for c in copies:
        c.start()
    for c in copies:
        c.wait()


def stack(values):
    count = len(values)
    return pl.pallas_call(
        stack_kernel,
        in_specs=[pl.BlockSpec(memory_space=pl.ANY)] * count,
        out_specs=pl.BlockSpec(memory_space=pltpu.VMEM),
        out_shape=jax.ShapeDtypeStruct((count,) + values[0].shape, values[0].dtype),
        scratch_shapes=[pltpu.SemaphoreType.DMA((count,))],
        compiler_params=SMALL_PARAMS,
        cost_estimate=small_cost(1 << 32),
        name="stack",
    )(*values)


def arrange_kernel(place_ref, kept_ref, crossed_ref, routed_ref, out_ref):
    count = crossed_ref.shape[0]
    shift = lax.rem(place_ref[1] - pl.program_id(0) + count + 1, count + 1)
    second = place_ref[0] > 0

    @pl.when(jnp.logical_not(second))
    def _():
        out_ref[...] = jnp.zeros_like(out_ref)

    @pl.when(jnp.logical_and(second, shift == 0))
    def _():
        out_ref[...] = kept_ref[...]

    @pl.when(jnp.logical_and(second, shift > 0))
    def _():
        out_ref[:, :, :KVW] = crossed_ref[shift - 1]
        out_ref[:, :, KVW:] = routed_ref[shift - 1]


def arrange(place, kept, crossed, routed):
    ranks = crossed.shape[0] + 1
    slots = kept.shape[0]
    return pl.pallas_call(
        arrange_kernel,
        grid=(ranks,),
        in_specs=[
            pl.BlockSpec(memory_space=pltpu.SMEM),
            pl.BlockSpec(kept.shape, lambda j: (0, 0, 0)),
            pl.BlockSpec(crossed.shape, lambda j: (0, 0, 0, 0)),
            pl.BlockSpec(routed.shape, lambda j: (0, 0, 0, 0)),
        ],
        out_specs=pl.BlockSpec((slots, PAGE, 2 * KVW), lambda j: (j, 0, 0)),
        out_shape=jax.ShapeDtypeStruct((ranks * slots, PAGE, 2 * KVW), jnp.bfloat16),
        compiler_params=PARAMS,
        cost_estimate=small_cost(1 << 18),
        name="arrange",
    )(place, kept, crossed, routed)


def after(value, earlier):
    return lax.optimization_barrier((value, earlier))[0]


def shards(queries, kv_cache, key_scale, fresh_input, kv_weight, lengths, page_list, owners):
    ranks = lax.axis_size("rank")
    secs = lax.axis_size("sec")
    me = lax.axis_index("rank").astype(jnp.int32)
    sec = lax.axis_index("sec").astype(jnp.int32)
    cache = kv_cache[0]
    length = lengths[0, 0]
    pieces, heads, _, _ = layout(ranks)

    def shifted(value, k):
        return lax.ppermute(value, "rank", [(i, (i + k) % ranks) for i in range(ranks)])

    def swapped(value, bit):
        return lax.ppermute(value, "rank", [(i, i ^ bit) for i in range(ranks)])

    def handed_on(value):
        return lax.ppermute(value, "sec", [(i, (i + 1) % secs) for i in range(secs)])

    part, (kept, *near), there = project(
        me, fresh_input[0], kv_weight, page_list, owners[:, 0], cache, ranks
    )
    fresh = [part[0]] + [shifted(part[k], k) for k in range(1, ranks)]

    q_tables = rope_tables(after(length, part) + jnp.arange(ROWS, dtype=jnp.int32))
    k_tables = rope_tables(after(me, part) * CTX + jnp.arange(CTX, dtype=jnp.int32))
    there = handed_on(there)
    kept = handed_on(kept)
    q_rot, keys = prepare(queries[0], cache, key_scale[None, :], q_tables, k_tables)
    chosen = choose(sec, near, after(there, q_rot))
    fresh = after(fresh, chosen)

    def attend_to(code, earlier, is_open):
        info = [length, me]
        for p in range(pieces):
            chosen = (me ^ code) * pieces + p
            info += [chosen, chosen * heads // GQ]
        return attend(
            jnp.stack(info), after(q_rot, earlier), keys, cache, q_tables, fresh, ranks, is_open
        )

    taken = {code: [] for code in range(ranks)}

    def send(value, code, bit):
        taken[code ^ bit].append(swapped(value, bit))

    routed = [shifted(c, k + 1) for k, c in enumerate(chosen)]
    last = chosen
    for code in range(ranks - 1, 1, -2):
        last = attend_to(code, last, False)
        send(last, code, 1)
    merging = {}
    for code in range(ranks - 2, 0, -2):
        last = merging[code] = attend_to(code, (last, kept), True)
    last = attend_to(1, last, False)
    send(last, 1, 1)
    both = stack(after(routed, last))
    bit = 2
    while bit < ranks:
        for code in range(ranks - bit, 0, -2 * bit):
            last = close(after(merging[code], both), taken[code], ranks)
            send(last, code, bit)
        bit *= 2
    crossed = handed_on(both)
    own = attend_to(0, last, True)

    handed = arrange(jnp.stack([sec, me]), kept, crossed, both)[None]
    attended = close(own, taken[0], ranks, is_last=True)[None]
    return (attended, handed)


def solution(mesh):
    return jax.shard_map(
        shards,
        mesh=mesh,
        in_specs=(
            P(("sec", "grp"), None, None),
            P(("sec", "grp"), "rank", None),
            P(),
            P(("sec", "grp"), None, "rank"),
            P("rank", None),
            P(("sec", "grp"), None),
            P(("sec", "grp", "rank")),
            P(("sec", "grp", "rank"), None),
        ),
        out_specs=(P(("sec", "grp"), None, "rank"), P(("sec", "grp", "rank"), None, None, None)),
        check_vma=False,
    )
```

```python
import functools
import math

import jax
import jax.numpy as jnp
import numpy as np
from jax import lax
from jax.experimental import pallas as pl
from jax.experimental.pallas import tpu as pltpu
from jax.sharding import PartitionSpec as P

HEADS = 64
KVH = 8
HD = 128
ROWS = 128
CTX = 1024
PAGE = 16
GQ = 8
KVW = 1024

ROPE_BASE = 500000.0
NEG_FILL = -1e30
LOW = -1e29
TINY = 1.2e-38
NO_LEVEL = -16000.0
LEVELS = 32767.0
SCALE = 1.0 / math.sqrt(HD)
EXP2_SCALE = SCALE * math.log2(math.e)
LANES = 256
KEYS = 256
DEPTH = 512
TAIL = 8
CONTRACT_FIRST = (((0,), (0,)), ((), ()))
CONTRACT_LAST = (((1,), (1,)), ((), ()))
PARAMS = pltpu.CompilerParams(vmem_limit_bytes=60 << 20)
SMALL_PARAMS = pltpu.CompilerParams(vmem_limit_bytes=40 << 20)


def small_cost(flops):
    return pl.CostEstimate(flops=flops, bytes_accessed=1 << 16, transcendentals=0)


def inverse_frequencies():
    steps = np.arange(HD // 2, dtype=np.float32) * np.float32(-2.0 * math.log(ROPE_BASE) / HD)
    return np.exp(steps.astype(np.float64)).astype(np.float32)


def rope_tables(positions):
    inverse = jnp.asarray(np.tile(inverse_frequencies(), 2))
    sign = np.repeat(np.array([-1.0, 1.0], np.float32), HD // 2)
    angles = positions.astype(jnp.float32)[:, None] * inverse[None, :]
    return jnp.cos(angles), jnp.sin(angles) * sign[None, :]


def rotated(values, cosine, signed_sine):
    return values * cosine + pltpu.roll(values, HD // 2, 1) * signed_sine


def project_kernel(ranks, rank_ref, x_ref, w_ref, page_ref, owner_ref, cache_ref, *refs):
    out_refs, page_refs, there_ref = refs[:ranks], refs[ranks:2 * ranks], refs[2 * ranks]
    weight, total, sems, counts, page_sems = refs[2 * ranks + 1:]
    entries = page_ref.shape[0]
    share = out_refs[0].shape[0]
    chunks = weight.shape[0]

    def weight_copy(j):
        rows = pl.ds(j * weight.shape[1], weight.shape[1])
        return pltpu.make_async_copy(w_ref.at[rows, :], weight.at[j], sems.at[j])

    def page_rows(e):
        return pl.ds(pl.multiple_of(page_ref[e] * PAGE, PAGE), PAGE)

    def kept(e, slot):
        return pltpu.make_async_copy(cache_ref.at[page_rows(e), :], page_refs[0].at[slot], page_sems.at[e])

    def near(e, k, slot):
        source = cache_ref.at[page_rows(e), pl.ds(0, KVW)]
        return pltpu.make_async_copy(source, page_refs[k].at[slot], page_sems.at[e])

    def far(e, k, slot):
        source = cache_ref.at[page_rows(e), pl.ds(KVW, KVW)]
        return pltpu.make_async_copy(source, there_ref.at[k - 1, slot], page_sems.at[e])

    for j in range(chunks):
        weight_copy(j).start()
    for ref in [*page_refs, there_ref]:
        ref[...] = jnp.zeros_like(ref)
    for r in range(ranks):
        counts[r] = 0

    def begin(e, carry):
        owner = owner_ref[e]
        slot = counts[owner]
        counts[owner] = slot + 1
        place = lax.rem(owner - rank_ref[0] + ranks, ranks)

        @pl.when(place == 0)
        def _():
            kept(e, slot).start()

        for k in range(1, ranks):
            @pl.when(place == k)
            def _():
                near(e, k, slot).start()
                far(e, k, slot).start()
        return carry

    lax.fori_loop(0, entries, begin, 0)
    for j in range(chunks):
        weight_copy(j).wait()
        depth = weight.shape[1]
        part = jnp.dot(
            x_ref[:, j * depth:(j + 1) * depth], weight[j], preferred_element_type=jnp.float32
        )
        if j:
            part = part + total[...]
        total[...] = part
    for k in range(ranks):
        dest = lax.rem(rank_ref[0] + k, ranks)
        out_refs[k][...] = total[pl.ds(pl.multiple_of(dest * share, share), share), :]

    def end(e, carry):
        kept(e, 0).wait()
        return carry

    lax.fori_loop(0, entries, end, 0)


def project(me, x, weight, page_list, owner_ids, cache, ranks):
    share = ROWS // ranks
    depth = weight.shape[0]
    block = min(depth, DEPTH)
    entries = page_list.shape[0]
    slots = 2 * entries // ranks
    smem = pl.BlockSpec(memory_space=pltpu.SMEM)
    vmem = pl.BlockSpec(memory_space=pltpu.VMEM)
    anywhere = pl.BlockSpec(memory_space=pl.ANY)
    out_shape = [jax.ShapeDtypeStruct((share, 2 * KVW), jnp.float32)] * ranks
    out_shape += [jax.ShapeDtypeStruct((slots, PAGE, 2 * KVW), jnp.bfloat16)]
    out_shape += [jax.ShapeDtypeStruct((slots, PAGE, KVW), jnp.bfloat16)] * (ranks - 1)
    out_shape += [jax.ShapeDtypeStruct((ranks - 1, slots, PAGE, KVW), jnp.bfloat16)]
    out = pl.pallas_call(
        functools.partial(project_kernel, ranks),
        in_specs=[smem, vmem, anywhere, smem, smem, anywhere],
        out_specs=[vmem] * len(out_shape),
        out_shape=out_shape,
        scratch_shapes=[
            pltpu.VMEM((depth // block, block, 2 * KVW), jnp.bfloat16),
            pltpu.VMEM((ROWS, 2 * KVW), jnp.float32),
            pltpu.SemaphoreType.DMA((depth // block,)),
            pltpu.SMEM((ranks,), jnp.int32),
            pltpu.SemaphoreType.DMA((entries,)),
        ],
        compiler_params=PARAMS,
        cost_estimate=small_cost(1 << 20),
        name="project",
    )(me.reshape(1), x, weight, page_list, owner_ids, cache)
    return out[:ranks], out[ranks:2 * ranks], out[2 * ranks]


def prepare_kernel(q_ref, k_ref, scale_ref, qc_ref, qs_ref, kc_ref, ks_ref, q_out, k_out):
    for g in range(GQ):
        q = rotated(q_ref[:, g * HD:(g + 1) * HD].astype(jnp.float32), qc_ref[...], qs_ref[...])
        q_out[g * ROWS:(g + 1) * ROWS, :] = q.astype(jnp.bfloat16)
    for h in range(KVH):
        columns = slice(h * HD, (h + 1) * HD)
        key = k_ref[:, columns].astype(jnp.float32) * scale_ref[:, columns]
        k_out[h] = rotated(key, kc_ref[...], ks_ref[...]).astype(jnp.bfloat16)


def prepare(queries, cache, key_scale, q_tables, k_tables):
    fixed = lambda j: (0, 0)
    rows = CTX // KVH
    return pl.pallas_call(
        prepare_kernel,
        grid=(KVH,),
        in_specs=[
            pl.BlockSpec((ROWS, GQ * HD), lambda j: (0, j)),
            pl.BlockSpec((rows, KVW), lambda j: (j, 0)),
            pl.BlockSpec((1, KVW), fixed),
            pl.BlockSpec((ROWS, HD), fixed),
            pl.BlockSpec((ROWS, HD), fixed),
            pl.BlockSpec((rows, HD), lambda j: (j, 0)),
            pl.BlockSpec((rows, HD), lambda j: (j, 0)),
        ],
        out_specs=[
            pl.BlockSpec((GQ * ROWS, HD), lambda j: (j, 0)),
            pl.BlockSpec((KVH, rows, HD), lambda j: (0, j, 0)),
        ],
        out_shape=[
            jax.ShapeDtypeStruct((HEADS * ROWS, HD), jnp.bfloat16),
            jax.ShapeDtypeStruct((KVH, CTX, HD), jnp.bfloat16),
        ],
        compiler_params=PARAMS,
        cost_estimate=small_cost(1 << 20),
        name="prepare",
    )(queries, cache, key_scale, *q_tables, *k_tables)


def split_level(level):
    doubled = jnp.maximum(level, NO_LEVEL) * 2.0
    high = jnp.floor(doubled)
    return [high, (doubled - high) * 65536.0 - 32768.0]


def joined_level(high, low):
    return (high + (low + 32768.0) * (1.0 / 65536.0)) * 0.5


def code_into(out_ref, lanes, top, total, numerator):
    largest = jnp.maximum(jnp.max(jnp.abs(numerator), axis=0, keepdims=True), TINY)
    coded = jnp.round(numerator * (1.0 / largest) * LEVELS)
    out_ref[:HD, lanes] = coded.astype(jnp.int32).astype(jnp.int16)
    tail = split_level(top + jnp.log2(largest)) + split_level(top + jnp.log2(total))
    tail = jnp.concatenate(tail + [jnp.zeros((TAIL - 4, top.shape[1]), jnp.float32)], axis=0)
    out_ref[HD:, lanes] = tail.astype(jnp.int32).astype(jnp.int16)


def decode(ref, lanes):
    tail = ref[HD:, lanes].astype(jnp.int32).astype(jnp.float32)
    values = ref[:HD, lanes].astype(jnp.int32).astype(jnp.float32)
    return joined_level(tail[0:1], tail[1:2]), joined_level(tail[2:3], tail[3:4]), values


def merged(top, total, numerator, parts):
    peak = functools.reduce(jnp.maximum, [p[1] for p in parts], top)
    if total is not None:
        factor = jnp.exp2(top - peak)
        total, numerator = total * factor, numerator * factor
    for level, weight, values in parts:
        more = jnp.exp2(weight - peak)
        part = values * (jnp.exp2(level - peak) * (1.0 / LEVELS))
        total = more if total is None else total + more
        numerator = part if numerator is None else numerator + part
    return peak, total, numerator


def fold_rows(values, combine):
    rows, cols = values.shape
    return combine(values.reshape(rows // 8, 8, cols), axis=0)


def gather_kernel(ranks, info, qc_ref, qs_ref, *refs):
    key_out, value_out = refs[ranks:]
    share = refs[0].shape[0]
    mine = pl.ds(pl.multiple_of(info[1] * share, share), share)
    cosine, signed_sine = qc_ref[mine, :], qs_ref[mine, :]
    for h in range(KVH):
        columns = slice(h * HD, (h + 1) * HD)
        key = sum(ref[:, columns] for ref in refs[:ranks])
        key = key.astype(jnp.bfloat16).astype(jnp.float32)
        key_out[h] = rotated(key, cosine, signed_sine).astype(jnp.bfloat16)
        columns = slice(KVW + h * HD, KVW + (h + 1) * HD)
        value_out[h] = sum(ref[:, columns] for ref in refs[:ranks]).astype(jnp.bfloat16)


def gather(info, q_tables, fresh):
    share = fresh[0].shape[0]
    vmem = pl.BlockSpec(memory_space=pltpu.VMEM)
    return pl.pallas_call(
        functools.partial(gather_kernel, len(fresh)),
        in_specs=[pl.BlockSpec(memory_space=pltpu.SMEM)] + [vmem] * (2 + len(fresh)),
        out_specs=[vmem] * 2,
        out_shape=[jax.ShapeDtypeStruct((KVH, share, HD), jnp.bfloat16)] * 2,
        compiler_params=SMALL_PARAMS,
        cost_estimate=small_cost(1 << 18),
        name="gather",
    )(info, *q_tables, *fresh)


def attend_kernel(is_open, info, q_ref, k_ref, v_ref, fk_ref, fv_ref, *refs):
    if is_open:
        num_ref, stat_ref, scores = refs
    else:
        out_ref, scores = refs
    rank = info[1]
    share = fk_ref.shape[1]
    valid = info[0] - rank * CTX
    first = rank * share
    fresh_key, fresh_value = fk_ref[0], fv_ref[0]
    cols = q_ref.shape[0]
    queries = q_ref[...]
    key_id = first + lax.broadcasted_iota(jnp.int32, (share, cols), 0)
    row_id = lax.broadcasted_iota(jnp.int32, (share, cols), 1) % ROWS
    fs = lax.dot_general(fresh_key, queries, CONTRACT_LAST, preferred_element_type=jnp.float32)
    fs = jnp.where(key_id <= row_id, fs, NEG_FILL)
    peak = fold_rows(fs, jnp.max)
    for t in range(CTX // KEYS):
        rows = slice(t * KEYS, (t + 1) * KEYS)
        s = lax.dot_general(
            k_ref[0, rows, :], queries, CONTRACT_LAST, preferred_element_type=jnp.float32
        )
        position = t * KEYS + lax.broadcasted_iota(jnp.int32, (KEYS, cols), 0)
        s = jnp.where(position < valid, s, NEG_FILL)
        scores[rows, :] = s
        peak = jnp.maximum(peak, fold_rows(s, jnp.max))
    peak = jnp.max(peak, axis=0, keepdims=True)
    base = jnp.maximum(peak, LOW)
    w = jnp.exp((fs - base) * SCALE)
    total = fold_rows(w, jnp.sum)
    numerator = lax.dot_general(
        fresh_value, w.astype(jnp.bfloat16), CONTRACT_FIRST, preferred_element_type=jnp.float32
    )
    for t in range(CTX // KEYS):
        rows = slice(t * KEYS, (t + 1) * KEYS)
        w = jnp.exp((scores[rows, :] - base) * SCALE)
        total = total + fold_rows(w, jnp.sum)
        numerator = numerator + lax.dot_general(
            v_ref[rows, :], w.astype(jnp.bfloat16), CONTRACT_FIRST, preferred_element_type=jnp.float32
        )
    total = jnp.sum(total, axis=0, keepdims=True)
    top = jnp.maximum(peak * EXP2_SCALE, NO_LEVEL)
    if is_open:
        num_ref[0] = numerator
        stat_ref[0] = jnp.concatenate([top, total, jnp.zeros((6, cols), jnp.float32)], axis=0)
    else:
        code_into(out_ref, slice(0, cols), top, total, numerator)


def layout(ranks):
    heads_here = HEADS // ranks
    pieces = max(1, heads_here // GQ)
    heads = heads_here // pieces
    return pieces, heads, heads * ROWS, ROWS // ranks


def whole(j, s):
    return (0, 0)


def opened_specs(cols):
    place = lambda j, s: (j, 0, 0)
    return [pl.BlockSpec((1, HD, cols), place), pl.BlockSpec((1, 8, cols), place)]


def attend(info, code, queries, keys, cache, fresh, ranks, is_open):
    pieces, heads, cols, share = layout(ranks)

    def piece(j, s):
        return (s[1] ^ code) * pieces + j

    def key_head(j, s):
        return piece(j, s) * heads // GQ

    if is_open:
        out_specs = opened_specs(cols)
        out_shape = [
            jax.ShapeDtypeStruct((pieces, HD, cols), jnp.float32),
            jax.ShapeDtypeStruct((pieces, 8, cols), jnp.float32),
        ]
    else:
        out_specs = pl.BlockSpec((HD + TAIL, cols), lambda j, s: (0, j))
        out_shape = jax.ShapeDtypeStruct((HD + TAIL, pieces * cols), jnp.int16)
    own_head = lambda j, s: (key_head(j, s), 0, 0)
    return pl.pallas_call(
        functools.partial(attend_kernel, is_open),
        grid_spec=pltpu.PrefetchScalarGridSpec(
            num_scalar_prefetch=1,
            grid=(pieces,),
            in_specs=[
                pl.BlockSpec((cols, HD), lambda j, s: (piece(j, s), 0)),
                pl.BlockSpec((1, CTX, HD), own_head),
                pl.BlockSpec((CTX, HD), lambda j, s: (0, KVH + key_head(j, s))),
                pl.BlockSpec((1, share, HD), own_head),
                pl.BlockSpec((1, share, HD), own_head),
            ],
            out_specs=out_specs,
            scratch_shapes=[pltpu.VMEM((CTX, cols), jnp.float32)],
        ),
        out_shape=out_shape,
        compiler_params=PARAMS,
        cost_estimate=small_cost(1 << 31),
        name="attend_open" if is_open else "attend",
    )(info, queries, keys, cache, *fresh)


def close_kernel(is_last, num_ref, stat_ref, *refs):
    in_refs, out_ref = refs[:-1], refs[-1]
    for b in range(out_ref.shape[1] // LANES):
        lanes = slice(b * LANES, (b + 1) * LANES)
        top, total, numerator = stat_ref[0, 0:1, lanes], stat_ref[0, 1:2, lanes], num_ref[0, :, lanes]
        parts = [decode(ref, lanes) for ref in in_refs]
        top, total, numerator = merged(top, total, numerator, parts)
        if not is_last:
            code_into(out_ref, lanes, top, total, numerator)
            continue
        numerator = numerator / total
        for h in range(LANES // ROWS):
            column = b * LANES + h * HD
            out_ref[:, column:column + HD] = (
                numerator[:, h * ROWS:(h + 1) * ROWS].T.astype(jnp.bfloat16)
            )


def close(opened, received, ranks, is_last=False):
    pieces, _, cols, _ = layout(ranks)
    rows, kind = (ROWS, jnp.bfloat16) if is_last else (HD + TAIL, jnp.int16)
    place = lambda j: (j, 0, 0)
    return pl.pallas_call(
        functools.partial(close_kernel, is_last),
        grid=(pieces,),
        in_specs=[pl.BlockSpec((1, HD, cols), place), pl.BlockSpec((1, 8, cols), place)]
        + [pl.BlockSpec((HD + TAIL, cols), lambda j: (0, j))] * len(received),
        out_specs=pl.BlockSpec((rows, cols), lambda j: (0, j)),
        out_shape=jax.ShapeDtypeStruct((rows, pieces * cols), kind),
        compiler_params=PARAMS,
        cost_estimate=small_cost(1 << 18),
        name="finish" if is_last else "close",
    )(*opened, *received)


def choose_kernel(sec_ref, *refs):
    count = (len(refs) - 2) // 2
    near, there_ref, out_refs, sems = refs[:count], refs[count], refs[count + 1:-1], refs[-1]
    first = sec_ref[0] == 0
    for k in range(count):
        @pl.when(first)
        def _():
            pltpu.make_async_copy(near[k], out_refs[k], sems.at[k]).start()

        @pl.when(jnp.logical_not(first))
        def _():
            pltpu.make_async_copy(there_ref.at[k], out_refs[k], sems.at[k]).start()

    for k in range(count):
        pltpu.make_async_copy(near[k], out_refs[k], sems.at[k]).wait()


def choose(sec, near, there):
    count = len(near)
    return pl.pallas_call(
        choose_kernel,
        in_specs=[pl.BlockSpec(memory_space=pltpu.SMEM)] + [pl.BlockSpec(memory_space=pl.ANY)] * (count + 1),
        out_specs=[pl.BlockSpec(memory_space=pltpu.VMEM)] * count,
        out_shape=[jax.ShapeDtypeStruct(there.shape[1:], there.dtype)] * count,
        scratch_shapes=[pltpu.SemaphoreType.DMA((count,))],
        compiler_params=SMALL_PARAMS,
        cost_estimate=small_cost(1 << 18),
        name="choose",
    )(sec.reshape(1), *near, there)


def stack_kernel(*refs):
    out_ref, sems = refs[-2:]
    copies = [
        pltpu.make_async_copy(ref, out_ref.at[k], sems.at[k]) for k, ref in enumerate(refs[:-2])
    ]
    for c in copies:
        c.start()
    for c in copies:
        c.wait()


def stack(values):
    count = len(values)
    return pl.pallas_call(
        stack_kernel,
        in_specs=[pl.BlockSpec(memory_space=pl.ANY)] * count,
        out_specs=pl.BlockSpec(memory_space=pltpu.VMEM),
        out_shape=jax.ShapeDtypeStruct((count,) + values[0].shape, values[0].dtype),
        scratch_shapes=[pltpu.SemaphoreType.DMA((count,))],
        compiler_params=SMALL_PARAMS,
        cost_estimate=small_cost(1 << 32),
        name="stack",
    )(*values)


def arrange_kernel(place_ref, kept_ref, crossed_ref, routed_ref, out_ref):
    count = crossed_ref.shape[0]
    shift = lax.rem(place_ref[1] - pl.program_id(0) + count + 1, count + 1)
    second = place_ref[0] > 0

    @pl.when(jnp.logical_not(second))
    def _():
        out_ref[...] = jnp.zeros_like(out_ref)

    @pl.when(jnp.logical_and(second, shift == 0))
    def _():
        out_ref[...] = kept_ref[...]

    @pl.when(jnp.logical_and(second, shift > 0))
    def _():
        out_ref[:, :, :KVW] = crossed_ref[shift - 1]
        out_ref[:, :, KVW:] = routed_ref[shift - 1]


def arrange(place, kept, crossed, routed):
    ranks = crossed.shape[0] + 1
    slots = kept.shape[0]
    return pl.pallas_call(
        arrange_kernel,
        grid=(ranks,),
        in_specs=[
            pl.BlockSpec(memory_space=pltpu.SMEM),
            pl.BlockSpec(kept.shape, lambda j: (0, 0, 0)),
            pl.BlockSpec(crossed.shape, lambda j: (0, 0, 0, 0)),
            pl.BlockSpec(routed.shape, lambda j: (0, 0, 0, 0)),
        ],
        out_specs=pl.BlockSpec((slots, PAGE, 2 * KVW), lambda j: (j, 0, 0)),
        out_shape=jax.ShapeDtypeStruct((ranks * slots, PAGE, 2 * KVW), jnp.bfloat16),
        compiler_params=PARAMS,
        cost_estimate=small_cost(1 << 18),
        name="arrange",
    )(place, kept, crossed, routed)


def after(value, earlier):
    return lax.optimization_barrier((value, earlier))[0]


def shards(queries, kv_cache, key_scale, fresh_input, kv_weight, lengths, page_list, owners):
    ranks = lax.axis_size("rank")
    secs = lax.axis_size("sec")
    me = lax.axis_index("rank").astype(jnp.int32)
    sec = lax.axis_index("sec").astype(jnp.int32)
    cache = kv_cache[0]
    length = lengths[0, 0]
    pieces, heads, _, _ = layout(ranks)

    def shifted(value, k):
        return lax.ppermute(value, "rank", [(i, (i + k) % ranks) for i in range(ranks)])

    def swapped(value, bit):
        return lax.ppermute(value, "rank", [(i, i ^ bit) for i in range(ranks)])

    def handed_on(value):
        return lax.ppermute(value, "sec", [(i, (i + 1) % secs) for i in range(secs)])

    part, (kept, *near), there = project(
        me, fresh_input[0], kv_weight, page_list, owners[:, 0], cache, ranks
    )
    fresh = [part[0]] + [shifted(part[k], k) for k in range(1, ranks)]

    q_tables = rope_tables(after(length, part) + jnp.arange(ROWS, dtype=jnp.int32))
    k_tables = rope_tables(after(me, part) * CTX + jnp.arange(CTX, dtype=jnp.int32))
    there = handed_on(there)
    kept = handed_on(kept)
    q_rot, keys = prepare(queries[0], cache, key_scale[None, :], q_tables, k_tables)
    chosen = choose(sec, near, after(there, q_rot))
    arrived = after(fresh, chosen)
    chosen = after(chosen, arrived)
    routed = [shifted(c, k + 1) for k, c in enumerate(chosen)]
    info = jnp.stack([length, me])
    fresh = gather(info, q_tables, arrived)

    def attend_to(code, earlier, is_open):
        return attend(info, code, after(q_rot, earlier), keys, cache, fresh, ranks, is_open)

    taken = {code: [] for code in range(ranks)}

    def send(value, code, bit):
        taken[code ^ bit].append(swapped(value, bit))

    last = chosen
    for code in range(ranks - 1, 1, -2):
        last = attend_to(code, last, False)
        send(last, code, 1)
    merging = {}
    for code in range(ranks - 2, 0, -2):
        last = merging[code] = attend_to(code, (last, kept), True)
    last = attend_to(1, last, False)
    send(last, 1, 1)
    both = stack(after(routed, last))
    bit = 2
    while bit < ranks:
        for code in range(ranks - bit, 0, -2 * bit):
            last = close(after(merging[code], both), taken[code], ranks)
            send(last, code, bit)
        bit *= 2
    crossed = handed_on(both)
    own = attend_to(0, last, True)

    handed = arrange(jnp.stack([sec, me]), kept, crossed, both)[None]
    attended = close(own, taken[0], ranks, is_last=True)[None]
    return (attended, handed)


def solution(mesh):
    return jax.shard_map(
        shards,
        mesh=mesh,
        in_specs=(
            P(("sec", "grp"), None, None),
            P(("sec", "grp"), "rank", None),
            P(),
            P(("sec", "grp"), None, "rank"),
            P("rank", None),
            P(("sec", "grp"), None),
            P(("sec", "grp", "rank")),
            P(("sec", "grp", "rank"), None),
        ),
        out_specs=(P(("sec", "grp"), None, "rank"), P(("sec", "grp", "rank"), None, None, None)),
        check_vma=False,
    )
```

```python
import functools
import math

import jax
import jax.numpy as jnp
import numpy as np
from jax import lax
from jax.experimental import pallas as pl
from jax.experimental.pallas import tpu as pltpu
from jax.sharding import PartitionSpec as P

HEADS = 64
KVH = 8
HD = 128
ROWS = 128
CTX = 1024
PAGE = 16
GQ = 8
KVW = 1024

ROPE_BASE = 500000.0
NEG_FILL = -1e30
LOW = -1e29
TINY = 1.2e-38
NO_LEVEL = -16000.0
LEVELS = 32767.0
SCALE = 1.0 / math.sqrt(HD)
EXP2_SCALE = SCALE * math.log2(math.e)
LANES = 256
KEYS = 512
DEPTH = 512
TAIL = 8
CONTRACT_FIRST = (((0,), (0,)), ((), ()))
CONTRACT_LAST = (((1,), (1,)), ((), ()))
PARAMS = pltpu.CompilerParams(vmem_limit_bytes=60 << 20)
SMALL_PARAMS = pltpu.CompilerParams(vmem_limit_bytes=40 << 20)


def small_cost(flops):
    return pl.CostEstimate(flops=flops, bytes_accessed=1 << 16, transcendentals=0)


def inverse_frequencies():
    steps = np.arange(HD // 2, dtype=np.float32) * np.float32(-2.0 * math.log(ROPE_BASE) / HD)
    return np.exp(steps.astype(np.float64)).astype(np.float32)


def rope_tables(positions):
    inverse = jnp.asarray(np.tile(inverse_frequencies(), 2))
    sign = np.repeat(np.array([-1.0, 1.0], np.float32), HD // 2)
    angles = positions.astype(jnp.float32)[:, None] * inverse[None, :]
    return jnp.cos(angles), jnp.sin(angles) * sign[None, :]


def rotated(values, cosine, signed_sine):
    return values * cosine + pltpu.roll(values, HD // 2, 1) * signed_sine


def project_kernel(ranks, rank_ref, x_ref, w_ref, page_ref, owner_ref, cache_ref, *refs):
    out_refs, page_refs, there_ref = refs[:ranks], refs[ranks:2 * ranks], refs[2 * ranks]
    weight, total, sems, counts, page_sems = refs[2 * ranks + 1:]
    entries = page_ref.shape[0]
    share = out_refs[0].shape[0]
    chunks = weight.shape[0]

    def weight_copy(j):
        rows = pl.ds(j * weight.shape[1], weight.shape[1])
        return pltpu.make_async_copy(w_ref.at[rows, :], weight.at[j], sems.at[j])

    def page_rows(e):
        return pl.ds(pl.multiple_of(page_ref[e] * PAGE, PAGE), PAGE)

    def kept(e, slot):
        return pltpu.make_async_copy(cache_ref.at[page_rows(e), :], page_refs[0].at[slot], page_sems.at[e])

    def near(e, k, slot):
        source = cache_ref.at[page_rows(e), pl.ds(0, KVW)]
        return pltpu.make_async_copy(source, page_refs[k].at[slot], page_sems.at[e])

    def far(e, k, slot):
        source = cache_ref.at[page_rows(e), pl.ds(KVW, KVW)]
        return pltpu.make_async_copy(source, there_ref.at[k - 1, slot], page_sems.at[e])

    for j in range(chunks):
        weight_copy(j).start()
    for ref in [*page_refs, there_ref]:
        ref[...] = jnp.zeros_like(ref)
    for r in range(ranks):
        counts[r] = 0

    def begin(e, carry):
        owner = owner_ref[e]
        slot = counts[owner]
        counts[owner] = slot + 1
        place = lax.rem(owner - rank_ref[0] + ranks, ranks)

        @pl.when(place == 0)
        def _():
            kept(e, slot).start()

        for k in range(1, ranks):
            @pl.when(place == k)
            def _():
                near(e, k, slot).start()
                far(e, k, slot).start()
        return carry

    lax.fori_loop(0, entries, begin, 0)
    for j in range(chunks):
        weight_copy(j).wait()
        depth = weight.shape[1]
        part = jnp.dot(
            x_ref[:, j * depth:(j + 1) * depth], weight[j], preferred_element_type=jnp.float32
        )
        if j:
            part = part + total[...]
        total[...] = part
    for k in range(ranks):
        dest = lax.rem(rank_ref[0] + k, ranks)
        out_refs[k][...] = total[pl.ds(pl.multiple_of(dest * share, share), share), :]

    def end(e, carry):
        kept(e, 0).wait()
        return carry

    lax.fori_loop(0, entries, end, 0)


def project(me, x, weight, page_list, owner_ids, cache, ranks):
    share = ROWS // ranks
    depth = weight.shape[0]
    block = min(depth, DEPTH)
    entries = page_list.shape[0]
    slots = 2 * entries // ranks
    smem = pl.BlockSpec(memory_space=pltpu.SMEM)
    vmem = pl.BlockSpec(memory_space=pltpu.VMEM)
    anywhere = pl.BlockSpec(memory_space=pl.ANY)
    out_shape = [jax.ShapeDtypeStruct((share, 2 * KVW), jnp.float32)] * ranks
    out_shape += [jax.ShapeDtypeStruct((slots, PAGE, 2 * KVW), jnp.bfloat16)]
    out_shape += [jax.ShapeDtypeStruct((slots, PAGE, KVW), jnp.bfloat16)] * (ranks - 1)
    out_shape += [jax.ShapeDtypeStruct((ranks - 1, slots, PAGE, KVW), jnp.bfloat16)]
    out = pl.pallas_call(
        functools.partial(project_kernel, ranks),
        in_specs=[smem, vmem, anywhere, smem, smem, anywhere],
        out_specs=[vmem] * len(out_shape),
        out_shape=out_shape,
        scratch_shapes=[
            pltpu.VMEM((depth // block, block, 2 * KVW), jnp.bfloat16),
            pltpu.VMEM((ROWS, 2 * KVW), jnp.float32),
            pltpu.SemaphoreType.DMA((depth // block,)),
            pltpu.SMEM((ranks,), jnp.int32),
            pltpu.SemaphoreType.DMA((entries,)),
        ],
        compiler_params=PARAMS,
        cost_estimate=small_cost(1 << 20),
        name="project",
    )(me.reshape(1), x, weight, page_list, owner_ids, cache)
    return out[:ranks], out[ranks:2 * ranks], out[2 * ranks]


def prepare_kernel(q_ref, k_ref, scale_ref, qc_ref, qs_ref, kc_ref, ks_ref, q_out, k_out):
    for g in range(GQ):
        q = rotated(q_ref[:, g * HD:(g + 1) * HD].astype(jnp.float32), qc_ref[...], qs_ref[...])
        q_out[g * ROWS:(g + 1) * ROWS, :] = q.astype(jnp.bfloat16)
    for h in range(KVH):
        columns = slice(h * HD, (h + 1) * HD)
        key = k_ref[:, columns].astype(jnp.float32) * scale_ref[:, columns]
        k_out[h] = rotated(key, kc_ref[...], ks_ref[...]).astype(jnp.bfloat16)


def prepare(queries, cache, key_scale, q_tables, k_tables):
    fixed = lambda j: (0, 0)
    rows = CTX // KVH
    return pl.pallas_call(
        prepare_kernel,
        grid=(KVH,),
        in_specs=[
            pl.BlockSpec((ROWS, GQ * HD), lambda j: (0, j)),
            pl.BlockSpec((rows, KVW), lambda j: (j, 0)),
            pl.BlockSpec((1, KVW), fixed),
            pl.BlockSpec((ROWS, HD), fixed),
            pl.BlockSpec((ROWS, HD), fixed),
            pl.BlockSpec((rows, HD), lambda j: (j, 0)),
            pl.BlockSpec((rows, HD), lambda j: (j, 0)),
        ],
        out_specs=[
            pl.BlockSpec((GQ * ROWS, HD), lambda j: (j, 0)),
            pl.BlockSpec((KVH, rows, HD), lambda j: (0, j, 0)),
        ],
        out_shape=[
            jax.ShapeDtypeStruct((HEADS * ROWS, HD), jnp.bfloat16),
            jax.ShapeDtypeStruct((KVH, CTX, HD), jnp.bfloat16),
        ],
        compiler_params=PARAMS,
        cost_estimate=small_cost(1 << 30),
        name="prepare",
    )(queries, cache, key_scale, *q_tables, *k_tables)


def split_level(level):
    doubled = jnp.maximum(level, NO_LEVEL) * 2.0
    high = jnp.floor(doubled)
    return [high, (doubled - high) * 65536.0 - 32768.0]


def joined_level(high, low):
    return (high + (low + 32768.0) * (1.0 / 65536.0)) * 0.5


def code_into(out_ref, lanes, top, total, numerator):
    largest = jnp.maximum(jnp.max(jnp.abs(numerator), axis=0, keepdims=True), TINY)
    coded = jnp.round(numerator * (1.0 / largest) * LEVELS)
    out_ref[:HD, lanes] = coded.astype(jnp.int32).astype(jnp.int16)
    tail = split_level(top + jnp.log2(largest)) + split_level(top + jnp.log2(total))
    tail = jnp.concatenate(tail + [jnp.zeros((TAIL - 4, top.shape[1]), jnp.float32)], axis=0)
    out_ref[HD:, lanes] = tail.astype(jnp.int32).astype(jnp.int16)


def decode(ref, lanes):
    tail = ref[HD:, lanes].astype(jnp.int32).astype(jnp.float32)
    values = ref[:HD, lanes].astype(jnp.int32).astype(jnp.float32)
    return joined_level(tail[0:1], tail[1:2]), joined_level(tail[2:3], tail[3:4]), values


def merged(top, total, numerator, parts):
    peak = functools.reduce(jnp.maximum, [p[1] for p in parts], top)
    if total is not None:
        factor = jnp.exp2(top - peak)
        total, numerator = total * factor, numerator * factor
    for level, weight, values in parts:
        more = jnp.exp2(weight - peak)
        part = values * (jnp.exp2(level - peak) * (1.0 / LEVELS))
        total = more if total is None else total + more
        numerator = part if numerator is None else numerator + part
    return peak, total, numerator


def fold_rows(values, combine):
    rows, cols = values.shape
    return combine(values.reshape(rows // 8, 8, cols), axis=0)


def gather_kernel(ranks, info, qc_ref, qs_ref, *refs):
    key_out, value_out = refs[ranks:]
    share = refs[0].shape[0]
    mine = pl.ds(pl.multiple_of(info[1] * share, share), share)
    cosine, signed_sine = qc_ref[mine, :], qs_ref[mine, :]
    for h in range(KVH):
        columns = slice(h * HD, (h + 1) * HD)
        key = sum(ref[:, columns] for ref in refs[:ranks])
        key = key.astype(jnp.bfloat16).astype(jnp.float32)
        key_out[h] = rotated(key, cosine, signed_sine).astype(jnp.bfloat16)
        columns = slice(KVW + h * HD, KVW + (h + 1) * HD)
        value_out[h] = sum(ref[:, columns] for ref in refs[:ranks]).astype(jnp.bfloat16)


def gather(info, q_tables, fresh):
    share = fresh[0].shape[0]
    vmem = pl.BlockSpec(memory_space=pltpu.VMEM)
    return pl.pallas_call(
        functools.partial(gather_kernel, len(fresh)),
        in_specs=[pl.BlockSpec(memory_space=pltpu.SMEM)] + [vmem] * (2 + len(fresh)),
        out_specs=[vmem] * 2,
        out_shape=[jax.ShapeDtypeStruct((KVH, share, HD), jnp.bfloat16)] * 2,
        compiler_params=PARAMS,
        cost_estimate=small_cost(1 << 18),
        name="gather",
    )(info, *q_tables, *fresh)


def attend_kernel(is_open, deps, info, q_ref, k_ref, v_ref, fk_ref, fv_ref, *refs):
    refs = refs[deps:]
    if is_open:
        num_ref, stat_ref, scores = refs
    else:
        out_ref, scores = refs
    rank = info[1]
    share = fk_ref.shape[1]
    valid = info[0] - rank * CTX
    first = rank * share
    fresh_key, fresh_value = fk_ref[0], fv_ref[0]
    cols = q_ref.shape[0]
    queries = q_ref[...]
    key_id = first + lax.broadcasted_iota(jnp.int32, (share, cols), 0)
    row_id = lax.broadcasted_iota(jnp.int32, (share, cols), 1) % ROWS
    fs = lax.dot_general(fresh_key, queries, CONTRACT_LAST, preferred_element_type=jnp.float32)
    fs = jnp.where(key_id <= row_id, fs, NEG_FILL)
    peak = fold_rows(fs, jnp.max)
    for t in range(CTX // KEYS):
        rows = slice(t * KEYS, (t + 1) * KEYS)
        s = lax.dot_general(
            k_ref[0, rows, :], queries, CONTRACT_LAST, preferred_element_type=jnp.float32
        )
        position = t * KEYS + lax.broadcasted_iota(jnp.int32, (KEYS, cols), 0)
        s = jnp.where(position < valid, s, NEG_FILL)
        scores[rows, :] = s
        peak = jnp.maximum(peak, fold_rows(s, jnp.max))
    peak = jnp.max(peak, axis=0, keepdims=True)
    base = jnp.maximum(peak, LOW)
    w = jnp.exp((fs - base) * SCALE)
    total = fold_rows(w, jnp.sum)
    numerator = lax.dot_general(
        fresh_value, w.astype(jnp.bfloat16), CONTRACT_FIRST, preferred_element_type=jnp.float32
    )
    for t in range(CTX // KEYS):
        rows = slice(t * KEYS, (t + 1) * KEYS)
        w = jnp.exp((scores[rows, :] - base) * SCALE)
        total = total + fold_rows(w, jnp.sum)
        numerator = numerator + lax.dot_general(
            v_ref[rows, :], w.astype(jnp.bfloat16), CONTRACT_FIRST, preferred_element_type=jnp.float32
        )
    total = jnp.sum(total, axis=0, keepdims=True)
    top = jnp.maximum(peak * EXP2_SCALE, NO_LEVEL)
    if is_open:
        num_ref[0] = numerator
        stat_ref[0] = jnp.concatenate([top, total, jnp.zeros((6, cols), jnp.float32)], axis=0)
    else:
        code_into(out_ref, slice(0, cols), top, total, numerator)


def layout(ranks):
    heads_here = HEADS // ranks
    pieces = max(1, heads_here // GQ)
    heads = heads_here // pieces
    return pieces, heads, heads * ROWS, ROWS // ranks


def whole(j, s):
    return (0, 0)


def opened_specs(cols):
    place = lambda j, s: (j, 0, 0)
    return [pl.BlockSpec((1, HD, cols), place), pl.BlockSpec((1, 8, cols), place)]


def attend(info, code, queries, keys, cache, fresh, earlier, ranks, is_open):
    pieces, heads, cols, share = layout(ranks)

    def piece(j, s):
        return (s[1] ^ code) * pieces + j

    def key_head(j, s):
        return piece(j, s) * heads // GQ

    if is_open:
        out_specs = opened_specs(cols)
        out_shape = [
            jax.ShapeDtypeStruct((pieces, HD, cols), jnp.float32),
            jax.ShapeDtypeStruct((pieces, 8, cols), jnp.float32),
        ]
    else:
        out_specs = pl.BlockSpec((HD + TAIL, cols), lambda j, s: (0, j))
        out_shape = jax.ShapeDtypeStruct((HD + TAIL, pieces * cols), jnp.int16)
    own_head = lambda j, s: (key_head(j, s), 0, 0)
    return pl.pallas_call(
        functools.partial(attend_kernel, is_open, len(earlier)),
        grid_spec=pltpu.PrefetchScalarGridSpec(
            num_scalar_prefetch=1,
            grid=(pieces,),
            in_specs=[
                pl.BlockSpec((cols, HD), lambda j, s: (piece(j, s), 0)),
                pl.BlockSpec((1, CTX, HD), own_head),
                pl.BlockSpec((CTX, HD), lambda j, s: (0, KVH + key_head(j, s))),
                pl.BlockSpec((1, share, HD), own_head),
                pl.BlockSpec((1, share, HD), own_head),
            ]
            + [pl.BlockSpec(memory_space=pl.ANY)] * len(earlier),
            out_specs=out_specs,
            scratch_shapes=[pltpu.VMEM((CTX, cols), jnp.float32)],
        ),
        out_shape=out_shape,
        compiler_params=PARAMS,
        cost_estimate=small_cost(1 << 28),
        name="attend_open" if is_open else "attend",
    )(info, queries, keys, cache, *fresh, *earlier)


def close_kernel(is_last, count, num_ref, stat_ref, *refs):
    in_refs, out_ref = refs[:count], refs[-1]
    for b in range(out_ref.shape[1] // LANES):
        lanes = slice(b * LANES, (b + 1) * LANES)
        top, total, numerator = stat_ref[0, 0:1, lanes], stat_ref[0, 1:2, lanes], num_ref[0, :, lanes]
        parts = [decode(ref, lanes) for ref in in_refs]
        top, total, numerator = merged(top, total, numerator, parts)
        if not is_last:
            code_into(out_ref, lanes, top, total, numerator)
            continue
        numerator = numerator / total
        for h in range(LANES // ROWS):
            column = b * LANES + h * HD
            out_ref[:, column:column + HD] = (
                numerator[:, h * ROWS:(h + 1) * ROWS].T.astype(jnp.bfloat16)
            )


def close(opened, received, earlier, ranks, is_last=False):
    pieces, _, cols, _ = layout(ranks)
    rows, kind = (ROWS, jnp.bfloat16) if is_last else (HD + TAIL, jnp.int16)
    place = lambda j: (j, 0, 0)
    return pl.pallas_call(
        functools.partial(close_kernel, is_last, len(received)),
        grid=(pieces,),
        in_specs=[pl.BlockSpec((1, HD, cols), place), pl.BlockSpec((1, 8, cols), place)]
        + [pl.BlockSpec((HD + TAIL, cols), lambda j: (0, j))] * len(received)
        + [pl.BlockSpec(memory_space=pl.ANY)] * len(earlier),
        out_specs=pl.BlockSpec((rows, cols), lambda j: (0, j)),
        out_shape=jax.ShapeDtypeStruct((rows, pieces * cols), kind),
        compiler_params=SMALL_PARAMS,
        cost_estimate=small_cost(1 << 18),
        name="finish" if is_last else "close",
    )(*opened, *received, *earlier)


def choose_kernel(sec_ref, *refs):
    count = (len(refs) - 2) // 2
    near, there_ref, out_refs, sems = refs[:count], refs[count], refs[count + 1:-1], refs[-1]
    first = sec_ref[0] == 0
    for k in range(count):
        @pl.when(first)
        def _():
            pltpu.make_async_copy(near[k], out_refs[k], sems.at[k]).start()

        @pl.when(jnp.logical_not(first))
        def _():
            pltpu.make_async_copy(there_ref.at[k], out_refs[k], sems.at[k]).start()

    for k in range(count):
        pltpu.make_async_copy(near[k], out_refs[k], sems.at[k]).wait()


def choose(sec, near, there):
    count = len(near)
    return pl.pallas_call(
        choose_kernel,
        in_specs=[pl.BlockSpec(memory_space=pltpu.SMEM)] + [pl.BlockSpec(memory_space=pl.ANY)] * (count + 1),
        out_specs=[pl.BlockSpec(memory_space=pltpu.VMEM)] * count,
        out_shape=[jax.ShapeDtypeStruct(there.shape[1:], there.dtype)] * count,
        scratch_shapes=[pltpu.SemaphoreType.DMA((count,))],
        compiler_params=SMALL_PARAMS,
        cost_estimate=small_cost(1 << 18),
        name="choose",
    )(sec.reshape(1), *near, there)


def stack_kernel(count, *refs):
    out_ref, token_ref, sems = refs[-3:]
    token_ref[...] = jnp.zeros_like(token_ref)
    copies = [
        pltpu.make_async_copy(ref, out_ref.at[k], sems.at[k]) for k, ref in enumerate(refs[:count])
    ]
    for c in copies:
        c.start()
    for c in copies:
        c.wait()


def stack(values, earlier):
    count = len(values)
    return pl.pallas_call(
        functools.partial(stack_kernel, count),
        in_specs=[pl.BlockSpec(memory_space=pl.ANY)] * (count + len(earlier)),
        out_specs=[pl.BlockSpec(memory_space=pltpu.VMEM)] * 2,
        out_shape=[
            jax.ShapeDtypeStruct((count,) + values[0].shape, values[0].dtype),
            jax.ShapeDtypeStruct((8, 128), jnp.float32),
        ],
        scratch_shapes=[pltpu.SemaphoreType.DMA((count,))],
        compiler_params=SMALL_PARAMS,
        cost_estimate=small_cost(1 << 32),
        name="stack",
    )(*values, *earlier)


def arrange_kernel(place_ref, kept_ref, crossed_ref, routed_ref, out_ref):
    count = crossed_ref.shape[0]
    shift = lax.rem(place_ref[1] - pl.program_id(0) + count + 1, count + 1)
    second = place_ref[0] > 0

    @pl.when(jnp.logical_not(second))
    def _():
        out_ref[...] = jnp.zeros_like(out_ref)

    @pl.when(jnp.logical_and(second, shift == 0))
    def _():
        out_ref[...] = kept_ref[...]

    @pl.when(jnp.logical_and(second, shift > 0))
    def _():
        out_ref[:, :, :KVW] = crossed_ref[shift - 1]
        out_ref[:, :, KVW:] = routed_ref[shift - 1]


def arrange(place, kept, crossed, routed):
    ranks = crossed.shape[0] + 1
    slots = kept.shape[0]
    return pl.pallas_call(
        arrange_kernel,
        grid=(ranks,),
        in_specs=[
            pl.BlockSpec(memory_space=pltpu.SMEM),
            pl.BlockSpec(kept.shape, lambda j: (0, 0, 0)),
            pl.BlockSpec(crossed.shape, lambda j: (0, 0, 0, 0)),
            pl.BlockSpec(routed.shape, lambda j: (0, 0, 0, 0)),
        ],
        out_specs=pl.BlockSpec((slots, PAGE, 2 * KVW), lambda j: (j, 0, 0)),
        out_shape=jax.ShapeDtypeStruct((ranks * slots, PAGE, 2 * KVW), jnp.bfloat16),
        compiler_params=SMALL_PARAMS,
        cost_estimate=small_cost(1 << 18),
        name="arrange",
    )(place, kept, crossed, routed)


def after(value, earlier):
    return lax.optimization_barrier((value, earlier))[0]


def shards(queries, kv_cache, key_scale, fresh_input, kv_weight, lengths, page_list, owners):
    ranks = lax.axis_size("rank")
    secs = lax.axis_size("sec")
    me = lax.axis_index("rank").astype(jnp.int32)
    sec = lax.axis_index("sec").astype(jnp.int32)
    cache = kv_cache[0]
    length = lengths[0, 0]
    pieces, heads, _, _ = layout(ranks)

    def shifted(value, k):
        return lax.ppermute(value, "rank", [(i, (i + k) % ranks) for i in range(ranks)])

    def swapped(value, bit):
        return lax.ppermute(value, "rank", [(i, i ^ bit) for i in range(ranks)])

    def handed_on(value):
        return lax.ppermute(value, "sec", [(i, (i + 1) % secs) for i in range(secs)])

    part, (kept, *near), there = project(
        me, fresh_input[0], kv_weight, page_list, owners[:, 0], cache, ranks
    )
    fresh = [part[0]] + [shifted(part[k], k) for k in range(1, ranks)]

    q_tables = rope_tables(after(length, part) + jnp.arange(ROWS, dtype=jnp.int32))
    k_tables = rope_tables(after(me, part) * CTX + jnp.arange(CTX, dtype=jnp.int32))
    there = handed_on(there)
    info = jnp.stack([after(length, part), me])
    q_rot, keys = prepare(queries[0], cache, key_scale[None, :], q_tables, k_tables)
    chosen = choose(sec, near, after(there, q_rot))
    arrived = after(fresh, chosen)
    chosen, kept = after((chosen, kept), arrived)
    routed = [shifted(c, k + 1) for k, c in enumerate(chosen)]
    kept = handed_on(kept)
    fresh = gather(info, q_tables, arrived)

    def attend_to(code, earlier, is_open):
        return attend(info, code, q_rot, keys, cache, fresh, earlier, ranks, is_open)

    taken = {code: [] for code in range(ranks)}

    def send(value, code, bit):
        taken[code ^ bit].append(swapped(value, bit))

    last = chosen[:1]
    for code in range(ranks - 1, 1, -2):
        last = [attend_to(code, last, False)]
        send(last[0], code, 1)
    merging = {}
    for code in range(ranks - 2, 0, -2):
        merging[code] = attend_to(code, last, True)
        last = merging[code][1:]
    direct = attend_to(1, last, False)
    both, token = stack(routed, [kept, direct])
    bit = 2
    while bit < ranks:
        for code in range(ranks - bit, 0, -2 * bit):
            last = [close(merging[code], taken[code], [token], ranks)]
            send(last[0], code, bit)
        bit *= 2
    crossed = handed_on(both)
    own = attend_to(0, last, True)
    handed = arrange(jnp.stack([sec, me]), kept, crossed, both)
    taken[0].append(swapped(direct, 1))
    attended = close(own, taken[0], [handed], ranks, is_last=True)[None]
    return (attended, handed[None])


def solution(mesh):
    return jax.shard_map(
        shards,
        mesh=mesh,
        in_specs=(
            P(("sec", "grp"), None, None),
            P(("sec", "grp"), "rank", None),
            P(),
            P(("sec", "grp"), None, "rank"),
            P("rank", None),
            P(("sec", "grp"), None),
            P(("sec", "grp", "rank")),
            P(("sec", "grp", "rank"), None),
        ),
        out_specs=(P(("sec", "grp"), None, "rank"), P(("sec", "grp", "rank"), None, None, None)),
        check_vma=False,
    )
```

```python
import functools
import math

import jax
import jax.numpy as jnp
import numpy as np
from jax import lax
from jax.experimental import pallas as pl
from jax.experimental.pallas import tpu as pltpu
from jax.sharding import PartitionSpec as P

HEADS = 64
KVH = 8
HD = 128
ROWS = 128
CTX = 1024
PAGE = 16
GQ = 8
KVW = 1024

ROPE_BASE = 500000.0
NEG_FILL = -1e30
LOW = -1e29
TINY = 1.2e-38
NO_LEVEL = -16000.0
LEVELS = 32767.0
SCALE = 1.0 / math.sqrt(HD)
EXP2_SCALE = SCALE * math.log2(math.e)
LANES = 256
KEYS = 512
DEPTH = 512
TAIL = 8
CONTRACT_FIRST = (((0,), (0,)), ((), ()))
CONTRACT_LAST = (((1,), (1,)), ((), ()))
PARAMS = pltpu.CompilerParams(vmem_limit_bytes=60 << 20)
ATTEND_PARAMS = pltpu.CompilerParams(vmem_limit_bytes=32 << 20)
SMALL_PARAMS = pltpu.CompilerParams(vmem_limit_bytes=40 << 20)


def small_cost(flops):
    return pl.CostEstimate(flops=flops, bytes_accessed=1 << 16, transcendentals=0)


def inverse_frequencies():
    steps = np.arange(HD // 2, dtype=np.float32) * np.float32(-2.0 * math.log(ROPE_BASE) / HD)
    return np.exp(steps.astype(np.float64)).astype(np.float32)


def rope_tables(positions):
    inverse = jnp.asarray(np.tile(inverse_frequencies(), 2))
    sign = np.repeat(np.array([-1.0, 1.0], np.float32), HD // 2)
    angles = positions.astype(jnp.float32)[:, None] * inverse[None, :]
    return jnp.cos(angles), jnp.sin(angles) * sign[None, :]


def rotated(values, cosine, signed_sine):
    return values * cosine + pltpu.roll(values, HD // 2, 1) * signed_sine


def project_kernel(ranks, rank_ref, x_ref, w_ref, page_ref, owner_ref, cache_ref, *refs):
    out_refs, page_refs, there_ref = refs[:ranks], refs[ranks:2 * ranks], refs[2 * ranks]
    weight, total, sems, counts, page_sems = refs[2 * ranks + 1:]
    entries = page_ref.shape[0]
    share = out_refs[0].shape[0]
    chunks = weight.shape[0]

    def weight_copy(j):
        rows = pl.ds(j * weight.shape[1], weight.shape[1])
        return pltpu.make_async_copy(w_ref.at[rows, :], weight.at[j], sems.at[j])

    def page_rows(e):
        return pl.ds(pl.multiple_of(page_ref[e] * PAGE, PAGE), PAGE)

    def kept(e, slot):
        return pltpu.make_async_copy(cache_ref.at[page_rows(e), :], page_refs[0].at[slot], page_sems.at[e])

    def near(e, k, slot):
        source = cache_ref.at[page_rows(e), pl.ds(0, KVW)]
        return pltpu.make_async_copy(source, page_refs[k].at[slot], page_sems.at[e])

    def far(e, k, slot):
        source = cache_ref.at[page_rows(e), pl.ds(KVW, KVW)]
        return pltpu.make_async_copy(source, there_ref.at[k - 1, slot], page_sems.at[e])

    for j in range(chunks):
        weight_copy(j).start()
    for ref in [*page_refs, there_ref]:
        ref[...] = jnp.zeros_like(ref)
    for r in range(ranks):
        counts[r] = 0

    def begin(e, carry):
        owner = owner_ref[e]
        slot = counts[owner]
        counts[owner] = slot + 1
        place = lax.rem(owner - rank_ref[0] + ranks, ranks)

        @pl.when(place == 0)
        def _():
            kept(e, slot).start()

        for k in range(1, ranks):
            @pl.when(place == k)
            def _():
                near(e, k, slot).start()
                far(e, k, slot).start()
        return carry

    lax.fori_loop(0, entries, begin, 0)
    for j in range(chunks):
        weight_copy(j).wait()
        depth = weight.shape[1]
        part = jnp.dot(
            x_ref[:, j * depth:(j + 1) * depth], weight[j], preferred_element_type=jnp.float32
        )
        if j:
            part = part + total[...]
        total[...] = part
    for k in range(ranks):
        dest = lax.rem(rank_ref[0] + k, ranks)
        out_refs[k][...] = total[pl.ds(pl.multiple_of(dest * share, share), share), :]

    def end(e, carry):
        kept(e, 0).wait()
        return carry

    lax.fori_loop(0, entries, end, 0)


def project(me, x, weight, page_list, owner_ids, cache, ranks):
    share = ROWS // ranks
    depth = weight.shape[0]
    block = min(depth, DEPTH)
    entries = page_list.shape[0]
    slots = 2 * entries // ranks
    smem = pl.BlockSpec(memory_space=pltpu.SMEM)
    vmem = pl.BlockSpec(memory_space=pltpu.VMEM)
    anywhere = pl.BlockSpec(memory_space=pl.ANY)
    out_shape = [jax.ShapeDtypeStruct((share, 2 * KVW), jnp.float32)] * ranks
    out_shape += [jax.ShapeDtypeStruct((slots, PAGE, 2 * KVW), jnp.bfloat16)]
    out_shape += [jax.ShapeDtypeStruct((slots, PAGE, KVW), jnp.bfloat16)] * (ranks - 1)
    out_shape += [jax.ShapeDtypeStruct((ranks - 1, slots, PAGE, KVW), jnp.bfloat16)]
    out = pl.pallas_call(
        functools.partial(project_kernel, ranks),
        in_specs=[smem, vmem, anywhere, smem, smem, anywhere],
        out_specs=[vmem] * len(out_shape),
        out_shape=out_shape,
        scratch_shapes=[
            pltpu.VMEM((depth // block, block, 2 * KVW), jnp.bfloat16),
            pltpu.VMEM((ROWS, 2 * KVW), jnp.float32),
            pltpu.SemaphoreType.DMA((depth // block,)),
            pltpu.SMEM((ranks,), jnp.int32),
            pltpu.SemaphoreType.DMA((entries,)),
        ],
        compiler_params=PARAMS,
        cost_estimate=small_cost(1 << 20),
        name="project",
    )(me.reshape(1), x, weight, page_list, owner_ids, cache)
    return out[:ranks], out[ranks:2 * ranks], out[2 * ranks]


def prepare_kernel(q_ref, k_ref, scale_ref, qc_ref, qs_ref, kc_ref, ks_ref, q_out, k_out):
    for g in range(GQ):
        q = rotated(q_ref[:, g * HD:(g + 1) * HD].astype(jnp.float32), qc_ref[...], qs_ref[...])
        q_out[g * ROWS:(g + 1) * ROWS, :] = q.astype(jnp.bfloat16)
    for h in range(KVH):
        columns = slice(h * HD, (h + 1) * HD)
        key = k_ref[:, columns].astype(jnp.float32) * scale_ref[:, columns]
        k_out[h] = rotated(key, kc_ref[...], ks_ref[...]).astype(jnp.bfloat16)


def prepare(queries, cache, key_scale, q_tables, k_tables):
    fixed = lambda j: (0, 0)
    rows = CTX // KVH
    return pl.pallas_call(
        prepare_kernel,
        grid=(KVH,),
        in_specs=[
            pl.BlockSpec((ROWS, GQ * HD), lambda j: (0, j)),
            pl.BlockSpec((rows, KVW), lambda j: (j, 0)),
            pl.BlockSpec((1, KVW), fixed),
            pl.BlockSpec((ROWS, HD), fixed),
            pl.BlockSpec((ROWS, HD), fixed),
            pl.BlockSpec((rows, HD), lambda j: (j, 0)),
            pl.BlockSpec((rows, HD), lambda j: (j, 0)),
        ],
        out_specs=[
            pl.BlockSpec((GQ * ROWS, HD), lambda j: (j, 0)),
            pl.BlockSpec((KVH, rows, HD), lambda j: (0, j, 0)),
        ],
        out_shape=[
            jax.ShapeDtypeStruct((HEADS * ROWS, HD), jnp.bfloat16),
            jax.ShapeDtypeStruct((KVH, CTX, HD), jnp.bfloat16),
        ],
        compiler_params=ATTEND_PARAMS,
        cost_estimate=small_cost(1 << 30),
        name="prepare",
    )(queries, cache, key_scale, *q_tables, *k_tables)


def split_level(level):
    doubled = jnp.maximum(level, NO_LEVEL) * 2.0
    high = jnp.floor(doubled)
    return [high, (doubled - high) * 65536.0 - 32768.0]


def joined_level(high, low):
    return (high + (low + 32768.0) * (1.0 / 65536.0)) * 0.5


def code_into(out_ref, lanes, top, total, numerator):
    largest = jnp.maximum(jnp.max(jnp.abs(numerator), axis=0, keepdims=True), TINY)
    coded = jnp.round(numerator * (1.0 / largest) * LEVELS)
    out_ref[:HD, lanes] = coded.astype(jnp.int32).astype(jnp.int16)
    tail = split_level(top + jnp.log2(largest)) + split_level(top + jnp.log2(total))
    tail = jnp.concatenate(tail + [jnp.zeros((TAIL - 4, top.shape[1]), jnp.float32)], axis=0)
    out_ref[HD:, lanes] = tail.astype(jnp.int32).astype(jnp.int16)


def decode(ref, lanes):
    tail = ref[HD:, lanes].astype(jnp.int32).astype(jnp.float32)
    values = ref[:HD, lanes].astype(jnp.int32).astype(jnp.float32)
    return joined_level(tail[0:1], tail[1:2]), joined_level(tail[2:3], tail[3:4]), values


def merged(top, total, numerator, parts):
    peak = functools.reduce(jnp.maximum, [p[1] for p in parts], top)
    if total is not None:
        factor = jnp.exp2(top - peak)
        total, numerator = total * factor, numerator * factor
    for level, weight, values in parts:
        more = jnp.exp2(weight - peak)
        part = values * (jnp.exp2(level - peak) * (1.0 / LEVELS))
        total = more if total is None else total + more
        numerator = part if numerator is None else numerator + part
    return peak, total, numerator


def fold_rows(values, combine):
    rows, cols = values.shape
    return combine(values.reshape(rows // 8, 8, cols), axis=0)


def gather_kernel(ranks, rank_ref, qc_ref, qs_ref, *refs):
    key_out, value_out = refs[ranks:]
    share = refs[0].shape[0]
    mine = pl.ds(pl.multiple_of(rank_ref[0] * share, share), share)
    cosine, signed_sine = qc_ref[mine, :], qs_ref[mine, :]
    for h in range(KVH):
        columns = slice(h * HD, (h + 1) * HD)
        key = sum(ref[:, columns] for ref in refs[:ranks])
        key = key.astype(jnp.bfloat16).astype(jnp.float32)
        key_out[h] = rotated(key, cosine, signed_sine).astype(jnp.bfloat16)
        columns = slice(KVW + h * HD, KVW + (h + 1) * HD)
        value_out[h] = sum(ref[:, columns] for ref in refs[:ranks]).astype(jnp.bfloat16)


def gather(me, q_tables, fresh):
    share = fresh[0].shape[0]
    vmem = pl.BlockSpec(memory_space=pltpu.VMEM)
    return pl.pallas_call(
        functools.partial(gather_kernel, len(fresh)),
        in_specs=[pl.BlockSpec(memory_space=pltpu.SMEM)] + [vmem] * (2 + len(fresh)),
        out_specs=[vmem] * 2,
        out_shape=[jax.ShapeDtypeStruct((KVH, share, HD), jnp.bfloat16)] * 2,
        compiler_params=ATTEND_PARAMS,
        cost_estimate=small_cost(1 << 18),
        name="gather",
    )(me.reshape(1), *q_tables, *fresh)


def attend_kernel(is_open, deps, length_ref, rank_ref, q_ref, k_ref, v_ref, fk_ref, fv_ref, *refs):
    refs = refs[deps:]
    if is_open:
        num_ref, stat_ref, scores = refs
    else:
        out_ref, scores = refs
    rank = rank_ref[0]
    share = fk_ref.shape[1]
    valid = length_ref[0] - rank * CTX
    first = rank * share
    fresh_key, fresh_value = fk_ref[0], fv_ref[0]
    cols = q_ref.shape[0]
    queries = q_ref[...]
    key_id = first + lax.broadcasted_iota(jnp.int32, (share, cols), 0)
    row_id = lax.broadcasted_iota(jnp.int32, (share, cols), 1) % ROWS
    fs = lax.dot_general(fresh_key, queries, CONTRACT_LAST, preferred_element_type=jnp.float32)
    fs = jnp.where(key_id <= row_id, fs, NEG_FILL)
    peak = fold_rows(fs, jnp.max)
    for t in range(CTX // KEYS):
        rows = slice(t * KEYS, (t + 1) * KEYS)
        s = lax.dot_general(
            k_ref[0, rows, :], queries, CONTRACT_LAST, preferred_element_type=jnp.float32
        )
        position = t * KEYS + lax.broadcasted_iota(jnp.int32, (KEYS, cols), 0)
        s = jnp.where(position < valid, s, NEG_FILL)
        scores[rows, :] = s
        peak = jnp.maximum(peak, fold_rows(s, jnp.max))
    peak = jnp.max(peak, axis=0, keepdims=True)
    base = jnp.maximum(peak, LOW)
    w = jnp.exp((fs - base) * SCALE)
    total = fold_rows(w, jnp.sum)
    numerator = lax.dot_general(
        fresh_value, w.astype(jnp.bfloat16), CONTRACT_FIRST, preferred_element_type=jnp.float32
    )
    for t in range(CTX // KEYS):
        rows = slice(t * KEYS, (t + 1) * KEYS)
        w = jnp.exp((scores[rows, :] - base) * SCALE)
        total = total + fold_rows(w, jnp.sum)
        numerator = numerator + lax.dot_general(
            v_ref[rows, :], w.astype(jnp.bfloat16), CONTRACT_FIRST, preferred_element_type=jnp.float32
        )
    total = jnp.sum(total, axis=0, keepdims=True)
    top = jnp.maximum(peak * EXP2_SCALE, NO_LEVEL)
    if is_open:
        num_ref[0] = numerator
        stat_ref[0] = jnp.concatenate([top, total, jnp.zeros((6, cols), jnp.float32)], axis=0)
    else:
        code_into(out_ref, slice(0, cols), top, total, numerator)


def layout(ranks):
    heads_here = HEADS // ranks
    pieces = max(1, heads_here // GQ)
    heads = heads_here // pieces
    return pieces, heads, heads * ROWS, ROWS // ranks


def whole(j, s):
    return (0, 0)


def opened_specs(cols):
    place = lambda j, n, r: (j, 0, 0)
    return [pl.BlockSpec((1, HD, cols), place), pl.BlockSpec((1, 8, cols), place)]


def attend(length, me, code, queries, keys, cache, fresh, earlier, ranks, is_open):
    pieces, heads, cols, share = layout(ranks)

    def piece(j, rank_ref):
        return (rank_ref[0] ^ code) * pieces + j

    def key_head(j, rank_ref):
        return piece(j, rank_ref) * heads // GQ

    if is_open:
        out_specs = opened_specs(cols)
        out_shape = [
            jax.ShapeDtypeStruct((pieces, HD, cols), jnp.float32),
            jax.ShapeDtypeStruct((pieces, 8, cols), jnp.float32),
        ]
    else:
        out_specs = pl.BlockSpec((HD + TAIL, cols), lambda j, n, r: (0, j))
        out_shape = jax.ShapeDtypeStruct((HD + TAIL, pieces * cols), jnp.int16)
    own_head = lambda j, n, r: (key_head(j, r), 0, 0)
    return pl.pallas_call(
        functools.partial(attend_kernel, is_open, len(earlier)),
        grid_spec=pltpu.PrefetchScalarGridSpec(
            num_scalar_prefetch=2,
            grid=(pieces,),
            in_specs=[
                pl.BlockSpec((cols, HD), lambda j, n, r: (piece(j, r), 0)),
                pl.BlockSpec((1, CTX, HD), own_head),
                pl.BlockSpec((CTX, HD), lambda j, n, r: (0, KVH + key_head(j, r))),
                pl.BlockSpec((1, share, HD), own_head),
                pl.BlockSpec((1, share, HD), own_head),
            ]
            + [pl.BlockSpec(memory_space=pl.ANY)] * len(earlier),
            out_specs=out_specs,
            scratch_shapes=[pltpu.VMEM((CTX, cols), jnp.float32)],
        ),
        out_shape=out_shape,
        compiler_params=ATTEND_PARAMS,
        cost_estimate=small_cost(1 << 28),
        name="attend_open" if is_open else "attend",
    )(length, me, queries, keys, cache, *fresh, *earlier)


def close_kernel(is_last, count, num_ref, stat_ref, *refs):
    in_refs, out_ref = refs[:count], refs[-1]
    for b in range(out_ref.shape[1] // LANES):
        lanes = slice(b * LANES, (b + 1) * LANES)
        top, total, numerator = stat_ref[0, 0:1, lanes], stat_ref[0, 1:2, lanes], num_ref[0, :, lanes]
        parts = [decode(ref, lanes) for ref in in_refs]
        top, total, numerator = merged(top, total, numerator, parts)
        if not is_last:
            code_into(out_ref, lanes, top, total, numerator)
            continue
        numerator = numerator / total
        for h in range(LANES // ROWS):
            column = b * LANES + h * HD
            out_ref[:, column:column + HD] = (
                numerator[:, h * ROWS:(h + 1) * ROWS].T.astype(jnp.bfloat16)
            )


def close(opened, received, earlier, ranks, is_last=False):
    pieces, _, cols, _ = layout(ranks)
    rows, kind = (ROWS, jnp.bfloat16) if is_last else (HD + TAIL, jnp.int16)
    place = lambda j: (j, 0, 0)
    return pl.pallas_call(
        functools.partial(close_kernel, is_last, len(received)),
        grid=(pieces,),
        in_specs=[pl.BlockSpec((1, HD, cols), place), pl.BlockSpec((1, 8, cols), place)]
        + [pl.BlockSpec((HD + TAIL, cols), lambda j: (0, j))] * len(received)
        + [pl.BlockSpec(memory_space=pl.ANY)] * len(earlier),
        out_specs=pl.BlockSpec((rows, cols), lambda j: (0, j)),
        out_shape=jax.ShapeDtypeStruct((rows, pieces * cols), kind),
        compiler_params=SMALL_PARAMS,
        cost_estimate=small_cost(1 << 18),
        name="finish" if is_last else "close",
    )(*opened, *received, *earlier)


def choose_kernel(sec_ref, *refs):
    count = (len(refs) - 2) // 2
    near, there_ref, out_refs, sems = refs[:count], refs[count], refs[count + 1:-1], refs[-1]
    first = sec_ref[0] == 0
    for k in range(count):
        @pl.when(first)
        def _():
            pltpu.make_async_copy(near[k], out_refs[k], sems.at[k]).start()

        @pl.when(jnp.logical_not(first))
        def _():
            pltpu.make_async_copy(there_ref.at[k], out_refs[k], sems.at[k]).start()

    for k in range(count):
        pltpu.make_async_copy(near[k], out_refs[k], sems.at[k]).wait()


def choose(sec, near, there):
    count = len(near)
    return pl.pallas_call(
        choose_kernel,
        in_specs=[pl.BlockSpec(memory_space=pltpu.SMEM)] + [pl.BlockSpec(memory_space=pl.ANY)] * (count + 1),
        out_specs=[pl.BlockSpec(memory_space=pltpu.VMEM)] * count,
        out_shape=[jax.ShapeDtypeStruct(there.shape[1:], there.dtype)] * count,
        scratch_shapes=[pltpu.SemaphoreType.DMA((count,))],
        compiler_params=SMALL_PARAMS,
        cost_estimate=small_cost(1 << 18),
        name="choose",
    )(sec.reshape(1), *near, there)


def stack_kernel(count, *refs):
    out_ref, token_ref, sems = refs[-3:]
    token_ref[...] = jnp.zeros_like(token_ref)
    copies = [
        pltpu.make_async_copy(ref, out_ref.at[k], sems.at[k]) for k, ref in enumerate(refs[:count])
    ]
    for c in copies:
        c.start()
    for c in copies:
        c.wait()


def stack(values, earlier):
    count = len(values)
    return pl.pallas_call(
        functools.partial(stack_kernel, count),
        in_specs=[pl.BlockSpec(memory_space=pl.ANY)] * (count + len(earlier)),
        out_specs=[pl.BlockSpec(memory_space=pltpu.VMEM)] * 2,
        out_shape=[
            jax.ShapeDtypeStruct((count,) + values[0].shape, values[0].dtype),
            jax.ShapeDtypeStruct((8, 128), jnp.float32),
        ],
        scratch_shapes=[pltpu.SemaphoreType.DMA((count,))],
        compiler_params=SMALL_PARAMS,
        cost_estimate=small_cost(1 << 32),
        name="stack",
    )(*values, *earlier)


def arrange_kernel(sec_ref, rank_ref, kept_ref, crossed_ref, routed_ref, out_ref, token_ref):
    token_ref[...] = jnp.zeros_like(token_ref)
    count = crossed_ref.shape[0]
    shift = lax.rem(rank_ref[0] - pl.program_id(0) + count + 1, count + 1)
    second = sec_ref[0] > 0

    @pl.when(jnp.logical_not(second))
    def _():
        out_ref[...] = jnp.zeros_like(out_ref)

    @pl.when(jnp.logical_and(second, shift == 0))
    def _():
        out_ref[...] = kept_ref[...]

    @pl.when(jnp.logical_and(second, shift > 0))
    def _():
        out_ref[:, :, :KVW] = crossed_ref[shift - 1]
        out_ref[:, :, KVW:] = routed_ref[shift - 1]


def arrange(sec, me, kept, crossed, routed):
    ranks = crossed.shape[0] + 1
    slots = kept.shape[0]
    return pl.pallas_call(
        arrange_kernel,
        grid=(ranks,),
        in_specs=[
            pl.BlockSpec(memory_space=pltpu.SMEM),
            pl.BlockSpec(memory_space=pltpu.SMEM),
            pl.BlockSpec(kept.shape, lambda j: (0, 0, 0)),
            pl.BlockSpec(crossed.shape, lambda j: (0, 0, 0, 0)),
            pl.BlockSpec(routed.shape, lambda j: (0, 0, 0, 0)),
        ],
        out_specs=[
            pl.BlockSpec((slots, PAGE, 2 * KVW), lambda j: (j, 0, 0)),
            pl.BlockSpec((8, 128), lambda j: (0, 0)),
        ],
        out_shape=[
            jax.ShapeDtypeStruct((ranks * slots, PAGE, 2 * KVW), jnp.bfloat16),
            jax.ShapeDtypeStruct((8, 128), jnp.float32),
        ],
        compiler_params=PARAMS,
        cost_estimate=small_cost(1 << 18),
        name="arrange",
    )(sec.reshape(1), me.reshape(1), kept, crossed, routed)


def after(value, earlier):
    return lax.optimization_barrier((value, earlier))[0]


def shards(queries, kv_cache, key_scale, fresh_input, kv_weight, lengths, page_list, owners):
    ranks = lax.axis_size("rank")
    secs = lax.axis_size("sec")
    me = lax.axis_index("rank").astype(jnp.int32)
    sec = lax.axis_index("sec").astype(jnp.int32)
    cache = kv_cache[0]
    length = lengths[0, 0]
    pieces, heads, _, _ = layout(ranks)

    def shifted(value, k):
        return lax.ppermute(value, "rank", [(i, (i + k) % ranks) for i in range(ranks)])

    def swapped(value, bit):
        return lax.ppermute(value, "rank", [(i, i ^ bit) for i in range(ranks)])

    def handed_on(value):
        return lax.ppermute(value, "sec", [(i, (i + 1) % secs) for i in range(secs)])

    part, (kept, *near), there = project(
        me, fresh_input[0], kv_weight, page_list, owners[:, 0], cache, ranks
    )
    fresh = [part[0]] + [shifted(part[k], k) for k in range(1, ranks)]

    q_tables = rope_tables(after(length, part) + jnp.arange(ROWS, dtype=jnp.int32))
    k_tables = rope_tables(after(me, part) * CTX + jnp.arange(CTX, dtype=jnp.int32))
    there = handed_on(there)
    q_rot, keys = prepare(queries[0], cache, key_scale[None, :], q_tables, k_tables)
    chosen = choose(sec, near, after(there, q_rot))
    arrived = after(fresh, chosen)
    chosen = after(chosen, arrived)
    routed = [shifted(c, k + 1) for k, c in enumerate(chosen)]
    fresh = gather(me, q_tables, arrived)
    kept = handed_on(after(kept, fresh))

    def attend_to(code, earlier, is_open):
        return attend(
            lengths[0], me.reshape(1), code, q_rot, keys, cache, fresh, earlier, ranks, is_open
        )

    taken = {code: [] for code in range(ranks)}

    def send(value, code, bit):
        taken[code ^ bit].append(swapped(value, bit))

    last = chosen[:1]
    for code in range(ranks - 1, 1, -2):
        last = [attend_to(code, last, False)]
        send(last[0], code, 1)
    merging = {}
    for code in range(ranks - 2, 0, -2):
        merging[code] = attend_to(code, last, True)
        last = merging[code][1:]
    direct = attend_to(1, last, False)
    both, token = stack(routed, [kept, direct])
    bit = 2
    while bit < ranks:
        for code in range(ranks - bit, 0, -2 * bit):
            last = [close(merging[code], taken[code], [token], ranks)]
            send(last[0], code, bit)
        bit *= 2
    crossed = handed_on(both)
    own = attend_to(0, last, True)
    handed, token = arrange(sec, me, kept, crossed, both)
    taken[0].append(swapped(direct, 1))
    attended = close(own, taken[0], [token], ranks, is_last=True)[None]
    return (attended, handed[None])


def solution(mesh):
    return jax.shard_map(
        shards,
        mesh=mesh,
        in_specs=(
            P(("sec", "grp"), None, None),
            P(("sec", "grp"), "rank", None),
            P(),
            P(("sec", "grp"), None, "rank"),
            P("rank", None),
            P(("sec", "grp"), None),
            P(("sec", "grp", "rank")),
            P(("sec", "grp", "rank"), None),
        ),
        out_specs=(P(("sec", "grp"), None, "rank"), P(("sec", "grp", "rank"), None, None, None)),
        check_vma=False,
    )
```

```python
import functools
import math

import jax
import jax.numpy as jnp
import numpy as np
from jax import lax
from jax.experimental import pallas as pl
from jax.experimental.pallas import tpu as pltpu
from jax.sharding import PartitionSpec as P

HEADS = 64
KVH = 8
HD = 128
ROWS = 128
CTX = 1024
PAGE = 16
GQ = 8
KVW = 1024

ROPE_BASE = 500000.0
NEG_FILL = -1e30
LOW = -1e29
TINY = 1.2e-38
NO_LEVEL = -16000.0
LEVELS = 32767.0
SCALE = 1.0 / math.sqrt(HD)
EXP2_SCALE = SCALE * math.log2(math.e)
LANES = 256
KEYS = 512
DEPTH = 512
TAIL = 8
CONTRACT_FIRST = (((0,), (0,)), ((), ()))
CONTRACT_LAST = (((1,), (1,)), ((), ()))
PARAMS = pltpu.CompilerParams(vmem_limit_bytes=60 << 20)
ATTEND_PARAMS = pltpu.CompilerParams(vmem_limit_bytes=32 << 20)
SMALL_PARAMS = pltpu.CompilerParams(vmem_limit_bytes=40 << 20)


def small_cost(flops):
    return pl.CostEstimate(flops=flops, bytes_accessed=1 << 16, transcendentals=0)


def inverse_frequencies():
    steps = np.arange(HD // 2, dtype=np.float32) * np.float32(-2.0 * math.log(ROPE_BASE) / HD)
    return np.exp(steps.astype(np.float64)).astype(np.float32)


def rope_tables(positions):
    inverse = jnp.asarray(np.tile(inverse_frequencies(), 2))
    sign = np.repeat(np.array([-1.0, 1.0], np.float32), HD // 2)
    angles = positions.astype(jnp.float32)[:, None] * inverse[None, :]
    return jnp.cos(angles), jnp.sin(angles) * sign[None, :]


def rotated(values, cosine, signed_sine):
    return values * cosine + pltpu.roll(values, HD // 2, 1) * signed_sine


def project_kernel(ranks, rank_ref, x_ref, w_ref, page_ref, owner_ref, cache_ref, *refs):
    out_refs, page_refs, there_ref = refs[:ranks], refs[ranks:2 * ranks], refs[2 * ranks]
    weight, total, sems, counts, page_sems = refs[2 * ranks + 1:]
    entries = page_ref.shape[0]
    share = out_refs[0].shape[0]
    chunks = weight.shape[0]

    def weight_copy(j):
        rows = pl.ds(j * weight.shape[1], weight.shape[1])
        return pltpu.make_async_copy(w_ref.at[rows, :], weight.at[j], sems.at[j])

    def page_rows(e):
        return pl.ds(pl.multiple_of(page_ref[e] * PAGE, PAGE), PAGE)

    def kept(e, slot):
        return pltpu.make_async_copy(cache_ref.at[page_rows(e), :], page_refs[0].at[slot], page_sems.at[e])

    def near(e, k, slot):
        source = cache_ref.at[page_rows(e), pl.ds(0, KVW)]
        return pltpu.make_async_copy(source, page_refs[k].at[slot], page_sems.at[e])

    def far(e, k, slot):
        source = cache_ref.at[page_rows(e), pl.ds(KVW, KVW)]
        return pltpu.make_async_copy(source, there_ref.at[k - 1, slot], page_sems.at[e])

    for j in range(chunks):
        weight_copy(j).start()
    for ref in [*page_refs, there_ref]:
        ref[...] = jnp.zeros_like(ref)
    for r in range(ranks):
        counts[r] = 0

    def begin(e, carry):
        owner = owner_ref[e]
        slot = counts[owner]
        counts[owner] = slot + 1
        place = lax.rem(owner - rank_ref[0] + ranks, ranks)

        @pl.when(place == 0)
        def _():
            kept(e, slot).start()

        for k in range(1, ranks):
            @pl.when(place == k)
            def _():
                near(e, k, slot).start()
                far(e, k, slot).start()
        return carry

    lax.fori_loop(0, entries, begin, 0)
    for j in range(chunks):
        weight_copy(j).wait()
        depth = weight.shape[1]
        part = jnp.dot(
            x_ref[:, j * depth:(j + 1) * depth], weight[j], preferred_element_type=jnp.float32
        )
        if j:
            part = part + total[...]
        total[...] = part
    for k in range(ranks):
        dest = lax.rem(rank_ref[0] + k, ranks)
        out_refs[k][...] = total[pl.ds(pl.multiple_of(dest * share, share), share), :]

    def end(e, carry):
        kept(e, 0).wait()
        return carry

    lax.fori_loop(0, entries, end, 0)


def project(me, x, weight, page_list, owner_ids, cache, ranks):
    share = ROWS // ranks
    depth = weight.shape[0]
    block = min(depth, DEPTH)
    entries = page_list.shape[0]
    slots = 2 * entries // ranks
    smem = pl.BlockSpec(memory_space=pltpu.SMEM)
    vmem = pl.BlockSpec(memory_space=pltpu.VMEM)
    anywhere = pl.BlockSpec(memory_space=pl.ANY)
    out_shape = [jax.ShapeDtypeStruct((share, 2 * KVW), jnp.float32)] * ranks
    out_shape += [jax.ShapeDtypeStruct((slots, PAGE, 2 * KVW), jnp.bfloat16)]
    out_shape += [jax.ShapeDtypeStruct((slots, PAGE, KVW), jnp.bfloat16)] * (ranks - 1)
    out_shape += [jax.ShapeDtypeStruct((ranks - 1, slots, PAGE, KVW), jnp.bfloat16)]
    out = pl.pallas_call(
        functools.partial(project_kernel, ranks),
        in_specs=[smem, vmem, anywhere, smem, smem, anywhere],
        out_specs=[vmem] * len(out_shape),
        out_shape=out_shape,
        scratch_shapes=[
            pltpu.VMEM((depth // block, block, 2 * KVW), jnp.bfloat16),
            pltpu.VMEM((ROWS, 2 * KVW), jnp.float32),
            pltpu.SemaphoreType.DMA((depth // block,)),
            pltpu.SMEM((ranks,), jnp.int32),
            pltpu.SemaphoreType.DMA((entries,)),
        ],
        compiler_params=PARAMS,
        cost_estimate=small_cost(1 << 20),
        name="project",
    )(me.reshape(1), x, weight, page_list, owner_ids, cache)
    return out[:ranks], out[ranks:2 * ranks], out[2 * ranks]


def prepare_kernel(q_ref, k_ref, scale_ref, qc_ref, qs_ref, kc_ref, ks_ref, q_out, k_out):
    for g in range(GQ):
        q = rotated(q_ref[:, g * HD:(g + 1) * HD].astype(jnp.float32), qc_ref[...], qs_ref[...])
        q_out[g * ROWS:(g + 1) * ROWS, :] = q.astype(jnp.bfloat16)
    for h in range(KVH):
        columns = slice(h * HD, (h + 1) * HD)
        key = k_ref[:, columns].astype(jnp.float32) * scale_ref[:, columns]
        k_out[h] = rotated(key, kc_ref[...], ks_ref[...]).astype(jnp.bfloat16)


def prepare(queries, cache, key_scale, q_tables, k_tables):
    fixed = lambda j: (0, 0)
    rows = CTX // KVH
    return pl.pallas_call(
        prepare_kernel,
        grid=(KVH,),
        in_specs=[
            pl.BlockSpec((ROWS, GQ * HD), lambda j: (0, j)),
            pl.BlockSpec((rows, KVW), lambda j: (j, 0)),
            pl.BlockSpec((1, KVW), fixed),
            pl.BlockSpec((ROWS, HD), fixed),
            pl.BlockSpec((ROWS, HD), fixed),
            pl.BlockSpec((rows, HD), lambda j: (j, 0)),
            pl.BlockSpec((rows, HD), lambda j: (j, 0)),
        ],
        out_specs=[
            pl.BlockSpec((GQ * ROWS, HD), lambda j: (j, 0)),
            pl.BlockSpec((KVH, rows, HD), lambda j: (0, j, 0)),
        ],
        out_shape=[
            jax.ShapeDtypeStruct((HEADS * ROWS, HD), jnp.bfloat16),
            jax.ShapeDtypeStruct((KVH, CTX, HD), jnp.bfloat16),
        ],
        compiler_params=ATTEND_PARAMS,
        cost_estimate=small_cost(1 << 30),
        name="prepare",
    )(queries, cache, key_scale, *q_tables, *k_tables)


def split_level(level):
    doubled = jnp.maximum(level, NO_LEVEL) * 2.0
    high = jnp.floor(doubled)
    return [high, (doubled - high) * 65536.0 - 32768.0]


def joined_level(high, low):
    return (high + (low + 32768.0) * (1.0 / 65536.0)) * 0.5


def code_into(out_ref, lanes, top, total, numerator):
    largest = jnp.maximum(jnp.max(jnp.abs(numerator), axis=0, keepdims=True), TINY)
    coded = jnp.round(numerator * (1.0 / largest) * LEVELS)
    out_ref[:HD, lanes] = coded.astype(jnp.int32).astype(jnp.int16)
    tail = split_level(top + jnp.log2(largest)) + split_level(top + jnp.log2(total))
    tail = jnp.concatenate(tail + [jnp.zeros((TAIL - 4, top.shape[1]), jnp.float32)], axis=0)
    out_ref[HD:, lanes] = tail.astype(jnp.int32).astype(jnp.int16)


def decode(ref, lanes):
    tail = ref[HD:, lanes].astype(jnp.int32).astype(jnp.float32)
    values = ref[:HD, lanes].astype(jnp.int32).astype(jnp.float32)
    return joined_level(tail[0:1], tail[1:2]), joined_level(tail[2:3], tail[3:4]), values


def merged(top, total, numerator, parts):
    peak = functools.reduce(jnp.maximum, [p[1] for p in parts], top)
    if total is not None:
        factor = jnp.exp2(top - peak)
        total, numerator = total * factor, numerator * factor
    for level, weight, values in parts:
        more = jnp.exp2(weight - peak)
        part = values * (jnp.exp2(level - peak) * (1.0 / LEVELS))
        total = more if total is None else total + more
        numerator = part if numerator is None else numerator + part
    return peak, total, numerator


def fold_rows(values, combine):
    rows, cols = values.shape
    return combine(values.reshape(rows // 8, 8, cols), axis=0)


def gather_kernel(ranks, rank_ref, qc_ref, qs_ref, *refs):
    key_out, value_out = refs[ranks:]
    share = refs[0].shape[0]
    mine = pl.ds(pl.multiple_of(rank_ref[0] * share, share), share)
    cosine, signed_sine = qc_ref[mine, :], qs_ref[mine, :]
    for h in range(KVH):
        columns = slice(h * HD, (h + 1) * HD)
        key = sum(ref[:, columns] for ref in refs[:ranks])
        key = key.astype(jnp.bfloat16).astype(jnp.float32)
        key_out[h] = rotated(key, cosine, signed_sine).astype(jnp.bfloat16)
        columns = slice(KVW + h * HD, KVW + (h + 1) * HD)
        value_out[h] = sum(ref[:, columns] for ref in refs[:ranks]).astype(jnp.bfloat16)


def gather(me, q_tables, fresh):
    share = fresh[0].shape[0]
    vmem = pl.BlockSpec(memory_space=pltpu.VMEM)
    return pl.pallas_call(
        functools.partial(gather_kernel, len(fresh)),
        in_specs=[pl.BlockSpec(memory_space=pltpu.SMEM)] + [vmem] * (2 + len(fresh)),
        out_specs=[vmem] * 2,
        out_shape=[jax.ShapeDtypeStruct((KVH, share, HD), jnp.bfloat16)] * 2,
        compiler_params=ATTEND_PARAMS,
        cost_estimate=small_cost(1 << 18),
        name="gather",
    )(me.reshape(1), *q_tables, *fresh)


def attend_kernel(is_open, deps, length_ref, rank_ref, q_ref, k_ref, v_ref, fk_ref, fv_ref, *refs):
    refs = refs[deps:]
    if is_open:
        num_ref, stat_ref, scores = refs
    else:
        out_ref, scores = refs
    rank = rank_ref[0]
    share = fk_ref.shape[1]
    valid = length_ref[0] - rank * CTX
    first = rank * share
    fresh_key, fresh_value = fk_ref[0], fv_ref[0]
    cols = q_ref.shape[0]
    queries = q_ref[...]
    key_id = first + lax.broadcasted_iota(jnp.int32, (share, cols), 0)
    row_id = lax.broadcasted_iota(jnp.int32, (share, cols), 1) % ROWS
    fs = lax.dot_general(fresh_key, queries, CONTRACT_LAST, preferred_element_type=jnp.float32)
    fs = jnp.where(key_id <= row_id, fs, NEG_FILL)
    peak = fold_rows(fs, jnp.max)
    for t in range(CTX // KEYS):
        rows = slice(t * KEYS, (t + 1) * KEYS)
        s = lax.dot_general(
            k_ref[0, rows, :], queries, CONTRACT_LAST, preferred_element_type=jnp.float32
        )
        position = t * KEYS + lax.broadcasted_iota(jnp.int32, (KEYS, cols), 0)
        s = jnp.where(position < valid, s, NEG_FILL)
        scores[rows, :] = s
        peak = jnp.maximum(peak, fold_rows(s, jnp.max))
    peak = jnp.max(peak, axis=0, keepdims=True)
    base = jnp.maximum(peak, LOW)
    w = jnp.exp((fs - base) * SCALE)
    total = fold_rows(w, jnp.sum)
    numerator = lax.dot_general(
        fresh_value, w.astype(jnp.bfloat16), CONTRACT_FIRST, preferred_element_type=jnp.float32
    )
    for t in range(CTX // KEYS):
        rows = slice(t * KEYS, (t + 1) * KEYS)
        w = jnp.exp((scores[rows, :] - base) * SCALE)
        total = total + fold_rows(w, jnp.sum)
        numerator = numerator + lax.dot_general(
            v_ref[rows, :], w.astype(jnp.bfloat16), CONTRACT_FIRST, preferred_element_type=jnp.float32
        )
    total = jnp.sum(total, axis=0, keepdims=True)
    top = jnp.maximum(peak * EXP2_SCALE, NO_LEVEL)
    if is_open:
        num_ref[0] = numerator
        stat_ref[0] = jnp.concatenate([top, total, jnp.zeros((6, cols), jnp.float32)], axis=0)
    else:
        code_into(out_ref, slice(0, cols), top, total, numerator)


def layout(ranks):
    heads_here = HEADS // ranks
    pieces = max(1, heads_here // GQ)
    heads = heads_here // pieces
    return pieces, heads, heads * ROWS, ROWS // ranks


def whole(j, s):
    return (0, 0)


def opened_specs(cols):
    place = lambda j, n, r: (j, 0, 0)
    return [pl.BlockSpec((1, HD, cols), place), pl.BlockSpec((1, 8, cols), place)]


def attend(length, me, code, queries, keys, cache, fresh, earlier, ranks, is_open):
    pieces, heads, cols, share = layout(ranks)

    def piece(j, rank_ref):
        return (rank_ref[0] ^ code) * pieces + j

    def key_head(j, rank_ref):
        return piece(j, rank_ref) * heads // GQ

    if is_open:
        out_specs = opened_specs(cols)
        out_shape = [
            jax.ShapeDtypeStruct((pieces, HD, cols), jnp.float32),
            jax.ShapeDtypeStruct((pieces, 8, cols), jnp.float32),
        ]
    else:
        out_specs = pl.BlockSpec((HD + TAIL, cols), lambda j, n, r: (0, j))
        out_shape = jax.ShapeDtypeStruct((HD + TAIL, pieces * cols), jnp.int16)
    own_head = lambda j, n, r: (key_head(j, r), 0, 0)
    return pl.pallas_call(
        functools.partial(attend_kernel, is_open, len(earlier)),
        grid_spec=pltpu.PrefetchScalarGridSpec(
            num_scalar_prefetch=2,
            grid=(pieces,),
            in_specs=[
                pl.BlockSpec((cols, HD), lambda j, n, r: (piece(j, r), 0)),
                pl.BlockSpec((1, CTX, HD), own_head),
                pl.BlockSpec((CTX, HD), lambda j, n, r: (0, KVH + key_head(j, r))),
                pl.BlockSpec((1, share, HD), own_head),
                pl.BlockSpec((1, share, HD), own_head),
            ]
            + [pl.BlockSpec(memory_space=pl.ANY)] * len(earlier),
            out_specs=out_specs,
            scratch_shapes=[pltpu.VMEM((CTX, cols), jnp.float32)],
        ),
        out_shape=out_shape,
        compiler_params=ATTEND_PARAMS,
        cost_estimate=small_cost(1 << 28),
        name="attend_open" if is_open else "attend",
    )(length, me, queries, keys, cache, *fresh, *earlier)


def close_kernel(is_last, count, num_ref, stat_ref, *refs):
    in_refs, out_ref = refs[:count], refs[-1]
    for b in range(out_ref.shape[1] // LANES):
        lanes = slice(b * LANES, (b + 1) * LANES)
        top, total, numerator = stat_ref[0, 0:1, lanes], stat_ref[0, 1:2, lanes], num_ref[0, :, lanes]
        parts = [decode(ref, lanes) for ref in in_refs]
        top, total, numerator = merged(top, total, numerator, parts)
        if not is_last:
            code_into(out_ref, lanes, top, total, numerator)
            continue
        numerator = numerator / total
        for h in range(LANES // ROWS):
            column = b * LANES + h * HD
            out_ref[:, column:column + HD] = (
                numerator[:, h * ROWS:(h + 1) * ROWS].T.astype(jnp.bfloat16)
            )


def close(opened, received, earlier, ranks, is_last=False):
    pieces, _, cols, _ = layout(ranks)
    rows, kind = (ROWS, jnp.bfloat16) if is_last else (HD + TAIL, jnp.int16)
    place = lambda j: (j, 0, 0)
    return pl.pallas_call(
        functools.partial(close_kernel, is_last, len(received)),
        grid=(pieces,),
        in_specs=[pl.BlockSpec((1, HD, cols), place), pl.BlockSpec((1, 8, cols), place)]
        + [pl.BlockSpec((HD + TAIL, cols), lambda j: (0, j))] * len(received)
        + [pl.BlockSpec(memory_space=pl.ANY)] * len(earlier),
        out_specs=pl.BlockSpec((rows, cols), lambda j: (0, j)),
        out_shape=jax.ShapeDtypeStruct((rows, pieces * cols), kind),
        compiler_params=SMALL_PARAMS,
        cost_estimate=small_cost(1 << 18),
        name="finish" if is_last else "close",
    )(*opened, *received, *earlier)


def choose_kernel(sec_ref, *refs):
    count = (len(refs) - 2) // 2
    near, there_ref, out_refs, sems = refs[:count], refs[count], refs[count + 1:-1], refs[-1]
    first = sec_ref[0] == 0
    for k in range(count):
        @pl.when(first)
        def _():
            pltpu.make_async_copy(near[k], out_refs[k], sems.at[k]).start()

        @pl.when(jnp.logical_not(first))
        def _():
            pltpu.make_async_copy(there_ref.at[k], out_refs[k], sems.at[k]).start()

    for k in range(count):
        pltpu.make_async_copy(near[k], out_refs[k], sems.at[k]).wait()


def choose(sec, near, there):
    count = len(near)
    return pl.pallas_call(
        choose_kernel,
        in_specs=[pl.BlockSpec(memory_space=pltpu.SMEM)] + [pl.BlockSpec(memory_space=pl.ANY)] * (count + 1),
        out_specs=[pl.BlockSpec(memory_space=pltpu.VMEM)] * count,
        out_shape=[jax.ShapeDtypeStruct(there.shape[1:], there.dtype)] * count,
        scratch_shapes=[pltpu.SemaphoreType.DMA((count,))],
        compiler_params=SMALL_PARAMS,
        cost_estimate=small_cost(1 << 18),
        name="choose",
    )(sec.reshape(1), *near, there)


def stack_kernel(count, *refs):
    out_ref, token_ref, sems = refs[-3:]
    token_ref[...] = jnp.zeros_like(token_ref)
    copies = [
        pltpu.make_async_copy(ref, out_ref.at[k], sems.at[k]) for k, ref in enumerate(refs[:count])
    ]
    for c in copies:
        c.start()
    for c in copies:
        c.wait()


def stack(values, earlier):
    count = len(values)
    return pl.pallas_call(
        functools.partial(stack_kernel, count),
        in_specs=[pl.BlockSpec(memory_space=pl.ANY)] * (count + len(earlier)),
        out_specs=[pl.BlockSpec(memory_space=pltpu.VMEM)] * 2,
        out_shape=[
            jax.ShapeDtypeStruct((count,) + values[0].shape, values[0].dtype),
            jax.ShapeDtypeStruct((8, 128), jnp.float32),
        ],
        scratch_shapes=[pltpu.SemaphoreType.DMA((count,))],
        compiler_params=SMALL_PARAMS,
        cost_estimate=small_cost(1 << 32),
        name="stack",
    )(*values, *earlier)


def arrange_kernel(sec_ref, rank_ref, kept_ref, crossed_ref, routed_ref, out_ref):
    count = crossed_ref.shape[0]
    shift = lax.rem(rank_ref[0] - pl.program_id(0) + count + 1, count + 1)
    second = sec_ref[0] > 0

    @pl.when(jnp.logical_not(second))
    def _():
        out_ref[...] = jnp.zeros_like(out_ref)

    @pl.when(jnp.logical_and(second, shift == 0))
    def _():
        out_ref[...] = kept_ref[...]

    @pl.when(jnp.logical_and(second, shift > 0))
    def _():
        out_ref[:, :, :KVW] = crossed_ref[shift - 1]
        out_ref[:, :, KVW:] = routed_ref[shift - 1]


def arrange(sec, me, kept, crossed, routed):
    ranks = crossed.shape[0] + 1
    slots = kept.shape[0]
    return pl.pallas_call(
        arrange_kernel,
        grid=(ranks,),
        in_specs=[
            pl.BlockSpec(memory_space=pltpu.SMEM),
            pl.BlockSpec(memory_space=pltpu.SMEM),
            pl.BlockSpec(kept.shape, lambda j: (0, 0, 0)),
            pl.BlockSpec(crossed.shape, lambda j: (0, 0, 0, 0)),
            pl.BlockSpec(routed.shape, lambda j: (0, 0, 0, 0)),
        ],
        out_specs=pl.BlockSpec((slots, PAGE, 2 * KVW), lambda j: (j, 0, 0)),
        out_shape=jax.ShapeDtypeStruct((ranks * slots, PAGE, 2 * KVW), jnp.bfloat16),
        compiler_params=SMALL_PARAMS,
        cost_estimate=small_cost(1 << 18),
        name="arrange",
    )(sec.reshape(1), me.reshape(1), kept, crossed, routed)


def after(value, earlier):
    return lax.optimization_barrier((value, earlier))[0]


def shards(queries, kv_cache, key_scale, fresh_input, kv_weight, lengths, page_list, owners):
    ranks = lax.axis_size("rank")
    secs = lax.axis_size("sec")
    me = lax.axis_index("rank").astype(jnp.int32)
    sec = lax.axis_index("sec").astype(jnp.int32)
    cache = kv_cache[0]
    length = lengths[0, 0]
    pieces, heads, _, _ = layout(ranks)

    def shifted(value, k):
        return lax.ppermute(value, "rank", [(i, (i + k) % ranks) for i in range(ranks)])

    def swapped(value, bit):
        return lax.ppermute(value, "rank", [(i, i ^ bit) for i in range(ranks)])

    def handed_on(value):
        return lax.ppermute(value, "sec", [(i, (i + 1) % secs) for i in range(secs)])

    part, (kept, *near), there = project(
        me, fresh_input[0], kv_weight, page_list, owners[:, 0], cache, ranks
    )
    fresh = [part[0]] + [shifted(part[k], k) for k in range(1, ranks)]

    q_tables = rope_tables(after(length, part) + jnp.arange(ROWS, dtype=jnp.int32))
    k_tables = rope_tables(after(me, part) * CTX + jnp.arange(CTX, dtype=jnp.int32))
    there = handed_on(there)
    q_rot, keys = prepare(queries[0], cache, key_scale[None, :], q_tables, k_tables)
    chosen = choose(sec, near, after(there, q_rot))
    arrived = after(fresh, chosen)
    chosen = after(chosen, arrived)
    routed = [shifted(c, k + 1) for k, c in enumerate(chosen)]
    fresh = gather(me, q_tables, arrived)
    kept = handed_on(after(kept, fresh))

    def attend_to(code, earlier, is_open):
        return attend(
            lengths[0], me.reshape(1), code, q_rot, keys, cache, fresh, earlier, ranks, is_open
        )

    taken = {code: [] for code in range(ranks)}

    def send(value, code, bit):
        taken[code ^ bit].append(swapped(value, bit))

    last = chosen[:1]
    for code in range(ranks - 1, 1, -2):
        last = [attend_to(code, last, False)]
        send(last[0], code, 1)
    merging = {}
    for code in range(ranks - 2, 0, -2):
        merging[code] = attend_to(code, last, True)
        last = merging[code][1:]
    waiting = attend_to(1, last, True)
    both, token = stack(routed, [kept, waiting[1]])
    bit = 2
    while bit < ranks:
        for code in range(ranks - bit, 0, -2 * bit):
            last = [close(merging[code], taken[code], [token], ranks)]
            send(last[0], code, bit)
        bit *= 2
    direct = close(waiting, [], last, ranks)
    crossed = handed_on(both)
    own = attend_to(0, [direct], True)
    handed = arrange(sec, me, kept, crossed, both)
    taken[0].insert(0, swapped(direct, 1))
    attended = close(after(own, handed), taken[0], [], ranks, is_last=True)[None]
    return (attended, handed[None])


def solution(mesh):
    return jax.shard_map(
        shards,
        mesh=mesh,
        in_specs=(
            P(("sec", "grp"), None, None),
            P(("sec", "grp"), "rank", None),
            P(),
            P(("sec", "grp"), None, "rank"),
            P("rank", None),
            P(("sec", "grp"), None),
            P(("sec", "grp", "rank")),
            P(("sec", "grp", "rank"), None),
        ),
        out_specs=(P(("sec", "grp"), None, "rank"), P(("sec", "grp", "rank"), None, None, None)),
        check_vma=False,
    )
```

```python
import functools
import math

import jax
import jax.numpy as jnp
import numpy as np
from jax import lax
from jax.experimental import pallas as pl
from jax.experimental.pallas import tpu as pltpu
from jax.sharding import PartitionSpec as P

HEADS = 64
KVH = 8
HD = 128
ROWS = 128
CTX = 1024
PAGE = 16
GQ = 8
KVW = 1024

ROPE_BASE = 500000.0
NEG_FILL = -1e30
LOW = -1e29
TINY = 1.2e-38
NO_LEVEL = -16000.0
LEVELS = 32767.0
SCALE = 1.0 / math.sqrt(HD)
EXP2_SCALE = SCALE * math.log2(math.e)
LANES = 256
KEYS = 512
DEPTH = 512
TAIL = 8
CONTRACT_FIRST = (((0,), (0,)), ((), ()))
CONTRACT_LAST = (((1,), (1,)), ((), ()))
PARAMS = pltpu.CompilerParams(vmem_limit_bytes=60 << 20)
ATTEND_PARAMS = pltpu.CompilerParams(vmem_limit_bytes=32 << 20)
SMALL_PARAMS = pltpu.CompilerParams(vmem_limit_bytes=40 << 20)


def small_cost(flops):
    return pl.CostEstimate(flops=flops, bytes_accessed=1 << 16, transcendentals=0)


def inverse_frequencies():
    steps = np.arange(HD // 2, dtype=np.float32) * np.float32(-2.0 * math.log(ROPE_BASE) / HD)
    return np.exp(steps.astype(np.float64)).astype(np.float32)


def rope_tables(positions):
    inverse = jnp.asarray(np.tile(inverse_frequencies(), 2))
    sign = np.repeat(np.array([-1.0, 1.0], np.float32), HD // 2)
    angles = positions.astype(jnp.float32)[:, None] * inverse[None, :]
    return jnp.cos(angles), jnp.sin(angles) * sign[None, :]


def rotated(values, cosine, signed_sine):
    return values * cosine + pltpu.roll(values, HD // 2, 1) * signed_sine


def project_kernel(ranks, rank_ref, x_ref, w_ref, page_ref, owner_ref, cache_ref, *refs):
    out_refs, page_refs, there_ref = refs[:ranks], refs[ranks:2 * ranks], refs[2 * ranks]
    weight, total, sems, counts, page_sems = refs[2 * ranks + 1:]
    entries = page_ref.shape[0]
    share = out_refs[0].shape[0]
    chunks = weight.shape[0]

    def weight_copy(j):
        rows = pl.ds(j * weight.shape[1], weight.shape[1])
        return pltpu.make_async_copy(w_ref.at[rows, :], weight.at[j], sems.at[j])

    def page_rows(e):
        return pl.ds(pl.multiple_of(page_ref[e] * PAGE, PAGE), PAGE)

    def kept(e, slot):
        return pltpu.make_async_copy(cache_ref.at[page_rows(e), :], page_refs[0].at[slot], page_sems.at[e])

    def near(e, k, slot):
        source = cache_ref.at[page_rows(e), pl.ds(0, KVW)]
        return pltpu.make_async_copy(source, page_refs[k].at[slot], page_sems.at[e])

    def far(e, k, slot):
        source = cache_ref.at[page_rows(e), pl.ds(KVW, KVW)]
        return pltpu.make_async_copy(source, there_ref.at[k - 1, slot], page_sems.at[e])

    for j in range(chunks):
        weight_copy(j).start()
    for ref in [*page_refs, there_ref]:
        ref[...] = jnp.zeros_like(ref)
    for r in range(ranks):
        counts[r] = 0

    def begin(e, carry):
        owner = owner_ref[e]
        slot = counts[owner]
        counts[owner] = slot + 1
        place = lax.rem(owner - rank_ref[0] + ranks, ranks)

        @pl.when(place == 0)
        def _():
            kept(e, slot).start()

        for k in range(1, ranks):
            @pl.when(place == k)
            def _():
                near(e, k, slot).start()
                far(e, k, slot).start()
        return carry

    lax.fori_loop(0, entries, begin, 0)
    for j in range(chunks):
        weight_copy(j).wait()
        depth = weight.shape[1]
        part = jnp.dot(
            x_ref[:, j * depth:(j + 1) * depth], weight[j], preferred_element_type=jnp.float32
        )
        if j:
            part = part + total[...]
        total[...] = part
    for k in range(ranks):
        dest = lax.rem(rank_ref[0] + k, ranks)
        out_refs[k][...] = total[pl.ds(pl.multiple_of(dest * share, share), share), :]

    def end(e, carry):
        kept(e, 0).wait()
        return carry

    lax.fori_loop(0, entries, end, 0)


def project(me, x, weight, page_list, owner_ids, cache, ranks):
    share = ROWS // ranks
    depth = weight.shape[0]
    block = min(depth, DEPTH)
    entries = page_list.shape[0]
    slots = 2 * entries // ranks
    smem = pl.BlockSpec(memory_space=pltpu.SMEM)
    vmem = pl.BlockSpec(memory_space=pltpu.VMEM)
    anywhere = pl.BlockSpec(memory_space=pl.ANY)
    out_shape = [jax.ShapeDtypeStruct((share, 2 * KVW), jnp.float32)] * ranks
    out_shape += [jax.ShapeDtypeStruct((slots, PAGE, 2 * KVW), jnp.bfloat16)]
    out_shape += [jax.ShapeDtypeStruct((slots, PAGE, KVW), jnp.bfloat16)] * (ranks - 1)
    out_shape += [jax.ShapeDtypeStruct((ranks - 1, slots, PAGE, KVW), jnp.bfloat16)]
    out = pl.pallas_call(
        functools.partial(project_kernel, ranks),
        in_specs=[smem, vmem, anywhere, smem, smem, anywhere],
        out_specs=[vmem] * len(out_shape),
        out_shape=out_shape,
        scratch_shapes=[
            pltpu.VMEM((depth // block, block, 2 * KVW), jnp.bfloat16),
            pltpu.VMEM((ROWS, 2 * KVW), jnp.float32),
            pltpu.SemaphoreType.DMA((depth // block,)),
            pltpu.SMEM((ranks,), jnp.int32),
            pltpu.SemaphoreType.DMA((entries,)),
        ],
        compiler_params=PARAMS,
        cost_estimate=small_cost(1 << 20),
        name="project",
    )(me.reshape(1), x, weight, page_list, owner_ids, cache)
    return out[:ranks], out[ranks:2 * ranks], out[2 * ranks]


def prepare_kernel(q_ref, k_ref, scale_ref, qc_ref, qs_ref, kc_ref, ks_ref, q_out, k_out):
    for g in range(GQ):
        q = rotated(q_ref[:, g * HD:(g + 1) * HD].astype(jnp.float32), qc_ref[...], qs_ref[...])
        q_out[g * ROWS:(g + 1) * ROWS, :] = q.astype(jnp.bfloat16)
    for h in range(KVH):
        columns = slice(h * HD, (h + 1) * HD)
        key = k_ref[:, columns].astype(jnp.float32) * scale_ref[:, columns]
        k_out[h] = rotated(key, kc_ref[...], ks_ref[...]).astype(jnp.bfloat16)


def prepare(queries, cache, key_scale, q_tables, k_tables):
    fixed = lambda j: (0, 0)
    rows = CTX // KVH
    return pl.pallas_call(
        prepare_kernel,
        grid=(KVH,),
        in_specs=[
            pl.BlockSpec((ROWS, GQ * HD), lambda j: (0, j)),
            pl.BlockSpec((rows, KVW), lambda j: (j, 0)),
            pl.BlockSpec((1, KVW), fixed),
            pl.BlockSpec((ROWS, HD), fixed),
            pl.BlockSpec((ROWS, HD), fixed),
            pl.BlockSpec((rows, HD), lambda j: (j, 0)),
            pl.BlockSpec((rows, HD), lambda j: (j, 0)),
        ],
        out_specs=[
            pl.BlockSpec((GQ * ROWS, HD), lambda j: (j, 0)),
            pl.BlockSpec((KVH, rows, HD), lambda j: (0, j, 0)),
        ],
        out_shape=[
            jax.ShapeDtypeStruct((HEADS * ROWS, HD), jnp.bfloat16),
            jax.ShapeDtypeStruct((KVH, CTX, HD), jnp.bfloat16),
        ],
        compiler_params=ATTEND_PARAMS,
        cost_estimate=small_cost(1 << 30),
        name="prepare",
    )(queries, cache, key_scale, *q_tables, *k_tables)


def split_level(level):
    doubled = jnp.maximum(level, NO_LEVEL) * 2.0
    high = jnp.floor(doubled)
    return [high, (doubled - high) * 65536.0 - 32768.0]


def joined_level(high, low):
    return (high + (low + 32768.0) * (1.0 / 65536.0)) * 0.5


def code_into(out_ref, lanes, top, total, numerator):
    largest = jnp.maximum(jnp.max(jnp.abs(numerator), axis=0, keepdims=True), TINY)
    coded = jnp.round(numerator * (1.0 / largest) * LEVELS)
    out_ref[:HD, lanes] = coded.astype(jnp.int32).astype(jnp.int16)
    tail = split_level(top + jnp.log2(largest)) + split_level(top + jnp.log2(total))
    tail = jnp.concatenate(tail + [jnp.zeros((TAIL - 4, top.shape[1]), jnp.float32)], axis=0)
    out_ref[HD:, lanes] = tail.astype(jnp.int32).astype(jnp.int16)


def decode(ref, lanes):
    tail = ref[HD:, lanes].astype(jnp.int32).astype(jnp.float32)
    values = ref[:HD, lanes].astype(jnp.int32).astype(jnp.float32)
    return joined_level(tail[0:1], tail[1:2]), joined_level(tail[2:3], tail[3:4]), values


def merged(top, total, numerator, parts):
    peak = functools.reduce(jnp.maximum, [p[1] for p in parts], top)
    if total is not None:
        factor = jnp.exp2(top - peak)
        total, numerator = total * factor, numerator * factor
    for level, weight, values in parts:
        more = jnp.exp2(weight - peak)
        part = values * (jnp.exp2(level - peak) * (1.0 / LEVELS))
        total = more if total is None else total + more
        numerator = part if numerator is None else numerator + part
    return peak, total, numerator


def fold_rows(values, combine):
    rows, cols = values.shape
    return combine(values.reshape(rows // 8, 8, cols), axis=0)


def gather_kernel(ranks, rank_ref, qc_ref, qs_ref, *refs):
    key_out, value_out = refs[ranks:]
    share = refs[0].shape[0]
    mine = pl.ds(pl.multiple_of(rank_ref[0] * share, share), share)
    cosine, signed_sine = qc_ref[mine, :], qs_ref[mine, :]
    for h in range(KVH):
        columns = slice(h * HD, (h + 1) * HD)
        key = sum(ref[:, columns] for ref in refs[:ranks])
        key = key.astype(jnp.bfloat16).astype(jnp.float32)
        key_out[h] = rotated(key, cosine, signed_sine).astype(jnp.bfloat16)
        columns = slice(KVW + h * HD, KVW + (h + 1) * HD)
        value_out[h] = sum(ref[:, columns] for ref in refs[:ranks]).astype(jnp.bfloat16)


def gather(me, q_tables, fresh):
    share = fresh[0].shape[0]
    vmem = pl.BlockSpec(memory_space=pltpu.VMEM)
    return pl.pallas_call(
        functools.partial(gather_kernel, len(fresh)),
        in_specs=[pl.BlockSpec(memory_space=pltpu.SMEM)] + [vmem] * (2 + len(fresh)),
        out_specs=[vmem] * 2,
        out_shape=[jax.ShapeDtypeStruct((KVH, share, HD), jnp.bfloat16)] * 2,
        compiler_params=ATTEND_PARAMS,
        cost_estimate=small_cost(1 << 18),
        name="gather",
    )(me.reshape(1), *q_tables, *fresh)


def attend_kernel(is_open, deps, length_ref, rank_ref, q_ref, k_ref, v_ref, fk_ref, fv_ref, *refs):
    refs = refs[deps:]
    if is_open:
        num_ref, stat_ref, scores = refs
    else:
        out_ref, scores = refs
    rank = rank_ref[0]
    share = fk_ref.shape[1]
    valid = length_ref[0] - rank * CTX
    first = rank * share
    fresh_key, fresh_value = fk_ref[0], fv_ref[0]
    cols = q_ref.shape[0]
    queries = q_ref[...]
    key_id = first + lax.broadcasted_iota(jnp.int32, (share, cols), 0)
    row_id = lax.broadcasted_iota(jnp.int32, (share, cols), 1) % ROWS
    fs = lax.dot_general(fresh_key, queries, CONTRACT_LAST, preferred_element_type=jnp.float32)
    fs = jnp.where(key_id <= row_id, fs, NEG_FILL)
    peak = fold_rows(fs, jnp.max)
    for t in range(CTX // KEYS):
        rows = slice(t * KEYS, (t + 1) * KEYS)
        s = lax.dot_general(
            k_ref[0, rows, :], queries, CONTRACT_LAST, preferred_element_type=jnp.float32
        )
        position = t * KEYS + lax.broadcasted_iota(jnp.int32, (KEYS, cols), 0)
        s = jnp.where(position < valid, s, NEG_FILL)
        scores[rows, :] = s
        peak = jnp.maximum(peak, fold_rows(s, jnp.max))
    peak = jnp.max(peak, axis=0, keepdims=True)
    base = jnp.maximum(peak, LOW)
    w = jnp.exp((fs - base) * SCALE)
    total = fold_rows(w, jnp.sum)
    numerator = lax.dot_general(
        fresh_value, w.astype(jnp.bfloat16), CONTRACT_FIRST, preferred_element_type=jnp.float32
    )
    for t in range(CTX // KEYS):
        rows = slice(t * KEYS, (t + 1) * KEYS)
        w = jnp.exp((scores[rows, :] - base) * SCALE)
        total = total + fold_rows(w, jnp.sum)
        numerator = numerator + lax.dot_general(
            v_ref[rows, :], w.astype(jnp.bfloat16), CONTRACT_FIRST, preferred_element_type=jnp.float32
        )
    total = jnp.sum(total, axis=0, keepdims=True)
    top = jnp.maximum(peak * EXP2_SCALE, NO_LEVEL)
    if is_open:
        num_ref[0] = numerator
        stat_ref[0] = jnp.concatenate([top, total, jnp.zeros((6, cols), jnp.float32)], axis=0)
    else:
        code_into(out_ref, slice(0, cols), top, total, numerator)


def layout(ranks):
    heads_here = HEADS // ranks
    pieces = max(1, heads_here // GQ)
    heads = heads_here // pieces
    return pieces, heads, heads * ROWS, ROWS // ranks


def whole(j, s):
    return (0, 0)


def opened_specs(cols):
    place = lambda j, n, r: (j, 0, 0)
    return [pl.BlockSpec((1, HD, cols), place), pl.BlockSpec((1, 8, cols), place)]


def attend(length, me, code, queries, keys, cache, fresh, earlier, ranks, is_open, cost):
    pieces, heads, cols, share = layout(ranks)

    def piece(j, rank_ref):
        return (rank_ref[0] ^ code) * pieces + j

    def key_head(j, rank_ref):
        return piece(j, rank_ref) * heads // GQ

    if is_open:
        out_specs = opened_specs(cols)
        out_shape = [
            jax.ShapeDtypeStruct((pieces, HD, cols), jnp.float32),
            jax.ShapeDtypeStruct((pieces, 8, cols), jnp.float32),
        ]
    else:
        out_specs = pl.BlockSpec((HD + TAIL, cols), lambda j, n, r: (0, j))
        out_shape = jax.ShapeDtypeStruct((HD + TAIL, pieces * cols), jnp.int16)
    own_head = lambda j, n, r: (key_head(j, r), 0, 0)
    return pl.pallas_call(
        functools.partial(attend_kernel, is_open, len(earlier)),
        grid_spec=pltpu.PrefetchScalarGridSpec(
            num_scalar_prefetch=2,
            grid=(pieces,),
            in_specs=[
                pl.BlockSpec((cols, HD), lambda j, n, r: (piece(j, r), 0)),
                pl.BlockSpec((1, CTX, HD), own_head),
                pl.BlockSpec((CTX, HD), lambda j, n, r: (0, KVH + key_head(j, r))),
                pl.BlockSpec((1, share, HD), own_head),
                pl.BlockSpec((1, share, HD), own_head),
            ]
            + [pl.BlockSpec(memory_space=pl.ANY)] * len(earlier),
            out_specs=out_specs,
            scratch_shapes=[pltpu.VMEM((CTX, cols), jnp.float32)],
        ),
        out_shape=out_shape,
        compiler_params=ATTEND_PARAMS,
        cost_estimate=small_cost(cost),
        name="attend_open" if is_open else "attend",
    )(length, me, queries, keys, cache, *fresh, *earlier)


def close_kernel(is_last, count, num_ref, stat_ref, *refs):
    in_refs, out_ref = refs[:count], refs[-1]
    for b in range(out_ref.shape[1] // LANES):
        lanes = slice(b * LANES, (b + 1) * LANES)
        top, total, numerator = stat_ref[0, 0:1, lanes], stat_ref[0, 1:2, lanes], num_ref[0, :, lanes]
        parts = [decode(ref, lanes) for ref in in_refs]
        top, total, numerator = merged(top, total, numerator, parts)
        if not is_last:
            code_into(out_ref, lanes, top, total, numerator)
            continue
        numerator = numerator / total
        for h in range(LANES // ROWS):
            column = b * LANES + h * HD
            out_ref[:, column:column + HD] = (
                numerator[:, h * ROWS:(h + 1) * ROWS].T.astype(jnp.bfloat16)
            )


def close(opened, received, earlier, ranks, is_last=False):
    pieces, _, cols, _ = layout(ranks)
    rows, kind = (ROWS, jnp.bfloat16) if is_last else (HD + TAIL, jnp.int16)
    place = lambda j: (j, 0, 0)
    return pl.pallas_call(
        functools.partial(close_kernel, is_last, len(received)),
        grid=(pieces,),
        in_specs=[pl.BlockSpec((1, HD, cols), place), pl.BlockSpec((1, 8, cols), place)]
        + [pl.BlockSpec((HD + TAIL, cols), lambda j: (0, j))] * len(received)
        + [pl.BlockSpec(memory_space=pl.ANY)] * len(earlier),
        out_specs=pl.BlockSpec((rows, cols), lambda j: (0, j)),
        out_shape=jax.ShapeDtypeStruct((rows, pieces * cols), kind),
        compiler_params=SMALL_PARAMS,
        cost_estimate=small_cost(1 << 18),
        name="finish" if is_last else "close",
    )(*opened, *received, *earlier)


def choose_kernel(sec_ref, *refs):
    count = (len(refs) - 2) // 2
    near, there_ref, out_refs, sems = refs[:count], refs[count], refs[count + 1:-1], refs[-1]
    first = sec_ref[0] == 0
    for k in range(count):
        @pl.when(first)
        def _():
            pltpu.make_async_copy(near[k], out_refs[k], sems.at[k]).start()

        @pl.when(jnp.logical_not(first))
        def _():
            pltpu.make_async_copy(there_ref.at[k], out_refs[k], sems.at[k]).start()

    for k in range(count):
        pltpu.make_async_copy(near[k], out_refs[k], sems.at[k]).wait()


def choose(sec, near, there):
    count = len(near)
    return pl.pallas_call(
        choose_kernel,
        in_specs=[pl.BlockSpec(memory_space=pltpu.SMEM)] + [pl.BlockSpec(memory_space=pl.ANY)] * (count + 1),
        out_specs=[pl.BlockSpec(memory_space=pltpu.VMEM)] * count,
        out_shape=[jax.ShapeDtypeStruct(there.shape[1:], there.dtype)] * count,
        scratch_shapes=[pltpu.SemaphoreType.DMA((count,))],
        compiler_params=SMALL_PARAMS,
        cost_estimate=small_cost(1 << 18),
        name="choose",
    )(sec.reshape(1), *near, there)


def arrange_kernel(sec_ref, rank_ref, kept_ref, *refs):
    count = (len(refs) - 2) // 2
    crossed, routed, out_ref = refs[:count], refs[count:2 * count], refs[-1]
    shift = lax.rem(rank_ref[0] - pl.program_id(0) + count + 1, count + 1)
    second = sec_ref[0] > 0

    @pl.when(jnp.logical_not(second))
    def _():
        out_ref[...] = jnp.zeros_like(out_ref)

    @pl.when(jnp.logical_and(second, shift == 0))
    def _():
        out_ref[...] = kept_ref[...]

    for k in range(count):
        @pl.when(jnp.logical_and(second, shift == k + 1))
        def _():
            out_ref[:, :, :KVW] = crossed[k][...]
            out_ref[:, :, KVW:] = routed[k][...]


def arrange(sec, me, kept, crossed, routed, earlier):
    ranks = len(crossed) + 1
    slots = kept.shape[0]
    smem = pl.BlockSpec(memory_space=pltpu.SMEM)
    return pl.pallas_call(
        arrange_kernel,
        grid=(ranks,),
        in_specs=[smem, smem]
        + [pl.BlockSpec(v.shape, lambda j: (0, 0, 0)) for v in [kept, *crossed, *routed]]
        + [pl.BlockSpec(memory_space=pl.ANY)],
        out_specs=pl.BlockSpec((slots, PAGE, 2 * KVW), lambda j: (j, 0, 0)),
        out_shape=jax.ShapeDtypeStruct((ranks * slots, PAGE, 2 * KVW), jnp.bfloat16),
        compiler_params=SMALL_PARAMS,
        cost_estimate=small_cost(1 << 18),
        name="arrange",
    )(sec.reshape(1), me.reshape(1), kept, *crossed, *routed, earlier)


def after(value, earlier):
    return lax.optimization_barrier((value, earlier))[0]


def shards(queries, kv_cache, key_scale, fresh_input, kv_weight, lengths, page_list, owners):
    ranks = lax.axis_size("rank")
    secs = lax.axis_size("sec")
    me = lax.axis_index("rank").astype(jnp.int32)
    sec = lax.axis_index("sec").astype(jnp.int32)
    cache = kv_cache[0]
    length = lengths[0, 0]
    pieces, heads, _, _ = layout(ranks)

    def shifted(value, k):
        return lax.ppermute(value, "rank", [(i, (i + k) % ranks) for i in range(ranks)])

    def swapped(value, bit):
        return lax.ppermute(value, "rank", [(i, i ^ bit) for i in range(ranks)])

    def handed_on(value):
        return lax.ppermute(value, "sec", [(i, (i + 1) % secs) for i in range(secs)])

    part, (kept, *near), there = project(
        me, fresh_input[0], kv_weight, page_list, owners[:, 0], cache, ranks
    )
    fresh = [part[0]] + [shifted(part[k], k) for k in range(1, ranks)]

    q_tables = rope_tables(after(length, part) + jnp.arange(ROWS, dtype=jnp.int32))
    k_tables = rope_tables(after(me, part) * CTX + jnp.arange(CTX, dtype=jnp.int32))
    there = handed_on(there)
    q_rot, keys = prepare(queries[0], cache, key_scale[None, :], q_tables, k_tables)
    chosen = choose(sec, near, after(there, q_rot))
    arrived = after(fresh, chosen)
    chosen = after(chosen, arrived)
    routed = [shifted(c, k + 1) for k, c in enumerate(chosen)]
    fresh = gather(me, q_tables, arrived)
    kept = handed_on(after(kept, fresh))

    def attend_to(code, earlier, is_open, cost=1 << 28):
        return attend(
            lengths[0], me.reshape(1), code, q_rot, keys, cache, fresh, earlier, ranks, is_open, cost
        )

    taken = {code: [] for code in range(ranks)}

    def send(value, code, bit):
        taken[code ^ bit].append(swapped(value, bit))

    last = chosen[:1]
    for code in range(ranks - 1, 1, -2):
        last = [attend_to(code, last, False)]
        send(last[0], code, 1)
    merging = {}
    for code in range(ranks - 2, 0, -2):
        merging[code] = attend_to(code, last, True)
        last = merging[code][1:]
    waiting = attend_to(1, [*routed[::2], *last], True, 1 << 32)
    last = waiting[1:]
    bit = 2
    while bit < ranks:
        for code in range(ranks - bit, 0, -2 * bit):
            last = [close(merging[code], taken[code], last, ranks)]
            send(last[0], code, bit)
        bit *= 2
    direct = close(waiting, [], [*last, *routed[1::2]], ranks)
    own = attend_to(0, [direct], True)
    handed = arrange(sec, me, kept, [handed_on(r) for r in routed], routed, own[1])
    taken[0].insert(0, swapped(direct, 1))
    attended = close(after(own, handed), taken[0], [], ranks, is_last=True)[None]
    return (attended, handed[None])


def solution(mesh):
    return jax.shard_map(
        shards,
        mesh=mesh,
        in_specs=(
            P(("sec", "grp"), None, None),
            P(("sec", "grp"), "rank", None),
            P(),
            P(("sec", "grp"), None, "rank"),
            P("rank", None),
            P(("sec", "grp"), None),
            P(("sec", "grp", "rank")),
            P(("sec", "grp", "rank"), None),
        ),
        out_specs=(P(("sec", "grp"), None, "rank"), P(("sec", "grp", "rank"), None, None, None)),
        check_vma=False,
    )
```

```python
import functools
import math

import jax
import jax.numpy as jnp
import numpy as np
from jax import lax
from jax.experimental import pallas as pl
from jax.experimental.pallas import tpu as pltpu
from jax.sharding import PartitionSpec as P

HEADS = 64
KVH = 8
HD = 128
ROWS = 128
CTX = 1024
PAGE = 16
GQ = 8
KVW = 1024

ROPE_BASE = 500000.0
NEG_FILL = -1e30
LOW = -1e29
TINY = 1.2e-38
NO_LEVEL = -16000.0
LEVELS = 32767.0
SCALE = 1.0 / math.sqrt(HD)
EXP2_SCALE = SCALE * math.log2(math.e)
LANES = 256
KEYS = 512
DEPTH = 512
TAIL = 8
CONTRACT_FIRST = (((0,), (0,)), ((), ()))
CONTRACT_LAST = (((1,), (1,)), ((), ()))
PARAMS = pltpu.CompilerParams(vmem_limit_bytes=60 << 20)
ATTEND_PARAMS = pltpu.CompilerParams(vmem_limit_bytes=32 << 20)
SMALL_PARAMS = pltpu.CompilerParams(vmem_limit_bytes=40 << 20)


def small_cost(flops):
    return pl.CostEstimate(flops=flops, bytes_accessed=1 << 16, transcendentals=0)


def inverse_frequencies():
    steps = np.arange(HD // 2, dtype=np.float32) * np.float32(-2.0 * math.log(ROPE_BASE) / HD)
    return np.exp(steps.astype(np.float64)).astype(np.float32)


def rope_tables(positions):
    inverse = jnp.asarray(np.tile(inverse_frequencies(), 2))
    sign = np.repeat(np.array([-1.0, 1.0], np.float32), HD // 2)
    angles = positions.astype(jnp.float32)[:, None] * inverse[None, :]
    return jnp.cos(angles), jnp.sin(angles) * sign[None, :]


def rotated(values, cosine, signed_sine):
    return values * cosine + pltpu.roll(values, HD // 2, 1) * signed_sine


def project_kernel(ranks, rank_ref, x_ref, w_ref, page_ref, owner_ref, cache_ref, *refs):
    out_refs, page_outs = refs[:ranks], refs[ranks:2 * ranks + 1]
    rows_in, weight, total, kept_pages, near_pages, far_pages, sems, counts, page_sems, out_sems = (
        refs[2 * ranks + 1:]
    )
    entries = page_ref.shape[0]
    share = out_refs[0].shape[0]
    chunks, depth = weight.shape[0], weight.shape[1]
    rows_copy = pltpu.make_async_copy(x_ref, rows_in, sems.at[chunks])

    def weight_copy(j):
        source = w_ref.at[pl.ds(j * depth, depth), :]
        return pltpu.make_async_copy(source, weight.at[j], sems.at[j])

    def page_rows(e):
        return pl.ds(pl.multiple_of(page_ref[e] * PAGE, PAGE), PAGE)

    def kept(e, slot):
        return pltpu.make_async_copy(cache_ref.at[page_rows(e), :], kept_pages.at[slot], page_sems.at[e])

    def near(e, k, slot):
        source = cache_ref.at[page_rows(e), pl.ds(0, KVW)]
        return pltpu.make_async_copy(source, near_pages.at[k - 1, slot], page_sems.at[e])

    def far(e, k, slot):
        source = cache_ref.at[page_rows(e), pl.ds(KVW, KVW)]
        return pltpu.make_async_copy(source, far_pages.at[k - 1, slot], page_sems.at[e])

    rows_copy.start()
    for j in range(chunks):
        weight_copy(j).start()
    for ref in (kept_pages, near_pages, far_pages):
        ref[...] = jnp.zeros_like(ref)
    for r in range(ranks):
        counts[r] = 0

    def begin(e, carry):
        owner = owner_ref[e]
        slot = counts[owner]
        counts[owner] = slot + 1
        place = lax.rem(owner - rank_ref[0] + ranks, ranks)

        @pl.when(place == 0)
        def _():
            kept(e, slot).start()

        @pl.when(place > 0)
        def _():
            near(e, place, slot).start()
            far(e, place, slot).start()

        return carry

    def end(e, carry):
        kept(e, 0).wait()
        return carry

    sources = [kept_pages, *[near_pages.at[k] for k in range(ranks - 1)], far_pages]
    page_copies = [
        pltpu.make_async_copy(source, out, out_sems.at[i])
        for i, (source, out) in enumerate(zip(sources, page_outs))
    ]
    lax.fori_loop(0, entries, begin, 0)
    rows_copy.wait()
    for j in range(chunks):
        weight_copy(j).wait()
        part = jnp.dot(
            rows_in[:, j * depth:(j + 1) * depth], weight[j], preferred_element_type=jnp.float32
        )
        if j:
            part = part + total[...]
        total[...] = part
        if j == min(1, chunks - 1):
            lax.fori_loop(0, entries, end, 0)
            for c in page_copies:
                c.start()
    for k in range(ranks):
        dest = lax.rem(rank_ref[0] + k, ranks)
        out_refs[k][...] = total[pl.ds(pl.multiple_of(dest * share, share), share), :]
    for c in page_copies:
        c.wait()


def project(me, x, weight, page_list, owner_ids, cache, ranks):
    share = ROWS // ranks
    depth = weight.shape[0]
    block = min(depth, DEPTH)
    entries = page_list.shape[0]
    slots = 2 * entries // ranks
    smem = pl.BlockSpec(memory_space=pltpu.SMEM)
    vmem = pl.BlockSpec(memory_space=pltpu.VMEM)
    anywhere = pl.BlockSpec(memory_space=pl.ANY)
    pages = [(slots, PAGE, 2 * KVW)] + [(slots, PAGE, KVW)] * (ranks - 1)
    pages += [(ranks - 1, slots, PAGE, KVW)]
    out = pl.pallas_call(
        functools.partial(project_kernel, ranks),
        in_specs=[smem, anywhere, anywhere, smem, smem, anywhere],
        out_specs=[vmem] * ranks + [anywhere] * len(pages),
        out_shape=[jax.ShapeDtypeStruct((share, 2 * KVW), jnp.float32)] * ranks
        + [jax.ShapeDtypeStruct(shape, jnp.bfloat16) for shape in pages],
        scratch_shapes=[
            pltpu.VMEM((ROWS, depth), jnp.bfloat16),
            pltpu.VMEM((depth // block, block, 2 * KVW), jnp.bfloat16),
            pltpu.VMEM((ROWS, 2 * KVW), jnp.float32),
            pltpu.VMEM(pages[0], jnp.bfloat16),
            pltpu.VMEM(pages[-1], jnp.bfloat16),
            pltpu.VMEM(pages[-1], jnp.bfloat16),
            pltpu.SemaphoreType.DMA((depth // block + 1,)),
            pltpu.SMEM((ranks,), jnp.int32),
            pltpu.SemaphoreType.DMA((entries,)),
            pltpu.SemaphoreType.DMA((len(pages),)),
        ],
        compiler_params=PARAMS,
        cost_estimate=small_cost(1 << 20),
        name="project",
    )(me.reshape(1), x, weight, page_list, owner_ids, cache)
    return out[:ranks], out[ranks:2 * ranks], out[2 * ranks]


def prepare_kernel(q_ref, k_ref, scale_ref, qc_ref, qs_ref, kc_ref, ks_ref, q_out, k_out):
    for g in range(GQ):
        q = rotated(q_ref[:, g * HD:(g + 1) * HD].astype(jnp.float32), qc_ref[...], qs_ref[...])
        q_out[g * ROWS:(g + 1) * ROWS, :] = q.astype(jnp.bfloat16)
    for h in range(KVH):
        columns = slice(h * HD, (h + 1) * HD)
        key = k_ref[:, columns].astype(jnp.float32) * scale_ref[:, columns]
        k_out[h] = rotated(key, kc_ref[...], ks_ref[...]).astype(jnp.bfloat16)


def prepare(queries, cache, key_scale, q_tables, k_tables):
    fixed = lambda j: (0, 0)
    rows = CTX // KVH
    return pl.pallas_call(
        prepare_kernel,
        grid=(KVH,),
        in_specs=[
            pl.BlockSpec((ROWS, GQ * HD), lambda j: (0, j)),
            pl.BlockSpec((rows, KVW), lambda j: (j, 0)),
            pl.BlockSpec((1, KVW), fixed),
            pl.BlockSpec((ROWS, HD), fixed),
            pl.BlockSpec((ROWS, HD), fixed),
            pl.BlockSpec((rows, HD), lambda j: (j, 0)),
            pl.BlockSpec((rows, HD), lambda j: (j, 0)),
        ],
        out_specs=[
            pl.BlockSpec((GQ * ROWS, HD), lambda j: (j, 0)),
            pl.BlockSpec((KVH, rows, HD), lambda j: (0, j, 0)),
        ],
        out_shape=[
            jax.ShapeDtypeStruct((HEADS * ROWS, HD), jnp.bfloat16),
            jax.ShapeDtypeStruct((KVH, CTX, HD), jnp.bfloat16),
        ],
        compiler_params=ATTEND_PARAMS,
        cost_estimate=small_cost(1 << 30),
        name="prepare",
    )(queries, cache, key_scale, *q_tables, *k_tables)


def split_level(level):
    doubled = jnp.maximum(level, NO_LEVEL) * 2.0
    high = jnp.floor(doubled)
    return [high, (doubled - high) * 65536.0 - 32768.0]


def joined_level(high, low):
    return (high + (low + 32768.0) * (1.0 / 65536.0)) * 0.5


def code_into(out_ref, lanes, top, total, numerator):
    largest = jnp.maximum(jnp.max(jnp.abs(numerator), axis=0, keepdims=True), TINY)
    coded = jnp.round(numerator * (1.0 / largest) * LEVELS)
    out_ref[:HD, lanes] = coded.astype(jnp.int32).astype(jnp.int16)
    tail = split_level(top + jnp.log2(largest)) + split_level(top + jnp.log2(total))
    tail = jnp.concatenate(tail + [jnp.zeros((TAIL - 4, top.shape[1]), jnp.float32)], axis=0)
    out_ref[HD:, lanes] = tail.astype(jnp.int32).astype(jnp.int16)


def decode(ref, lanes):
    tail = ref[HD:, lanes].astype(jnp.int32).astype(jnp.float32)
    values = ref[:HD, lanes].astype(jnp.int32).astype(jnp.float32)
    return joined_level(tail[0:1], tail[1:2]), joined_level(tail[2:3], tail[3:4]), values


def merged(top, total, numerator, parts):
    peak = functools.reduce(jnp.maximum, [p[1] for p in parts], top)
    if total is not None:
        factor = jnp.exp2(top - peak)
        total, numerator = total * factor, numerator * factor
    for level, weight, values in parts:
        more = jnp.exp2(weight - peak)
        part = values * (jnp.exp2(level - peak) * (1.0 / LEVELS))
        total = more if total is None else total + more
        numerator = part if numerator is None else numerator + part
    return peak, total, numerator


def fold_rows(values, combine):
    rows, cols = values.shape
    return combine(values.reshape(rows // 8, 8, cols), axis=0)


def gather_kernel(ranks, rank_ref, qc_ref, qs_ref, *refs):
    key_out, value_out = refs[ranks:]
    share = refs[0].shape[0]
    mine = pl.ds(pl.multiple_of(rank_ref[0] * share, share), share)
    cosine, signed_sine = qc_ref[mine, :], qs_ref[mine, :]
    for h in range(KVH):
        columns = slice(h * HD, (h + 1) * HD)
        key = sum(ref[:, columns] for ref in refs[:ranks])
        key = key.astype(jnp.bfloat16).astype(jnp.float32)
        key_out[h] = rotated(key, cosine, signed_sine).astype(jnp.bfloat16)
        columns = slice(KVW + h * HD, KVW + (h + 1) * HD)
        value_out[h] = sum(ref[:, columns] for ref in refs[:ranks]).astype(jnp.bfloat16)


def gather(me, q_tables, fresh):
    share = fresh[0].shape[0]
    vmem = pl.BlockSpec(memory_space=pltpu.VMEM)
    return pl.pallas_call(
        functools.partial(gather_kernel, len(fresh)),
        in_specs=[pl.BlockSpec(memory_space=pltpu.SMEM)] + [vmem] * (2 + len(fresh)),
        out_specs=[vmem] * 2,
        out_shape=[jax.ShapeDtypeStruct((KVH, share, HD), jnp.bfloat16)] * 2,
        compiler_params=ATTEND_PARAMS,
        cost_estimate=small_cost(1 << 18),
        name="gather",
    )(me.reshape(1), *q_tables, *fresh)


def attend_kernel(is_open, deps, length_ref, rank_ref, q_ref, k_ref, v_ref, fk_ref, fv_ref, *refs):
    refs = refs[deps:]
    if is_open:
        num_ref, stat_ref, scores = refs
    else:
        out_ref, scores = refs
    rank = rank_ref[0]
    share = fk_ref.shape[1]
    valid = length_ref[0] - rank * CTX
    first = rank * share
    fresh_key, fresh_value = fk_ref[0], fv_ref[0]
    cols = q_ref.shape[0]
    queries = q_ref[...]
    key_id = first + lax.broadcasted_iota(jnp.int32, (share, cols), 0)
    row_id = lax.broadcasted_iota(jnp.int32, (share, cols), 1) % ROWS
    fs = lax.dot_general(fresh_key, queries, CONTRACT_LAST, preferred_element_type=jnp.float32)
    fs = jnp.where(key_id <= row_id, fs, NEG_FILL)
    peak = fold_rows(fs, jnp.max)
    for t in range(CTX // KEYS):
        rows = slice(t * KEYS, (t + 1) * KEYS)
        s = lax.dot_general(
            k_ref[0, rows, :], queries, CONTRACT_LAST, preferred_element_type=jnp.float32
        )
        position = t * KEYS + lax.broadcasted_iota(jnp.int32, (KEYS, cols), 0)
        s = jnp.where(position < valid, s, NEG_FILL)
        scores[rows, :] = s
        peak = jnp.maximum(peak, fold_rows(s, jnp.max))
    peak = jnp.max(peak, axis=0, keepdims=True)
    base = jnp.maximum(peak, LOW)
    w = jnp.exp((fs - base) * SCALE)
    total = fold_rows(w, jnp.sum)
    numerator = lax.dot_general(
        fresh_value, w.astype(jnp.bfloat16), CONTRACT_FIRST, preferred_element_type=jnp.float32
    )
    for t in range(CTX // KEYS):
        rows = slice(t * KEYS, (t + 1) * KEYS)
        w = jnp.exp((scores[rows, :] - base) * SCALE)
        total = total + fold_rows(w, jnp.sum)
        numerator = numerator + lax.dot_general(
            v_ref[rows, :], w.astype(jnp.bfloat16), CONTRACT_FIRST, preferred_element_type=jnp.float32
        )
    total = jnp.sum(total, axis=0, keepdims=True)
    top = jnp.maximum(peak * EXP2_SCALE, NO_LEVEL)
    if is_open:
        num_ref[0] = numerator
        stat_ref[0] = jnp.concatenate([top, total, jnp.zeros((6, cols), jnp.float32)], axis=0)
    else:
        code_into(out_ref, slice(0, cols), top, total, numerator)


def layout(ranks):
    heads_here = HEADS // ranks
    pieces = max(1, heads_here // GQ)
    heads = heads_here // pieces
    return pieces, heads, heads * ROWS, ROWS // ranks


def whole(j, s):
    return (0, 0)


def opened_specs(cols):
    place = lambda j, n, r: (j, 0, 0)
    return [pl.BlockSpec((1, HD, cols), place), pl.BlockSpec((1, 8, cols), place)]


def attend(length, me, code, queries, keys, cache, fresh, earlier, ranks, is_open, cost):
    pieces, heads, cols, share = layout(ranks)

    def piece(j, rank_ref):
        return (rank_ref[0] ^ code) * pieces + j

    def key_head(j, rank_ref):
        return piece(j, rank_ref) * heads // GQ

    if is_open:
        out_specs = opened_specs(cols)
        out_shape = [
            jax.ShapeDtypeStruct((pieces, HD, cols), jnp.float32),
            jax.ShapeDtypeStruct((pieces, 8, cols), jnp.float32),
        ]
    else:
        out_specs = pl.BlockSpec((HD + TAIL, cols), lambda j, n, r: (0, j))
        out_shape = jax.ShapeDtypeStruct((HD + TAIL, pieces * cols), jnp.int16)
    own_head = lambda j, n, r: (key_head(j, r), 0, 0)
    return pl.pallas_call(
        functools.partial(attend_kernel, is_open, len(earlier)),
        grid_spec=pltpu.PrefetchScalarGridSpec(
            num_scalar_prefetch=2,
            grid=(pieces,),
            in_specs=[
                pl.BlockSpec((cols, HD), lambda j, n, r: (piece(j, r), 0)),
                pl.BlockSpec((1, CTX, HD), own_head),
                pl.BlockSpec((CTX, HD), lambda j, n, r: (0, KVH + key_head(j, r))),
                pl.BlockSpec((1, share, HD), own_head),
                pl.BlockSpec((1, share, HD), own_head),
            ]
            + [pl.BlockSpec(memory_space=pl.ANY)] * len(earlier),
            out_specs=out_specs,
            scratch_shapes=[pltpu.VMEM((CTX, cols), jnp.float32)],
        ),
        out_shape=out_shape,
        compiler_params=ATTEND_PARAMS,
        cost_estimate=small_cost(cost),
        name="attend_open" if is_open else "attend",
    )(length, me, queries, keys, cache, *fresh, *earlier)


def close_kernel(is_last, count, num_ref, stat_ref, *refs):
    in_refs, out_ref = refs[:count], refs[-1]
    for b in range(out_ref.shape[1] // LANES):
        lanes = slice(b * LANES, (b + 1) * LANES)
        top, total, numerator = stat_ref[0, 0:1, lanes], stat_ref[0, 1:2, lanes], num_ref[0, :, lanes]
        parts = [decode(ref, lanes) for ref in in_refs]
        top, total, numerator = merged(top, total, numerator, parts)
        if not is_last:
            code_into(out_ref, lanes, top, total, numerator)
            continue
        numerator = numerator / total
        for h in range(LANES // ROWS):
            column = b * LANES + h * HD
            out_ref[:, column:column + HD] = (
                numerator[:, h * ROWS:(h + 1) * ROWS].T.astype(jnp.bfloat16)
            )


def close(opened, received, earlier, ranks, is_last=False):
    pieces, _, cols, _ = layout(ranks)
    rows, kind = (ROWS, jnp.bfloat16) if is_last else (HD + TAIL, jnp.int16)
    place = lambda j: (j, 0, 0)
    return pl.pallas_call(
        functools.partial(close_kernel, is_last, len(received)),
        grid=(pieces,),
        in_specs=[pl.BlockSpec((1, HD, cols), place), pl.BlockSpec((1, 8, cols), place)]
        + [pl.BlockSpec((HD + TAIL, cols), lambda j: (0, j))] * len(received)
        + [pl.BlockSpec(memory_space=pl.ANY)] * len(earlier),
        out_specs=pl.BlockSpec((rows, cols), lambda j: (0, j)),
        out_shape=jax.ShapeDtypeStruct((rows, pieces * cols), kind),
        compiler_params=SMALL_PARAMS,
        cost_estimate=small_cost(1 << 18),
        name="finish" if is_last else "close",
    )(*opened, *received, *earlier)


def choose_kernel(sec_ref, *refs):
    count = (len(refs) - 2) // 2
    near, there_ref, out_refs, sems = refs[:count], refs[count], refs[count + 1:-1], refs[-1]
    first = sec_ref[0] == 0
    for k in range(count):
        @pl.when(first)
        def _():
            pltpu.make_async_copy(near[k], out_refs[k], sems.at[k]).start()

        @pl.when(jnp.logical_not(first))
        def _():
            pltpu.make_async_copy(there_ref.at[k], out_refs[k], sems.at[k]).start()

    for k in range(count):
        pltpu.make_async_copy(near[k], out_refs[k], sems.at[k]).wait()


def choose(sec, near, there):
    count = len(near)
    return pl.pallas_call(
        choose_kernel,
        in_specs=[pl.BlockSpec(memory_space=pltpu.SMEM)] + [pl.BlockSpec(memory_space=pl.ANY)] * (count + 1),
        out_specs=[pl.BlockSpec(memory_space=pltpu.VMEM)] * count,
        out_shape=[jax.ShapeDtypeStruct(there.shape[1:], there.dtype)] * count,
        scratch_shapes=[pltpu.SemaphoreType.DMA((count,))],
        compiler_params=SMALL_PARAMS,
        cost_estimate=small_cost(1 << 18),
        name="choose",
    )(sec.reshape(1), *near, there)


def arrange_kernel(sec_ref, rank_ref, kept_ref, *refs):
    count = (len(refs) - 2) // 2
    crossed, routed, out_ref = refs[:count], refs[count:2 * count], refs[-1]
    shift = lax.rem(rank_ref[0] - pl.program_id(0) + count + 1, count + 1)
    second = sec_ref[0] > 0

    @pl.when(jnp.logical_not(second))
    def _():
        out_ref[...] = jnp.zeros_like(out_ref)

    @pl.when(jnp.logical_and(second, shift == 0))
    def _():
        out_ref[...] = kept_ref[...]

    for k in range(count):
        @pl.when(jnp.logical_and(second, shift == k + 1))
        def _():
            out_ref[:, :, :KVW] = crossed[k][...]
            out_ref[:, :, KVW:] = routed[k][...]


def arrange(sec, me, kept, crossed, routed, earlier):
    ranks = len(crossed) + 1
    slots = kept.shape[0]
    smem = pl.BlockSpec(memory_space=pltpu.SMEM)
    return pl.pallas_call(
        arrange_kernel,
        grid=(ranks,),
        in_specs=[smem, smem]
        + [pl.BlockSpec(v.shape, lambda j: (0, 0, 0)) for v in [kept, *crossed, *routed]]
        + [pl.BlockSpec(memory_space=pl.ANY)],
        out_specs=pl.BlockSpec((slots, PAGE, 2 * KVW), lambda j: (j, 0, 0)),
        out_shape=jax.ShapeDtypeStruct((ranks * slots, PAGE, 2 * KVW), jnp.bfloat16),
        compiler_params=SMALL_PARAMS,
        cost_estimate=small_cost(1 << 18),
        name="arrange",
    )(sec.reshape(1), me.reshape(1), kept, *crossed, *routed, earlier)


def after(value, earlier):
    return lax.optimization_barrier((value, earlier))[0]


def shards(queries, kv_cache, key_scale, fresh_input, kv_weight, lengths, page_list, owners):
    ranks = lax.axis_size("rank")
    secs = lax.axis_size("sec")
    me = lax.axis_index("rank").astype(jnp.int32)
    sec = lax.axis_index("sec").astype(jnp.int32)
    cache = kv_cache[0]
    length = lengths[0, 0]
    pieces, heads, _, _ = layout(ranks)

    def shifted(value, k):
        return lax.ppermute(value, "rank", [(i, (i + k) % ranks) for i in range(ranks)])

    def swapped(value, bit):
        return lax.ppermute(value, "rank", [(i, i ^ bit) for i in range(ranks)])

    def handed_on(value):
        return lax.ppermute(value, "sec", [(i, (i + 1) % secs) for i in range(secs)])

    part, (kept, *near), there = project(
        me, fresh_input[0], kv_weight, page_list, owners[:, 0], cache, ranks
    )
    fresh = [part[0]] + [shifted(part[k], k) for k in range(1, ranks)]

    q_tables = rope_tables(after(length, part) + jnp.arange(ROWS, dtype=jnp.int32))
    k_tables = rope_tables(after(me, part) * CTX + jnp.arange(CTX, dtype=jnp.int32))
    there = handed_on(there)
    q_rot, keys = prepare(queries[0], cache, key_scale[None, :], q_tables, k_tables)
    chosen = choose(sec, near, after(there, q_rot))
    arrived = after(fresh, chosen)
    chosen = after(chosen, arrived)
    routed = [shifted(c, k + 1) for k, c in enumerate(chosen)]
    fresh = gather(me, q_tables, arrived)
    kept = handed_on(after(kept, fresh))

    def attend_to(code, earlier, is_open, cost=1 << 28):
        return attend(
            lengths[0], me.reshape(1), code, q_rot, keys, cache, fresh, earlier, ranks, is_open, cost
        )

    taken = {code: [] for code in range(ranks)}

    def send(value, code, bit):
        taken[code ^ bit].append(swapped(value, bit))

    last = chosen[:1]
    for code in range(ranks - 1, 1, -2):
        last = [attend_to(code, last, False)]
        send(last[0], code, 1)
    merging = {}
    for code in range(ranks - 2, 0, -2):
        merging[code] = attend_to(code, last, True)
        last = merging[code][1:]
    waiting = attend_to(1, [*routed[::2], *last], True, 1 << 32)
    last = waiting[1:]
    bit = 2
    while bit < ranks:
        for code in range(ranks - bit, 0, -2 * bit):
            last = [close(merging[code], taken[code], last, ranks)]
            send(last[0], code, bit)
        bit *= 2
    direct = close(waiting, [], [*last, *routed[1::2]], ranks)
    own = attend_to(0, [direct], True)
    handed = arrange(sec, me, kept, [handed_on(r) for r in routed], routed, own[1])
    taken[0].insert(0, swapped(direct, 1))
    attended = close(after(own, handed), taken[0], [], ranks, is_last=True)[None]
    return (attended, handed[None])


def solution(mesh):
    return jax.shard_map(
        shards,
        mesh=mesh,
        in_specs=(
            P(("sec", "grp"), None, None),
            P(("sec", "grp"), "rank", None),
            P(),
            P(("sec", "grp"), None, "rank"),
            P("rank", None),
            P(("sec", "grp"), None),
            P(("sec", "grp", "rank")),
            P(("sec", "grp", "rank"), None),
        ),
        out_specs=(P(("sec", "grp"), None, "rank"), P(("sec", "grp", "rank"), None, None, None)),
        check_vma=False,
    )
```

```python
import functools
import math

import jax
import jax.numpy as jnp
import numpy as np
from jax import lax
from jax.experimental import pallas as pl
from jax.experimental.pallas import tpu as pltpu
from jax.sharding import PartitionSpec as P

HEADS = 64
KVH = 8
HD = 128
ROWS = 128
CTX = 1024
PAGE = 16
GQ = 8
KVW = 1024

ROPE_BASE = 500000.0
NEG_FILL = -1e30
LOW = -1e29
TINY = 1.2e-38
NO_LEVEL = -16000.0
LEVELS = 32767.0
SCALE = 1.0 / math.sqrt(HD)
EXP2_SCALE = SCALE * math.log2(math.e)
LANES = 256
KEYS = 512
DEPTH = 1024
TAIL = 8
CONTRACT_FIRST = (((0,), (0,)), ((), ()))
CONTRACT_LAST = (((1,), (1,)), ((), ()))
PARAMS = pltpu.CompilerParams(vmem_limit_bytes=60 << 20)
ATTEND_PARAMS = pltpu.CompilerParams(vmem_limit_bytes=32 << 20)
SMALL_PARAMS = pltpu.CompilerParams(vmem_limit_bytes=40 << 20)


def small_cost(flops):
    return pl.CostEstimate(flops=flops, bytes_accessed=1 << 16, transcendentals=0)


def inverse_frequencies():
    steps = np.arange(HD // 2, dtype=np.float32) * np.float32(-2.0 * math.log(ROPE_BASE) / HD)
    return np.exp(steps.astype(np.float64)).astype(np.float32)


def rope_tables(positions):
    inverse = jnp.asarray(np.tile(inverse_frequencies(), 2))
    sign = np.repeat(np.array([-1.0, 1.0], np.float32), HD // 2)
    angles = positions.astype(jnp.float32)[:, None] * inverse[None, :]
    return jnp.cos(angles), jnp.sin(angles) * sign[None, :]


def rotated(values, cosine, signed_sine):
    return values * cosine + pltpu.roll(values, HD // 2, 1) * signed_sine


def project_kernel(ranks, rank_ref, x_ref, w_ref, page_ref, owner_ref, cache_ref, *refs):
    out_refs, page_outs = refs[:ranks], refs[ranks:2 * ranks + 1]
    rows_in, weight, total, kept_pages, near_pages, far_pages, sems, counts, page_sems, out_sems = (
        refs[2 * ranks + 1:]
    )
    entries = page_ref.shape[0]
    share = out_refs[0].shape[0]
    chunks, depth = weight.shape[0], weight.shape[1]
    rows_copy = pltpu.make_async_copy(x_ref, rows_in, sems.at[chunks])

    def weight_copy(j):
        source = w_ref.at[pl.ds(j * depth, depth), :]
        return pltpu.make_async_copy(source, weight.at[j], sems.at[j])

    def page_rows(e):
        return pl.ds(pl.multiple_of(page_ref[e] * PAGE, PAGE), PAGE)

    def kept(e, slot):
        return pltpu.make_async_copy(cache_ref.at[page_rows(e), :], kept_pages.at[slot], page_sems.at[e])

    def near(e, k, slot):
        source = cache_ref.at[page_rows(e), pl.ds(0, KVW)]
        return pltpu.make_async_copy(source, near_pages.at[k - 1, slot], page_sems.at[e])

    def far(e, k, slot):
        source = cache_ref.at[page_rows(e), pl.ds(KVW, KVW)]
        return pltpu.make_async_copy(source, far_pages.at[k - 1, slot], page_sems.at[e])

    rows_copy.start()
    for j in range(chunks):
        weight_copy(j).start()
    for ref in (kept_pages, near_pages, far_pages):
        ref[...] = jnp.zeros_like(ref)
    for r in range(ranks):
        counts[r] = 0

    def begin(e, carry):
        owner = owner_ref[e]
        slot = counts[owner]
        counts[owner] = slot + 1
        place = lax.rem(owner - rank_ref[0] + ranks, ranks)

        @pl.when(place == 0)
        def _():
            kept(e, slot).start()

        @pl.when(place > 0)
        def _():
            near(e, place, slot).start()
            far(e, place, slot).start()

        return carry

    def end(e, carry):
        kept(e, 0).wait()
        return carry

    sources = [kept_pages, *[near_pages.at[k] for k in range(ranks - 1)], far_pages]
    page_copies = [
        pltpu.make_async_copy(source, out, out_sems.at[i])
        for i, (source, out) in enumerate(zip(sources, page_outs))
    ]
    lax.fori_loop(0, entries, begin, 0)
    rows_copy.wait()
    for j in range(chunks):
        weight_copy(j).wait()
        part = jnp.dot(
            rows_in[:, j * depth:(j + 1) * depth], weight[j], preferred_element_type=jnp.float32
        )
        if j:
            part = part + total[...]
        total[...] = part
        if j == min(1, chunks - 1):
            lax.fori_loop(0, entries, end, 0)
            for c in page_copies:
                c.start()
    for k in range(ranks):
        dest = lax.rem(rank_ref[0] + k, ranks)
        out_refs[k][...] = total[pl.ds(pl.multiple_of(dest * share, share), share), :]
    for c in page_copies:
        c.wait()


def project(me, x, weight, page_list, owner_ids, cache, ranks):
    share = ROWS // ranks
    depth = weight.shape[0]
    block = min(depth, DEPTH)
    entries = page_list.shape[0]
    slots = 2 * entries // ranks
    smem = pl.BlockSpec(memory_space=pltpu.SMEM)
    vmem = pl.BlockSpec(memory_space=pltpu.VMEM)
    anywhere = pl.BlockSpec(memory_space=pl.ANY)
    pages = [(slots, PAGE, 2 * KVW)] + [(slots, PAGE, KVW)] * (ranks - 1)
    pages += [(ranks - 1, slots, PAGE, KVW)]
    out = pl.pallas_call(
        functools.partial(project_kernel, ranks),
        in_specs=[smem, anywhere, anywhere, smem, smem, anywhere],
        out_specs=[vmem] * ranks + [anywhere] * len(pages),
        out_shape=[jax.ShapeDtypeStruct((share, 2 * KVW), jnp.float32)] * ranks
        + [jax.ShapeDtypeStruct(shape, jnp.bfloat16) for shape in pages],
        scratch_shapes=[
            pltpu.VMEM((ROWS, depth), jnp.bfloat16),
            pltpu.VMEM((depth // block, block, 2 * KVW), jnp.bfloat16),
            pltpu.VMEM((ROWS, 2 * KVW), jnp.float32),
            pltpu.VMEM(pages[0], jnp.bfloat16),
            pltpu.VMEM(pages[-1], jnp.bfloat16),
            pltpu.VMEM(pages[-1], jnp.bfloat16),
            pltpu.SemaphoreType.DMA((depth // block + 1,)),
            pltpu.SMEM((ranks,), jnp.int32),
            pltpu.SemaphoreType.DMA((entries,)),
            pltpu.SemaphoreType.DMA((len(pages),)),
        ],
        compiler_params=PARAMS,
        cost_estimate=small_cost(1 << 20),
        name="project",
    )(me.reshape(1), x, weight, page_list, owner_ids, cache)
    return out[:ranks], out[ranks:2 * ranks], out[2 * ranks]


def prepare_kernel(q_ref, k_ref, scale_ref, qc_ref, qs_ref, kc_ref, ks_ref, q_out, k_out):
    for g in range(GQ):
        q = rotated(q_ref[:, g * HD:(g + 1) * HD].astype(jnp.float32), qc_ref[...], qs_ref[...])
        q_out[g * ROWS:(g + 1) * ROWS, :] = q.astype(jnp.bfloat16)
    for h in range(KVH):
        columns = slice(h * HD, (h + 1) * HD)
        key = k_ref[:, columns].astype(jnp.float32) * scale_ref[:, columns]
        k_out[h] = rotated(key, kc_ref[...], ks_ref[...]).astype(jnp.bfloat16)


def prepare(queries, cache, key_scale, q_tables, k_tables):
    fixed = lambda j: (0, 0)
    rows = CTX // KVH
    return pl.pallas_call(
        prepare_kernel,
        grid=(KVH,),
        in_specs=[
            pl.BlockSpec((ROWS, GQ * HD), lambda j: (0, j)),
            pl.BlockSpec((rows, KVW), lambda j: (j, 0)),
            pl.BlockSpec((1, KVW), fixed),
            pl.BlockSpec((ROWS, HD), fixed),
            pl.BlockSpec((ROWS, HD), fixed),
            pl.BlockSpec((rows, HD), lambda j: (j, 0)),
            pl.BlockSpec((rows, HD), lambda j: (j, 0)),
        ],
        out_specs=[
            pl.BlockSpec((GQ * ROWS, HD), lambda j: (j, 0)),
            pl.BlockSpec((KVH, rows, HD), lambda j: (0, j, 0)),
        ],
        out_shape=[
            jax.ShapeDtypeStruct((HEADS * ROWS, HD), jnp.bfloat16),
            jax.ShapeDtypeStruct((KVH, CTX, HD), jnp.bfloat16),
        ],
        compiler_params=ATTEND_PARAMS,
        cost_estimate=small_cost(1 << 30),
        name="prepare",
    )(queries, cache, key_scale, *q_tables, *k_tables)


def split_level(level):
    doubled = jnp.maximum(level, NO_LEVEL) * 2.0
    high = jnp.floor(doubled)
    return [high, (doubled - high) * 65536.0 - 32768.0]


def joined_level(high, low):
    return (high + (low + 32768.0) * (1.0 / 65536.0)) * 0.5


def code_into(out_ref, lanes, top, total, numerator):
    largest = jnp.maximum(jnp.max(jnp.abs(numerator), axis=0, keepdims=True), TINY)
    coded = jnp.round(numerator * (1.0 / largest) * LEVELS)
    out_ref[:HD, lanes] = coded.astype(jnp.int32).astype(jnp.int16)
    tail = split_level(top + jnp.log2(largest)) + split_level(top + jnp.log2(total))
    tail = jnp.concatenate(tail + [jnp.zeros((TAIL - 4, top.shape[1]), jnp.float32)], axis=0)
    out_ref[HD:, lanes] = tail.astype(jnp.int32).astype(jnp.int16)


def decode(ref, lanes):
    tail = ref[HD:, lanes].astype(jnp.int32).astype(jnp.float32)
    values = ref[:HD, lanes].astype(jnp.int32).astype(jnp.float32)
    return joined_level(tail[0:1], tail[1:2]), joined_level(tail[2:3], tail[3:4]), values


def merged(top, total, numerator, parts):
    peak = functools.reduce(jnp.maximum, [p[1] for p in parts], top)
    if total is not None:
        factor = jnp.exp2(top - peak)
        total, numerator = total * factor, numerator * factor
    for level, weight, values in parts:
        more = jnp.exp2(weight - peak)
        part = values * (jnp.exp2(level - peak) * (1.0 / LEVELS))
        total = more if total is None else total + more
        numerator = part if numerator is None else numerator + part
    return peak, total, numerator


def fold_rows(values, combine):
    rows, cols = values.shape
    return combine(values.reshape(rows // 8, 8, cols), axis=0)


def gather_kernel(ranks, rank_ref, qc_ref, qs_ref, *refs):
    key_out, value_out = refs[ranks:]
    share = refs[0].shape[0]
    mine = pl.ds(pl.multiple_of(rank_ref[0] * share, share), share)
    cosine, signed_sine = qc_ref[mine, :], qs_ref[mine, :]
    for h in range(KVH):
        columns = slice(h * HD, (h + 1) * HD)
        key = sum(ref[:, columns] for ref in refs[:ranks])
        key = key.astype(jnp.bfloat16).astype(jnp.float32)
        key_out[h] = rotated(key, cosine, signed_sine).astype(jnp.bfloat16)
        columns = slice(KVW + h * HD, KVW + (h + 1) * HD)
        value_out[h] = sum(ref[:, columns] for ref in refs[:ranks]).astype(jnp.bfloat16)


def gather(me, q_tables, fresh):
    share = fresh[0].shape[0]
    vmem = pl.BlockSpec(memory_space=pltpu.VMEM)
    return pl.pallas_call(
        functools.partial(gather_kernel, len(fresh)),
        in_specs=[pl.BlockSpec(memory_space=pltpu.SMEM)] + [vmem] * (2 + len(fresh)),
        out_specs=[vmem] * 2,
        out_shape=[jax.ShapeDtypeStruct((KVH, share, HD), jnp.bfloat16)] * 2,
        compiler_params=ATTEND_PARAMS,
        cost_estimate=small_cost(1 << 18),
        name="gather",
    )(me.reshape(1), *q_tables, *fresh)


def attend_kernel(is_open, deps, length_ref, rank_ref, q_ref, k_ref, v_ref, fk_ref, fv_ref, *refs):
    refs = refs[deps:]
    if is_open:
        num_ref, stat_ref, scores = refs
    else:
        out_ref, scores = refs
    rank = rank_ref[0]
    share = fk_ref.shape[1]
    valid = length_ref[0] - rank * CTX
    first = rank * share
    fresh_key, fresh_value = fk_ref[0], fv_ref[0]
    cols = q_ref.shape[0]
    queries = q_ref[...]
    key_id = first + lax.broadcasted_iota(jnp.int32, (share, cols), 0)
    row_id = lax.broadcasted_iota(jnp.int32, (share, cols), 1) % ROWS
    fs = lax.dot_general(fresh_key, queries, CONTRACT_LAST, preferred_element_type=jnp.float32)
    fs = jnp.where(key_id <= row_id, fs, NEG_FILL)
    peak = fold_rows(fs, jnp.max)
    for t in range(CTX // KEYS):
        rows = slice(t * KEYS, (t + 1) * KEYS)
        s = lax.dot_general(
            k_ref[0, rows, :], queries, CONTRACT_LAST, preferred_element_type=jnp.float32
        )
        position = t * KEYS + lax.broadcasted_iota(jnp.int32, (KEYS, cols), 0)
        s = jnp.where(position < valid, s, NEG_FILL)
        scores[rows, :] = s
        peak = jnp.maximum(peak, fold_rows(s, jnp.max))
    peak = jnp.max(peak, axis=0, keepdims=True)
    base = jnp.maximum(peak, LOW)
    w = jnp.exp((fs - base) * SCALE)
    total = fold_rows(w, jnp.sum)
    numerator = lax.dot_general(
        fresh_value, w.astype(jnp.bfloat16), CONTRACT_FIRST, preferred_element_type=jnp.float32
    )
    for t in range(CTX // KEYS):
        rows = slice(t * KEYS, (t + 1) * KEYS)
        w = jnp.exp((scores[rows, :] - base) * SCALE)
        total = total + fold_rows(w, jnp.sum)
        numerator = numerator + lax.dot_general(
            v_ref[rows, :], w.astype(jnp.bfloat16), CONTRACT_FIRST, preferred_element_type=jnp.float32
        )
    total = jnp.sum(total, axis=0, keepdims=True)
    top = jnp.maximum(peak * EXP2_SCALE, NO_LEVEL)
    if is_open:
        num_ref[0] = numerator
        stat_ref[0] = jnp.concatenate([top, total, jnp.zeros((6, cols), jnp.float32)], axis=0)
    else:
        code_into(out_ref, slice(0, cols), top, total, numerator)


def layout(ranks):
    heads_here = HEADS // ranks
    pieces = max(1, heads_here // GQ)
    heads = heads_here // pieces
    return pieces, heads, heads * ROWS, ROWS // ranks


def whole(j, s):
    return (0, 0)


def opened_specs(cols):
    place = lambda j, n, r: (j, 0, 0)
    return [pl.BlockSpec((1, HD, cols), place), pl.BlockSpec((1, 8, cols), place)]


def attend(length, me, code, queries, keys, cache, fresh, earlier, ranks, is_open, cost):
    pieces, heads, cols, share = layout(ranks)

    def piece(j, rank_ref):
        return (rank_ref[0] ^ code) * pieces + j

    def key_head(j, rank_ref):
        return piece(j, rank_ref) * heads // GQ

    if is_open:
        out_specs = opened_specs(cols)
        out_shape = [
            jax.ShapeDtypeStruct((pieces, HD, cols), jnp.float32),
            jax.ShapeDtypeStruct((pieces, 8, cols), jnp.float32),
        ]
    else:
        out_specs = pl.BlockSpec((HD + TAIL, cols), lambda j, n, r: (0, j))
        out_shape = jax.ShapeDtypeStruct((HD + TAIL, pieces * cols), jnp.int16)
    own_head = lambda j, n, r: (key_head(j, r), 0, 0)
    return pl.pallas_call(
        functools.partial(attend_kernel, is_open, len(earlier)),
        grid_spec=pltpu.PrefetchScalarGridSpec(
            num_scalar_prefetch=2,
            grid=(pieces,),
            in_specs=[
                pl.BlockSpec((cols, HD), lambda j, n, r: (piece(j, r), 0)),
                pl.BlockSpec((1, CTX, HD), own_head),
                pl.BlockSpec((CTX, HD), lambda j, n, r: (0, KVH + key_head(j, r))),
                pl.BlockSpec((1, share, HD), own_head),
                pl.BlockSpec((1, share, HD), own_head),
            ]
            + [pl.BlockSpec(memory_space=pl.ANY)] * len(earlier),
            out_specs=out_specs,
            scratch_shapes=[pltpu.VMEM((CTX, cols), jnp.float32)],
        ),
        out_shape=out_shape,
        compiler_params=ATTEND_PARAMS,
        cost_estimate=small_cost(cost),
        name="attend_open" if is_open else "attend",
    )(length, me, queries, keys, cache, *fresh, *earlier)


def close_kernel(is_last, count, num_ref, stat_ref, *refs):
    in_refs, out_ref = refs[:count], refs[-1]
    for b in range(out_ref.shape[1] // LANES):
        lanes = slice(b * LANES, (b + 1) * LANES)
        top, total, numerator = stat_ref[0, 0:1, lanes], stat_ref[0, 1:2, lanes], num_ref[0, :, lanes]
        parts = [decode(ref, lanes) for ref in in_refs]
        top, total, numerator = merged(top, total, numerator, parts)
        if not is_last:
            code_into(out_ref, lanes, top, total, numerator)
            continue
        numerator = numerator / total
        for h in range(LANES // ROWS):
            column = b * LANES + h * HD
            out_ref[:, column:column + HD] = (
                numerator[:, h * ROWS:(h + 1) * ROWS].T.astype(jnp.bfloat16)
            )


def close(opened, received, earlier, ranks, is_last=False):
    pieces, _, cols, _ = layout(ranks)
    rows, kind = (ROWS, jnp.bfloat16) if is_last else (HD + TAIL, jnp.int16)
    place = lambda j: (j, 0, 0)
    return pl.pallas_call(
        functools.partial(close_kernel, is_last, len(received)),
        grid=(pieces,),
        in_specs=[pl.BlockSpec((1, HD, cols), place), pl.BlockSpec((1, 8, cols), place)]
        + [pl.BlockSpec((HD + TAIL, cols), lambda j: (0, j))] * len(received)
        + [pl.BlockSpec(memory_space=pl.ANY)] * len(earlier),
        out_specs=pl.BlockSpec((rows, cols), lambda j: (0, j)),
        out_shape=jax.ShapeDtypeStruct((rows, pieces * cols), kind),
        compiler_params=SMALL_PARAMS,
        cost_estimate=small_cost(1 << 18),
        name="finish" if is_last else "close",
    )(*opened, *received, *earlier)


def choose_kernel(sec_ref, *refs):
    count = (len(refs) - 2) // 2
    near, there_ref, out_refs, sems = refs[:count], refs[count], refs[count + 1:-1], refs[-1]
    first = sec_ref[0] == 0
    for k in range(count):
        @pl.when(first)
        def _():
            pltpu.make_async_copy(near[k], out_refs[k], sems.at[k]).start()

        @pl.when(jnp.logical_not(first))
        def _():
            pltpu.make_async_copy(there_ref.at[k], out_refs[k], sems.at[k]).start()

    for k in range(count):
        pltpu.make_async_copy(near[k], out_refs[k], sems.at[k]).wait()


def choose(sec, near, there):
    count = len(near)
    return pl.pallas_call(
        choose_kernel,
        in_specs=[pl.BlockSpec(memory_space=pltpu.SMEM)] + [pl.BlockSpec(memory_space=pl.ANY)] * (count + 1),
        out_specs=[pl.BlockSpec(memory_space=pltpu.VMEM)] * count,
        out_shape=[jax.ShapeDtypeStruct(there.shape[1:], there.dtype)] * count,
        scratch_shapes=[pltpu.SemaphoreType.DMA((count,))],
        compiler_params=SMALL_PARAMS,
        cost_estimate=small_cost(1 << 18),
        name="choose",
    )(sec.reshape(1), *near, there)


def arrange_kernel(sec_ref, rank_ref, kept_ref, *refs):
    count = (len(refs) - 2) // 2
    crossed, routed, out_ref = refs[:count], refs[count:2 * count], refs[-1]
    shift = lax.rem(rank_ref[0] - pl.program_id(0) + count + 1, count + 1)
    second = sec_ref[0] > 0

    @pl.when(jnp.logical_not(second))
    def _():
        out_ref[...] = jnp.zeros_like(out_ref)

    @pl.when(jnp.logical_and(second, shift == 0))
    def _():
        out_ref[...] = kept_ref[...]

    for k in range(count):
        @pl.when(jnp.logical_and(second, shift == k + 1))
        def _():
            out_ref[:, :, :KVW] = crossed[k][...]
            out_ref[:, :, KVW:] = routed[k][...]


def arrange(sec, me, kept, crossed, routed, earlier):
    ranks = len(crossed) + 1
    slots = kept.shape[0]
    smem = pl.BlockSpec(memory_space=pltpu.SMEM)
    return pl.pallas_call(
        arrange_kernel,
        grid=(ranks,),
        in_specs=[smem, smem]
        + [pl.BlockSpec(v.shape, lambda j: (0, 0, 0)) for v in [kept, *crossed, *routed]]
        + [pl.BlockSpec(memory_space=pl.ANY)],
        out_specs=pl.BlockSpec((slots, PAGE, 2 * KVW), lambda j: (j, 0, 0)),
        out_shape=jax.ShapeDtypeStruct((ranks * slots, PAGE, 2 * KVW), jnp.bfloat16),
        compiler_params=SMALL_PARAMS,
        cost_estimate=small_cost(1 << 18),
        name="arrange",
    )(sec.reshape(1), me.reshape(1), kept, *crossed, *routed, earlier)


def after(value, earlier):
    return lax.optimization_barrier((value, earlier))[0]


def shards(queries, kv_cache, key_scale, fresh_input, kv_weight, lengths, page_list, owners):
    ranks = lax.axis_size("rank")
    secs = lax.axis_size("sec")
    me = lax.axis_index("rank").astype(jnp.int32)
    sec = lax.axis_index("sec").astype(jnp.int32)
    cache = kv_cache[0]
    length = lengths[0, 0]
    pieces, heads, _, _ = layout(ranks)

    def shifted(value, k):
        return lax.ppermute(value, "rank", [(i, (i + k) % ranks) for i in range(ranks)])

    def swapped(value, bit):
        return lax.ppermute(value, "rank", [(i, i ^ bit) for i in range(ranks)])

    def handed_on(value):
        return lax.ppermute(value, "sec", [(i, (i + 1) % secs) for i in range(secs)])

    part, (kept, *near), there = project(
        me, fresh_input[0], kv_weight, page_list, owners[:, 0], cache, ranks
    )
    fresh = [part[0]] + [shifted(part[k], k) for k in range(1, ranks)]

    q_tables = rope_tables(after(length, part) + jnp.arange(ROWS, dtype=jnp.int32))
    k_tables = rope_tables(after(me, part) * CTX + jnp.arange(CTX, dtype=jnp.int32))
    there = handed_on(there)
    q_rot, keys = prepare(queries[0], cache, key_scale[None, :], q_tables, k_tables)
    chosen = choose(sec, near, after(there, q_rot))
    arrived = after(fresh, chosen)
    chosen = after(chosen, arrived)
    routed = [shifted(c, k + 1) for k, c in enumerate(chosen)]
    fresh = gather(me, q_tables, arrived)
    kept = handed_on(after(kept, fresh))

    def attend_to(code, earlier, is_open, cost=1 << 28):
        return attend(
            lengths[0], me.reshape(1), code, q_rot, keys, cache, fresh, earlier, ranks, is_open, cost
        )

    taken = {code: [] for code in range(ranks)}

    def send(value, code, bit):
        taken[code ^ bit].append(swapped(value, bit))

    last = chosen[:1]
    for code in range(ranks - 1, 1, -2):
        last = [attend_to(code, last, False)]
        send(last[0], code, 1)
    merging = {}
    for code in range(ranks - 2, 0, -2):
        merging[code] = attend_to(code, last, True)
        last = merging[code][1:]
    waiting = attend_to(1, [*routed[::2], *last], True, 1 << 32)
    last = waiting[1:]
    bit = 2
    while bit < ranks:
        for code in range(ranks - bit, 0, -2 * bit):
            last = [close(merging[code], taken[code], last, ranks)]
            send(last[0], code, bit)
        bit *= 2
    direct = close(waiting, [], [*last, *routed[1::2]], ranks)
    own = attend_to(0, [direct], True)
    handed = arrange(sec, me, kept, [handed_on(r) for r in routed], routed, own[1])
    taken[0].insert(0, swapped(direct, 1))
    attended = close(after(own, handed), taken[0], [], ranks, is_last=True)[None]
    return (attended, handed[None])


def solution(mesh):
    return jax.shard_map(
        shards,
        mesh=mesh,
        in_specs=(
            P(("sec", "grp"), None, None),
            P(("sec", "grp"), "rank", None),
            P(),
            P(("sec", "grp"), None, "rank"),
            P("rank", None),
            P(("sec", "grp"), None),
            P(("sec", "grp", "rank")),
            P(("sec", "grp", "rank"), None),
        ),
        out_specs=(P(("sec", "grp"), None, "rank"), P(("sec", "grp", "rank"), None, None, None)),
        check_vma=False,
    )
```
